32 devices in a mesh: section: 2 (over x), dp: 16 (over z, y, core).
Axes of the slice: x: 2, y: 2, z: 4, core: 2. Of those that a mesh axis runs over, the one named last changes fastest.
Arguments:
- inputs: bfloat16 [2, 32, 512, 512], P('section', 'dp'), may hold values from -6 to 6
- cotangent: bfloat16 [2, 32, 512, 512], P('section', 'dp'), may hold values from -6 to 6
- lengths: int32 [2, 32, 16], P(None, 'dp'), may hold values from 1 to 256, 512 in all within a row
- running: int32 [2, 32, 512], P('section', 'dp'), may hold values 0 or 1
- norm_gain: float32 [2, 2, 512], P('section'), may hold values from 0.25 to 1.75
- norm_shift: float32 [2, 2, 512], P('section'), may hold values from -1.5 to 1.5
- qkv_weight: bfloat16 [2, 512, 1536], P('section'), may hold values from -0.25 to 0.25
- out_weight: bfloat16 [2, 512, 512], P('section'), may hold values from -2 to 2
- up_weight: bfloat16 [2, 512, 2048], P('section'), may hold values from -0.25 to 0.25
- up_bias: float32 [2, 2048], P('section'), may hold values from -2.5 to 2.5
- down_weight: bfloat16 [2, 2048, 512], P('section'), may hold values from -0.125 to 0.125
- down_bias: float32 [2, 512], P('section'), may hold values from -2.5 to 2.5
- halt_weight: float32 [2, 512], P('section'), may hold values from -0.25 to 0.25
- halt_bias: float32 [2], P('section'), may hold values from -1 to 1
- cross_gain: float32 [512], replicated, may hold values from 0.25 to 1.75
- cross_shift: float32 [512], replicated, may hold values from -1.5 to 1.5
- cross_query: bfloat16 [512, 512], replicated, may hold values from -0.25 to 0.25
- cross_kv: bfloat16 [512, 1024], replicated, may hold values from -0.25 to 0.25
- cross_out: bfloat16 [512, 512], replicated, may hold values from -2 to 2
Outputs:
- activations: bfloat16 [2, 32, 512, 512], P('section', 'dp')
- input_grad: float32 [2, 32, 512, 512], P('section', 'dp')
- row_rms: float32 [2, 32, 2], P('section', 'dp')
- norm_gain_grad: float32 [2, 2, 512], P('section')
- norm_shift_grad: float32 [2, 2, 512], P('section')
- qkv_weight_grad: float32 [2, 512, 1536], P('section')
- out_weight_grad: float32 [2, 512, 512], P('section')
- up_weight_grad: float32 [2, 512, 2048], P('section')
- up_bias_grad: float32 [2, 2048], P('section')
- down_weight_grad: float32 [2, 2048, 512], P('section')
- down_bias_grad: float32 [2, 512], P('section')
- halt_weight_grad: float32 [2, 512], P('section')
- halt_bias_grad: float32 [2], P('section')
- cross_gain_grad: float32 [512], replicated
- cross_shift_grad: float32 [512], replicated
- cross_query_grad: float32 [512, 512], replicated
- cross_kv_grad: float32 [512, 1024], replicated
- cross_out_grad: float32 [512, 512], replicated
The draws below stay inside these ranges and needn't reach their ends.
Inputs may be any that keep to these rules, and one draw needn't show every extreme that they name: Each row's 16 sentence lengths sum to 512; sentence k of a row's source pairs with sentence k of its target.
All inputs are finite; a program needn't handle non-finite values. No bound on the sum of `running` on one device may be relied on, other than what follows from the above.
Results may differ from the reference program's by a relative error of at most 0.025.
Values may be sent and summed in bfloat16 or wider, within the bound.
No kernel may reach another device: no remote copies, remote signals or barrier semaphores. Data moves between devices by JAX's collectives and lax.ppermute only.
A program may use at most 192 MiB of HBM per device.

```python
import math
import jax
import jax.numpy as jnp
import numpy as np
from jax import lax

D = 512
FF = 2048
HEADS = 8
HEAD_DIM = 64
L = 512
SEGS = 16
MOSTLEN = 256
ROWS = 32


def plant(values, key, least, top_value):
    place = [jax.random.randint(jax.random.fold_in(key, axis), (), 0, length) for axis, length in enumerate(values.shape)]
    longest = values.shape.index(max(values.shape))
    next_to = place[:longest] + [(place[longest] + 1) % values.shape[longest]] + place[longest + 1:]
    return values.at[tuple(place)].set(least).at[tuple(next_to)].set(top_value)


def level_of(own_key, extent, cuts, smallest, top_value):
    factor_of, own = 1.0, jax.random.fold_in(own_key, 6)
    for dim, shards_of in cuts:
        draws = jnp.exp(jax.random.uniform(jax.random.fold_in(own, dim), (shards_of,), jnp.float32, smallest / len(cuts), top_value / len(cuts)))
        factor_of = factor_of * jnp.repeat(draws, extent[dim] // shards_of).reshape([-1 if axis == dim else 1 for axis in range(len(extent))])
    return factor_of


def split_up(number_of, total, reach, lean):
    portions = [(1 << 20) // math.isqrt(standing ** lean) + 1 for standing in range(2, number_of + 1)]
    rest, holding = total - reach - (number_of - 1), [1] * (number_of - 1)
    while rest > 0:
        movable = [i for i in range(number_of - 1) if holding[i] < reach]
        whole, remaining = sum([portions[i] for i in movable]), rest
        for i in movable:
            extra = min(reach - holding[i], max(1, remaining * portions[i] // whole), rest)
            holding[i] = holding[i] + extra
            rest = rest - extra
    return np.array([reach] + holding)


def ragged(key, amount, total, most, slope):
    if amount == 2:
        one = jax.random.randint(key, (), max(1, total - most), min(most, total - 1) + 1)
        return jnp.stack([one, total - one])
    sizes = jnp.asarray(split_up(amount, total, most, slope), jnp.int32)
    twos = (amount - 1) // 2
    giver, sink = sizes[1:1 + 2 * twos:2], sizes[2:2 + 2 * twos:2]
    margin = jnp.minimum(giver - 1, most - sink)
    moved = jax.random.randint(jax.random.fold_in(key, 1), (twos,), 0, 1 << 20) % (margin + 1)
    sizes = sizes.at[1:1 + 2 * twos:2].set(giver - moved).at[2:2 + 2 * twos:2].set(sink + moved)
    return sizes[jax.random.permutation(jax.random.fold_in(key, 2), amount)]


def normal_values(key, dims, width, most, cuts=(), kind=jnp.bfloat16):
    values = width * jax.random.normal(key, dims, jnp.float32)
    if cuts:
        values = values * level_of(key, dims, cuts, -0.22, 0.18)
    return jnp.clip(values, -most, most).astype(kind)


def setup_inputs(seed: int = 0) -> dict:
    key_list = jax.random.split(jax.random.key(seed), 20)
    return {
        "inputs": normal_values(key_list[0], (2, ROWS, L, D), 1.0, 6.0, ((0, 2), (1, 16))),
        "cotangent": normal_values(key_list[1], (2, ROWS, L, D), 1.0, 6.0, ((0, 2), (1, 16))),
        "lengths": jax.vmap(lambda own: ragged(own, SEGS, L, MOSTLEN, 2))(jax.random.split(key_list[2], 2 * ROWS)).reshape((2, ROWS, SEGS)).astype(jnp.int32),
        "running": plant((jax.random.randint(key_list[3], (2, ROWS, L), 0, 4) < 3).astype(jnp.int32), jax.random.fold_in(key_list[3], 1), 0, 1),
        "norm_gain": jnp.clip(1.0 + 0.15 * jax.random.normal(key_list[4], (2, 2, D), jnp.float32), 0.25, 1.75),
        "norm_shift": normal_values(key_list[5], (2, 2, D), 0.3, 1.5, ((0, 2),), jnp.float32),
        "qkv_weight": normal_values(key_list[6], (2, D, 3 * D), D ** -0.5, 0.25, ((0, 2),)),
        "out_weight": normal_values(key_list[7], (2, D, D), (max(8, D // 64)) ** -0.5, 2.0, ((0, 2),)),
        "up_weight": normal_values(key_list[8], (2, D, FF), D ** -0.5, 0.25, ((0, 2),)),
        "up_bias": normal_values(key_list[9], (2, FF), 0.5, 2.5, ((0, 2),), jnp.float32),
        "down_weight": normal_values(key_list[10], (2, FF, D), FF ** -0.5, 0.125, ((0, 2),)),
        "down_bias": normal_values(key_list[11], (2, D), 0.5, 2.5, ((0, 2),), jnp.float32),
        "halt_weight": normal_values(key_list[12], (2, D), D ** -0.5, 0.25, ((0, 2),), jnp.float32),
        "halt_bias": jnp.clip(jax.random.uniform(key_list[13], (2,), jnp.float32, -1.0, 1.0) * level_of(key_list[13], (2,), ((0, 2),), -0.4, 0.0), -1.0, 1.0),
        "cross_gain": jnp.clip(1.0 + 0.15 * jax.random.normal(key_list[14], (D,), jnp.float32), 0.25, 1.75),
        "cross_shift": normal_values(key_list[15], (D,), 0.3, 1.5, (), jnp.float32),
        "cross_query": normal_values(key_list[16], (D, D), D ** -0.5, 0.25),
        "cross_kv": normal_values(key_list[17], (D, 2 * D), D ** -0.5, 0.25),
        "cross_out": normal_values(key_list[18], (D, D), (max(8, D // 64)) ** -0.5, 2.0),
    }


highest = lax.Precision.HIGHEST

@jax.custom_vjp
def low(v):
    return lax.optimization_barrier(v.astype(jnp.bfloat16)).astype(jnp.float32)

@jax.custom_vjp
def low_back(v):
    return v

def low_keep(v):
    return (low(v), None)

def low_pass(kept, grad):
    return (grad,)

def back_keep(v):
    return (v, None)

def back_low(kept, grad):
    return (low(grad),)
low.defvjp(low_keep, low_pass)
low_back.defvjp(back_keep, back_low)

def product(left_in, right_in):
    return jnp.dot(left_in, right_in, precision=highest)

def segment_ids(lengths):
    boundaries = jnp.cumsum(lengths, dtype=jnp.int32)
    places = jnp.arange(L, dtype=jnp.int32)
    return lax.optimization_barrier(jnp.sum((places[:, None] >= boundaries[None, :]).astype(jnp.int32), axis=1, dtype=jnp.int32))

def layer_norm(current, gain_vec, shift_vec):
    centered = current - lax.optimization_barrier(jnp.mean(current, axis=-1, keepdims=True))
    spread = lax.optimization_barrier(jnp.mean(centered * centered, axis=-1, keepdims=True))
    return centered * lax.rsqrt(spread + 1e-05) * gain_vec + shift_vec

def attention(queries, key_rows, values, allowed):
    length = queries.shape[0]
    query_heads = queries.reshape(length, HEADS, HEAD_DIM)
    key_heads = key_rows.reshape(key_rows.shape[0], HEADS, HEAD_DIM)
    value_heads = values.reshape(values.shape[0], HEADS, HEAD_DIM)
    scores = jnp.einsum('qhd,khd->hqk', query_heads, key_heads, precision=highest) * HEAD_DIM ** (-0.5)
    scores = low_back(scores)
    scores = jnp.where(allowed[None], scores, -1000000000.0)
    weights = low(jax.nn.softmax(scores, axis=-1))
    attended = jnp.einsum('hqk,khd->qhd', weights, value_heads, precision=highest)
    return attended.reshape(length, D)

def self_attend(current, gain_vec, shift_vec, w_qkv, w_out, allowed):
    normed = low(layer_norm(current, gain_vec, shift_vec))
    packed = low_back(low(product(normed, w_qkv)))
    attended = low_back(low(attention(packed[:, :D], packed[:, D:2 * D], packed[:, 2 * D:], allowed)))
    return current + low_back(product(attended, w_out))

def feed_forward(current, gain_vec, shift_vec, w_up, up_offset, w_down, down_offset):
    normed = low(layer_norm(current, gain_vec, shift_vec))
    pre_act = low_back(product(normed, w_up) + up_offset)
    activated = low(jax.nn.gelu(pre_act, approximate=True))
    return current + low_back(product(activated, w_down) + down_offset)

def halting(current, updated, weight, offset, running_f):
    halt_rate = jax.nn.sigmoid(lax.optimization_barrier(jnp.sum(current * weight, axis=-1)) + offset)
    halt_share = running_f * halt_rate
    return current + halt_share[:, None] * (updated - current)

def row_forward(params, source, target, src_seg, tgt_seg, src_run, tgt_run):
    gain_pair, shift_pair, w_qkv, w_out, w_up, up_offset, w_down, down_offset, w_halt, halt_offset, cross_gain, cross_shift, cross_query, cross_kv, cross_out = params
    places = jnp.arange(L, dtype=jnp.int32)
    enc_allowed = src_seg[:, None] == src_seg[None, :]
    dec_allowed = (tgt_seg[:, None] == tgt_seg[None, :]) & (places[None, :] <= places[:, None])
    cross_allowed = tgt_seg[:, None] == src_seg[None, :]
    after_self = self_attend(source, gain_pair[0, 0], shift_pair[0, 0], w_qkv[0], w_out[0], enc_allowed)
    updated = feed_forward(after_self, gain_pair[0, 1], shift_pair[0, 1], w_up[0], up_offset[0], w_down[0], down_offset[0])
    memory = halting(source, updated, w_halt[0], halt_offset[0], src_run)
    after_self = self_attend(target, gain_pair[1, 0], shift_pair[1, 0], w_qkv[1], w_out[1], dec_allowed)
    normed = low(layer_norm(after_self, cross_gain, cross_shift))
    cross_queries = low_back(low(product(normed, cross_query)))
    memory_in = low_back(low(memory))
    cross_pairs = low_back(low(product(memory_in, cross_kv)))
    cross_att = low_back(low(attention(cross_queries, cross_pairs[:, :D], cross_pairs[:, D:], cross_allowed)))
    after_cross = after_self + low_back(product(cross_att, cross_out))
    updated = feed_forward(after_cross, gain_pair[1, 1], shift_pair[1, 1], w_up[1], up_offset[1], w_down[1], down_offset[1])
    result = halting(target, updated, w_halt[1], halt_offset[1], tgt_run)
    return (memory, result)

def row_stats(result, current):
    change = result - current
    return jnp.stack([jnp.sqrt(jnp.mean(result * result) + 1e-06), jnp.sqrt(jnp.mean(change * change) + 1e-06)])

def reference(inputs, cotangent, lengths, running, norm_gain, norm_shift, qkv_weight, out_weight, up_weight, up_bias, down_weight, down_bias, halt_weight, halt_bias, cross_gain, cross_shift, cross_query, cross_kv, cross_out):
    params = tuple((array.astype(jnp.float32) for array in (norm_gain, norm_shift, qkv_weight, out_weight, up_weight, up_bias, down_weight, down_bias, halt_weight, halt_bias, cross_gain, cross_shift, cross_query, cross_kv, cross_out)))
    inputs_f = inputs.astype(jnp.float32)
    cotangents = cotangent.astype(jnp.float32)
    running_f = running.astype(jnp.float32)

    def one_row(totals, row_data):
        source, target, cot_src, cot_tgt, src_len, tgt_len, src_run, tgt_run = row_data
        src_seg = segment_ids(src_len)
        tgt_seg = segment_ids(tgt_len)

        def forward(weights, first_in, second_in):
            return row_forward(weights, first_in, second_in, src_seg, tgt_seg, src_run, tgt_run)
        (memory, result), pullback = jax.vjp(forward, params, source, target)
        gradients, grad_src, grad_tgt = pullback((cot_src, cot_tgt))
        totals = jax.tree.map(jnp.add, totals, gradients)
        statistics = jnp.stack([row_stats(memory, source), row_stats(result, target)])
        return (totals, (memory, result, grad_src, grad_tgt, statistics))
    start = jax.tree.map(jnp.zeros_like, params)
    totals, outputs = lax.scan(one_row, start, (inputs_f[0], inputs_f[1], cotangents[0], cotangents[1], lengths[0], lengths[1], running_f[0], running_f[1]))
    memories, results, grad_srcs, grad_tgts, statistics = outputs
    activations = jnp.stack([memories, results]).astype(jnp.bfloat16)
    input_grad = jnp.stack([grad_srcs, grad_tgts])
    row_rms = jnp.swapaxes(statistics, 0, 1)
    return (activations, input_grad, row_rms, totals[0], totals[1], totals[2], totals[3], totals[4], totals[5], totals[6], totals[7], totals[8], totals[9], totals[10], totals[11], totals[12], totals[13], totals[14])
```

```python
import jax
import jax.numpy as jnp
from jax import lax
from jax.sharding import PartitionSpec as P

HEADS = 8
L = 512
QB = 512


def from_behind(value, axis, steps):
    count = lax.axis_size(axis)
    initial, last = (max(0, -steps), min(count, count - steps))
    return lax.ppermute(value, axis, [(source, source + steps) for source in range(initial, last)])


def project(operand, weight):
    return jnp.einsum("rlk,kn->rln", operand, weight, preferred_element_type=jnp.float32)


def project_back(gradient, weight):
    return jnp.einsum("rln,kn->rlk", gradient, weight, preferred_element_type=jnp.float32)


def weight_grad(operand, gradient):
    return jnp.einsum("rlk,rln->kn", operand, gradient, preferred_element_type=jnp.float32)


def layer_norm(current, gain_vec, shift_vec):
    centered = current - jnp.mean(current, axis=-1, keepdims=True)
    spread = jnp.mean(centered * centered, axis=-1, keepdims=True)
    return centered * lax.rsqrt(spread + 1e-05) * gain_vec + shift_vec


def norm_back(current, gain_vec, shift_vec, gradient):
    outputs, pullback = jax.vjp(layer_norm, current, gain_vec, shift_vec)
    return pullback(gradient)


def gelu_tanh(pre_act):
    return jax.nn.gelu(pre_act, approximate=True)


def halting(current, updated, weight, offset, running_f):
    halt_rate = jax.nn.sigmoid(jnp.sum(current * weight, axis=-1) + offset)
    return current + (running_f * halt_rate)[..., None] * (updated - current)


def segment_ids(lengths):
    boundaries = jnp.cumsum(lengths, axis=-1, dtype=jnp.int32)
    places = jnp.arange(L, dtype=jnp.int32)
    return jnp.sum(
        (places[None, :, None] >= boundaries[:, None, :]).astype(jnp.int32),
        axis=-1,
        dtype=jnp.int32,
    )


def block_mask(query_seg, key_seg, start, causal):
    query_pos = start + jnp.arange(query_seg.shape[1], dtype=jnp.int32)
    key_pos = jnp.arange(key_seg.shape[1], dtype=jnp.int32)
    ordered = (key_pos[None, :] <= query_pos[:, None]) | (causal == 0)
    return ((query_seg[:, :, None] == key_seg[:, None, :]) & ordered[None])[:, None]


def split_heads(array_in):
    return array_in.reshape(array_in.shape[0], array_in.shape[1], HEADS, array_in.shape[2] // HEADS)


def attend_forward(queries, key_rows, values, query_seg, key_seg, causal):
    row_count, length, feature_count = queries.shape
    score_scale = (feature_count // HEADS) ** (-0.5)
    query_heads = split_heads(queries)
    key_heads = split_heads(key_rows)
    value_heads = split_heads(values)

    def one_block(block_index):
        start = block_index * QB
        allowed = block_mask(query_seg, key_seg, start, causal)
        scores = (
            jnp.einsum(
                "rqhd,rkhd->rhqk", query_heads, key_heads, preferred_element_type=jnp.float32
            )
            * score_scale
        )
        scores = jnp.where(allowed, scores, -1000000000.0)
        row_max = jnp.max(scores, axis=-1, keepdims=True)
        expanded = jnp.exp(scores - row_max)
        denominator = jnp.sum(expanded, axis=-1, keepdims=True)
        weights = (expanded / denominator).astype(jnp.bfloat16)
        attended = jnp.einsum(
            "rhqk,rkhd->rqhd", weights, value_heads, preferred_element_type=jnp.float32
        )
        return (attended.astype(jnp.bfloat16), (row_max + jnp.log(denominator))[..., 0])

    attended, log_total = lax.map(one_block, jnp.arange(length // QB, dtype=jnp.int32))
    attended = jnp.moveaxis(attended, 0, 1).reshape(row_count, length, feature_count)
    return (attended, log_total)


def attend_backward(queries, key_rows, values, log_total, grad_out, query_seg, key_seg, causal):
    row_count, length, feature_count = queries.shape
    score_scale = (feature_count // HEADS) ** (-0.5)
    query_heads = split_heads(queries)
    key_heads = split_heads(key_rows)
    value_heads = split_heads(values)
    grad_heads = split_heads(grad_out)

    def one_block(carry, block_index):
        key_grad, value_grad = carry
        start = block_index * QB
        log_block = lax.dynamic_index_in_dim(log_total, block_index, 0, keepdims=False)
        allowed = block_mask(query_seg, key_seg, start, causal)
        scores = (
            jnp.einsum(
                "rqhd,rkhd->rhqk", query_heads, key_heads, preferred_element_type=jnp.float32
            )
            * score_scale
        )
        scores = jnp.where(allowed, scores, -1000000000.0)
        probability = jnp.exp(scores - log_block[..., None])
        grad_weights = jnp.einsum(
            "rqhd,rkhd->rhqk", grad_heads, value_heads, preferred_element_type=jnp.float32
        )
        grad_scores = probability * (
            grad_weights - jnp.sum(grad_weights * probability, axis=-1, keepdims=True)
        )
        grad_scores = grad_scores.astype(jnp.bfloat16)
        query_grad = (
            jnp.einsum(
                "rhqk,rkhd->rqhd", grad_scores, key_heads, preferred_element_type=jnp.float32
            )
            * score_scale
        )
        key_grad = (
            key_grad
            + jnp.einsum(
                "rhqk,rqhd->rkhd", grad_scores, query_heads, preferred_element_type=jnp.float32
            )
            * score_scale
        )
        value_grad = value_grad + jnp.einsum(
            "rhqk,rqhd->rkhd",
            probability.astype(jnp.bfloat16),
            grad_heads,
            preferred_element_type=jnp.float32,
        )
        return ((key_grad, value_grad), query_grad.astype(jnp.bfloat16))

    zero_heads = jnp.zeros(key_heads.shape, jnp.float32)
    (key_grad, value_grad), query_grad = lax.scan(
        one_block, (zero_heads, zero_heads), jnp.arange(length // QB, dtype=jnp.int32)
    )
    query_grad = jnp.moveaxis(query_grad, 0, 1).reshape(row_count, length, feature_count)
    key_grad = key_grad.reshape(key_rows.shape).astype(jnp.bfloat16)
    value_grad = value_grad.reshape(values.shape).astype(jnp.bfloat16)
    return (query_grad, key_grad, value_grad)


def self_forward(current, gain_vec, shift_vec, w_qkv, w_out, segments, causal):
    feature_count = current.shape[-1]
    normed = layer_norm(current, gain_vec, shift_vec).astype(jnp.bfloat16)
    packed = project(normed, w_qkv).astype(jnp.bfloat16)
    queries = packed[..., :feature_count]
    key_rows = packed[..., feature_count : 2 * feature_count]
    values = packed[..., 2 * feature_count :]
    attended, log_total = attend_forward(queries, key_rows, values, segments, segments, causal)
    after_self = current + project(attended, w_out)
    return (after_self, (normed, queries, key_rows, values, attended, log_total))


def self_backward(current, grad_after, kept, gain_vec, shift_vec, w_qkv, w_out, segments, causal):
    normed, queries, key_rows, values, attended, log_total = kept
    grad_branch = grad_after.astype(jnp.bfloat16)
    out_grad = weight_grad(attended, grad_branch)
    grad_attended = project_back(grad_branch, w_out).astype(jnp.bfloat16)
    query_grad, key_grad, value_grad = attend_backward(
        queries, key_rows, values, log_total, grad_attended, segments, segments, causal
    )
    grad_packed = jnp.concatenate([query_grad, key_grad, value_grad], axis=-1)
    qkv_grad = weight_grad(normed, grad_packed)
    grad_in, gain_grad, shift_grad = norm_back(
        current, gain_vec, shift_vec, project_back(grad_packed, w_qkv)
    )
    return (grad_after + grad_in, gain_grad, shift_grad, qkv_grad, out_grad)


def feed_forward(current, ffn_params):
    gain_vec, shift_vec, w_up, up_offset, w_down, down_offset = ffn_params
    normed = layer_norm(current, gain_vec, shift_vec).astype(jnp.bfloat16)
    pre_act = project(normed, w_up) + up_offset
    activated = gelu_tanh(pre_act).astype(jnp.bfloat16)
    return (current + project(activated, w_down) + down_offset, (normed, pre_act, activated))


def feed_backward(current, grad_after, kept, ffn_params):
    gain_vec, shift_vec, w_up, up_offset, w_down, down_offset = ffn_params
    normed, pre_act, activated = kept
    grad_branch = grad_after.astype(jnp.bfloat16)
    down_grad = weight_grad(activated, grad_branch)
    down_offset_grad = jnp.sum(grad_branch.astype(jnp.float32), axis=(0, 1))
    grad_act = project_back(grad_branch, w_down)
    outputs, pullback = jax.vjp(gelu_tanh, pre_act)
    grad_pre = pullback(grad_act)[0].astype(jnp.bfloat16)
    up_grad = weight_grad(normed, grad_pre)
    up_offset_grad = jnp.sum(grad_pre.astype(jnp.float32), axis=(0, 1))
    grad_in, gain_grad, shift_grad = norm_back(
        current, gain_vec, shift_vec, project_back(grad_pre, w_up)
    )
    return (
        grad_after + grad_in,
        (gain_grad, shift_grad, up_grad, up_offset_grad, down_grad, down_offset_grad),
    )


def gather_sums(own, crossing, width):
    count = lax.axis_size("dp")

    def laid_out(arrays):
        return jnp.concatenate(
            [array.astype(jnp.bfloat16).reshape(count, -1, width) for array in arrays], axis=1
        )

    held = jnp.concatenate([laid_out(own), laid_out(crossing)], axis=1)
    own_rows = sum(array.size for array in own) // (width * count)
    share = lax.psum_scatter(held.reshape(-1, width), "dp", tiled=True)
    cross_share = share[own_rows:]
    swapped = lax.ppermute(cross_share, "section", [(0, 1), (1, 0)])
    cross_share = cross_share.astype(jnp.float32) + swapped.astype(jnp.float32)
    share = jnp.concatenate([share[:own_rows], cross_share.astype(jnp.bfloat16)])
    return lax.all_gather(share, "dp")


def shards(
    inputs,
    cotangent,
    lengths,
    running,
    norm_gain,
    norm_shift,
    qkv_weight,
    out_weight,
    up_weight,
    up_bias,
    down_weight,
    down_bias,
    halt_weight,
    halt_bias,
    cross_gain,
    cross_shift,
    cross_query,
    cross_kv,
    cross_out,
):
    section_index = lax.axis_index("section")
    decoding = section_index == 1
    current = inputs[0].astype(jnp.float32)
    running_f = running[0].astype(jnp.float32)
    src_seg = segment_ids(lengths[0])
    tgt_seg = segment_ids(lengths[1])
    own_seg = jnp.where(decoding, tgt_seg, src_seg)
    feature_count = current.shape[-1]
    ffn_params = (
        norm_gain[0, 1],
        norm_shift[0, 1],
        up_weight[0],
        up_bias[0],
        down_weight[0],
        down_bias[0],
    )
    halt_vec = halt_weight[0]
    halt_offset = halt_bias[0]

    def halt_local(state_in, updated_in, vec_in, offset_in):
        return halting(state_in, updated_in, vec_in, offset_in, running_f)

    after_self, self_kept = self_forward(
        current,
        norm_gain[0, 0],
        norm_shift[0, 0],
        qkv_weight[0],
        out_weight[0],
        own_seg,
        section_index,
    )

    def encoder_head(after):
        updated, unused = feed_forward(after, ffn_params)
        return halt_local(current, updated, halt_vec, halt_offset)

    def decoder_head(after):
        return after

    first_out = lax.cond(decoding, decoder_head, encoder_head, after_self)
    memory_low = first_out.astype(jnp.bfloat16)
    received = from_behind(memory_low, "section", 1)

    def decoder_tail(operands):
        after, arrived = operands
        normed_c = layer_norm(after, cross_gain, cross_shift).astype(jnp.bfloat16)
        cross_queries = project(normed_c, cross_query).astype(jnp.bfloat16)
        cross_pairs = project(arrived, cross_kv).astype(jnp.bfloat16)
        cross_keys = cross_pairs[..., :feature_count]
        cross_values = cross_pairs[..., feature_count:]
        cross_att, cross_log = attend_forward(
            cross_queries, cross_keys, cross_values, tgt_seg, src_seg, 0
        )
        after_cross = after + project(cross_att, cross_out)
        updated, ffn_kept = feed_forward(after_cross, ffn_params)
        result, pullback = jax.vjp(halt_local, current, updated, halt_vec, halt_offset)
        grad_current, grad_updated, vec_grad, offset_grad = pullback(
            cotangent[0].astype(jnp.float32)
        )
        grad_cross, ffn_grads = feed_backward(after_cross, grad_updated, ffn_kept, ffn_params)
        grad_branch = grad_cross.astype(jnp.bfloat16)
        cross_out_grad = weight_grad(cross_att, grad_branch)
        grad_att = project_back(grad_branch, cross_out).astype(jnp.bfloat16)
        query_grad, key_grad, value_grad = attend_backward(
            cross_queries, cross_keys, cross_values, cross_log, grad_att, tgt_seg, src_seg, 0
        )
        cross_query_grad = weight_grad(normed_c, query_grad)
        grad_in, cross_gain_grad, cross_shift_grad = norm_back(
            after, cross_gain, cross_shift, project_back(query_grad, cross_query)
        )
        grad_pairs = jnp.concatenate([key_grad, value_grad], axis=-1)
        tail_grads = ffn_grads + (vec_grad, offset_grad)
        cross_grads = (
            cross_gain_grad,
            cross_shift_grad,
            cross_query_grad,
            jnp.zeros(cross_kv.shape, jnp.float32),
            cross_out_grad,
        )
        return (result, grad_cross + grad_in, grad_current, grad_pairs, tail_grads, cross_grads)

    def encoder_rest(operands):
        after, arrived = operands
        zero_rows = jnp.zeros(after.shape, jnp.float32)
        zero_vec = jnp.zeros((feature_count,), jnp.float32)
        returned_zero = jnp.zeros(after.shape[:-1] + (2 * feature_count,), jnp.bfloat16)
        tail_zero = (
            zero_vec,
            zero_vec,
            jnp.zeros(up_weight[0].shape, jnp.float32),
            jnp.zeros(up_bias[0].shape, jnp.float32),
            jnp.zeros(down_weight[0].shape, jnp.float32),
            jnp.zeros(down_bias[0].shape, jnp.float32),
            zero_vec,
            jnp.zeros((), jnp.float32),
        )
        cross_zero = (
            zero_vec,
            zero_vec,
            jnp.zeros(cross_query.shape, jnp.float32),
            jnp.zeros(cross_kv.shape, jnp.float32),
            jnp.zeros(cross_out.shape, jnp.float32),
        )
        return (zero_rows, zero_rows, zero_rows, returned_zero, tail_zero, cross_zero)

    tail_out = lax.cond(decoding, decoder_tail, encoder_rest, (after_self, received))
    result, dec_grad_after, dec_grad_halt, returned_grad, dec_tail_grads, cross_grads = tail_out
    returned = from_behind(returned_grad, "section", -1)

    def encoder_tail():
        updated, ffn_kept = feed_forward(after_self, ffn_params)
        kv_extra = weight_grad(memory_low, returned)
        grad_memory = lax.optimization_barrier(
            project_back(returned, cross_kv).astype(jnp.bfloat16)
        ).astype(jnp.float32)
        grad_result = cotangent[0].astype(jnp.float32) + grad_memory
        outputs, pullback = jax.vjp(halt_local, current, updated, halt_vec, halt_offset)
        grad_current, grad_updated, vec_grad, offset_grad = pullback(grad_result)
        grad_after, ffn_grads = feed_backward(after_self, grad_updated, ffn_kept, ffn_params)
        return (grad_after, grad_current, ffn_grads + (vec_grad, offset_grad), kv_extra)

    def decoder_keep():
        return (
            dec_grad_after,
            dec_grad_halt,
            dec_tail_grads,
            jnp.zeros(cross_kv.shape, jnp.float32),
        )

    grad_after, grad_halt, tail_grads, kv_extra = lax.cond(decoding, decoder_keep, encoder_tail)
    grad_input, gain_grad, shift_grad, qkv_grad, out_grad = self_backward(
        current,
        grad_after,
        self_kept,
        norm_gain[0, 0],
        norm_shift[0, 0],
        qkv_weight[0],
        out_weight[0],
        own_seg,
        section_index,
    )
    input_grad = grad_input + grad_halt
    final = jnp.where(decoding, result, first_out)
    change = final - current
    row_rms = jnp.stack(
        [
            jnp.sqrt(jnp.mean(final * final, axis=(1, 2)) + 1e-06),
            jnp.sqrt(jnp.mean(change * change, axis=(1, 2)) + 1e-06),
        ],
        axis=-1,
    )
    vectors = jnp.concatenate(
        [
            jnp.stack([gain_grad, tail_grads[0], shift_grad, tail_grads[1]]),
            tail_grads[3].reshape(-1, feature_count),
            jnp.stack([tail_grads[5], tail_grads[6]]),
            jnp.full((1, feature_count), tail_grads[7]),
            jnp.stack([cross_grads[0], cross_grads[1]]),
        ]
    )
    vectors = jnp.sum(lax.all_gather(vectors, "dp"), axis=0)
    cross_vectors = vectors[-2:] + lax.ppermute(vectors[-2:], "section", [(0, 1), (1, 0)])
    count = lax.axis_size("dp")
    own = (qkv_grad, out_grad, tail_grads[2], tail_grads[4])
    crossing = (cross_grads[2], cross_grads[3] + kv_extra, cross_grads[4])
    own_rows = [array.size // (feature_count * count) for array in own]
    cross_rows = [array.size // (feature_count * count) for array in crossing]
    gathered = gather_sums(own, crossing, feature_count)
    summed, place = [], 0
    for array, rows in zip(own + crossing, own_rows + cross_rows):
        summed.append(
            gathered[:, place : place + rows].reshape(array.shape).astype(jnp.float32)
        )
        place += rows
    return (
        final.astype(jnp.bfloat16)[None],
        input_grad[None],
        row_rms[None],
        vectors[None, 0:2],
        vectors[None, 2:4],
        summed[0][None],
        summed[1][None],
        summed[2][None],
        vectors[4:-5].reshape(1, -1),
        summed[3][None],
        vectors[None, -5],
        vectors[None, -4],
        vectors[-3, :1],
        cross_vectors[0],
        cross_vectors[1],
        summed[4],
        summed[5],
        summed[6],
    )


def solution(mesh):
    in_specs = (
        P("section", "dp", None, None),
        P("section", "dp", None, None),
        P(None, "dp", None),
        P("section", "dp", None),
        P("section", None, None),
        P("section", None, None),
        P("section", None, None),
        P("section", None, None),
        P("section", None, None),
        P("section", None),
        P("section", None, None),
        P("section", None),
        P("section", None),
        P("section"),
        P(),
        P(),
        P(),
        P(),
        P(),
    )
    out_specs = (
        P("section", "dp", None, None),
        P("section", "dp", None, None),
        P("section", "dp", None),
        P("section", None, None),
        P("section", None, None),
        P("section", None, None),
        P("section", None, None),
        P("section", None, None),
        P("section", None),
        P("section", None, None),
        P("section", None),
        P("section", None),
        P("section"),
        P(),
        P(),
        P(),
        P(),
        P(),
    )
    return jax.shard_map(shards, mesh=mesh, in_specs=in_specs, out_specs=out_specs, check_vma=False)
```

```python
import functools

import jax
import jax.numpy as jnp
from jax import lax
from jax.experimental import pallas as pl
from jax.experimental.pallas import tpu as pltpu
from jax.sharding import PartitionSpec as P

L = 512
D = 512
FF = 2048
HEADS = 8
HEAD = D // HEADS
GROUP = 256
PER = GROUP // HEAD
RC = 256
EPS = 1e-05
MASKED = -1000000000.0
GELU_A = 0.7978845608028654
GELU_B = 0.044715
F32 = jnp.float32
BF16 = jnp.bfloat16

V_GAIN2, V_SHIFT2, V_UPB, V_DOWNB, V_HW, V_HB = 0, 1, 2, 6, 7, 8
V_GAINC, V_SHIFTC, V_GAIN1, V_SHIFT1, V_RMS = 9, 10, 11, 12, 13
V_ROWS = 16


def nn(left, right):
    return lax.dot_general(left, right, (((1,), (0,)), ((), ())), preferred_element_type=F32)


def nt(left, right):
    return lax.dot_general(left, right, (((1,), (1,)), ((), ())), preferred_element_type=F32)


def tn(left, right):
    return lax.dot_general(left, right, (((0,), (0,)), ((), ())), preferred_element_type=F32)


def col_sum(value):
    return jnp.sum(value, axis=0, keepdims=True)


def row_mean(value):
    return jnp.mean(value, axis=1, keepdims=True)


def normalize(value):
    centered = value - row_mean(value)
    scale = lax.rsqrt(row_mean(centered * centered) + EPS)
    return centered * scale, scale


def norm_input_grad(grad, gain, xhat, scale):
    scaled = grad * gain
    return scale * (scaled - row_mean(scaled) - xhat * row_mean(scaled * xhat))


def row_chunks():
    return [slice(place, place + RC) for place in range(0, L, RC)]


def head_masks():
    lane = lax.broadcasted_iota(jnp.int32, (1, GROUP), 1)
    return [(lane // HEAD) == place for place in range(PER)]


def keep(mask, value):
    return jnp.where(mask, value, jnp.zeros_like(value))


def segments(len_ref, side, row, shape, dim):
    place = lax.broadcasted_iota(jnp.int32, shape, dim)
    total = jnp.int32(0)
    found = jnp.zeros(shape, jnp.int32)
    for index in range(len_ref.shape[2]):
        total = total + len_ref[side, row, index]
        found = found + (place >= total).astype(jnp.int32)
    return found


def write_bias(bias_ref, len_ref, row, row_side, col_side, causal_sign, causal):
    down = segments(len_ref, row_side, row, (L, 1), 0)
    across = segments(len_ref, col_side, row, (1, L), 1)
    for part in row_chunks():
        allowed = down[part] == across
        if causal is not None:
            row_place = lax.broadcasted_iota(jnp.int32, (RC, L), 0) + part.start
            col_place = lax.broadcasted_iota(jnp.int32, (RC, L), 1)
            ordered = (row_place - col_place) * causal_sign >= 0
            allowed = allowed & (ordered | jnp.logical_not(causal))
        bias_ref[part, :] = jnp.where(allowed, 0.0, MASKED)


def attend_forward(queries, keys, values, bias_ref, out_ref, stat_ref):
    masks = head_masks()
    lane = lax.broadcasted_iota(jnp.int32, (1, 128), 1)
    stats = jnp.zeros((L, 128), F32)
    for group in range(HEADS // PER):
        cols = slice(group * GROUP, (group + 1) * GROUP)
        weights = []
        for place in range(PER):
            scores = nt(keep(masks[place], queries(cols)), keys(cols)) + bias_ref[...]
            top = jnp.max(scores, axis=1, keepdims=True)
            expanded = jnp.exp(scores - top)
            total = jnp.sum(expanded, axis=1, keepdims=True)
            weights.append((expanded * (1.0 / total)).astype(BF16))
            stats = jnp.where(lane == group * PER + place, top + jnp.log(total), stats)
        stacked = jnp.concatenate([keep(mask, values(cols)) for mask in masks], axis=0)
        out_ref[:, cols] = nn(jnp.concatenate(weights, axis=1), stacked).astype(BF16)
    stat_ref[...] = stats.T


def attend_backward(queries, keys, values, grads, bias_ref, stat_ref, turned_ref, dq_ref, out):
    masks = head_masks()
    for group in range(HEADS // PER):
        cols = slice(group * GROUP, (group + 1) * GROUP)
        turned_ref[cols, :] = keys(cols).T
        grad_scores, weights = [], []
        for place in range(PER):
            head = group * PER + place
            rows = slice(head * HEAD, (head + 1) * HEAD)
            scores = nt(keep(masks[place], keys(cols)), queries(cols)) + bias_ref[...]
            probs = jnp.exp(scores - stat_ref[head : head + 1, :])
            grad_weights = nt(keep(masks[place], values(cols)), grads(cols))
            inner = col_sum(probs * grad_weights)
            grad_score = (probs * (grad_weights - inner)).astype(BF16)
            dq_ref[rows, :] = nn(turned_ref[rows, :], grad_score)
            grad_scores.append(grad_score)
            weights.append(probs.astype(BF16))
        stacked = jnp.concatenate([keep(mask, queries(cols)) for mask in masks], axis=0)
        out(1, cols, nn(jnp.concatenate(grad_scores, axis=1), stacked).astype(BF16))
        stacked = jnp.concatenate([keep(mask, grads(cols)) for mask in masks], axis=0)
        out(2, cols, nn(jnp.concatenate(weights, axis=1), stacked).astype(BF16))


def gelu_parts(pre):
    square = pre * pre
    inner = jnp.tanh(GELU_A * pre * (1.0 + GELU_B * square))
    half = 0.5 * (1.0 + inner)
    slope = half + 0.5 * pre * (1.0 - inner * inner) * (GELU_A * (1.0 + 3.0 * GELU_B * square))
    return pre * half, slope


def feed_forward(after_ref, norm_gain, norm_shift, w_up, up_bias, w_down, down_bias, n2_ref, act_ref, slope_ref, part):
    after = after_ref[part, :]
    normed = (normalize(after)[0] * norm_gain[1:2] + norm_shift[1:2]).astype(BF16)
    n2_ref[part, :] = normed
    total = after + down_bias[...]
    for start in range(0, FF, D):
        cols = slice(start, start + D)
        activated, slope = gelu_parts(nn(normed, w_up[:, cols]) + up_bias[:, cols])
        activated = activated.astype(BF16)
        act_ref[part, cols] = activated
        slope_ref[part, cols] = slope.astype(BF16)
        total = total + nn(activated, w_down[cols, :])
    return total


def feed_backward(after_ref, grad, norm_gain, w_up, w_down, slope_ref, gb_ref, gp_ref, vec_ref, part):
    branch = grad.astype(BF16)
    gb_ref[part, :] = branch
    vec_ref[V_DOWNB : V_DOWNB + 1, :] += col_sum(branch.astype(F32))
    back = jnp.zeros((RC, D), F32)
    for index, start in enumerate(range(0, FF, D)):
        cols = slice(start, start + D)
        pre_grad = (nt(branch, w_down[cols, :]) * slope_ref[part, cols].astype(F32)).astype(BF16)
        gp_ref[part, cols] = pre_grad
        vec_ref[V_UPB + index : V_UPB + index + 1, :] += col_sum(pre_grad.astype(F32))
        back = back + nt(pre_grad, w_up[:, cols])
    xhat, scale = normalize(after_ref[part, :])
    vec_ref[V_GAIN2 : V_GAIN2 + 1, :] += col_sum(back * xhat)
    vec_ref[V_SHIFT2 : V_SHIFT2 + 1, :] += col_sum(back)
    return grad + norm_input_grad(back, norm_gain[1:2], xhat, scale)


def halting_share(current, run_ref, halt_weight, halt_bias, part):
    logit = jnp.sum(current * halt_weight[...], axis=1, keepdims=True) + halt_bias[0]
    rate = jax.nn.sigmoid(logit)
    return run_ref[part, :] * rate, rate


def halting_backward(grad, change, current, share, rate, run_ref, halt_weight, vec_ref, part):
    logit_grad = (
        run_ref[part, :] * jnp.sum(grad * change, axis=1, keepdims=True) * rate * (1.0 - rate)
    )
    vec_ref[V_HW : V_HW + 1, :] += col_sum(logit_grad * current)
    vec_ref[V_HB : V_HB + 1, :] += jnp.broadcast_to(col_sum(logit_grad), (1, D))
    return share * grad, (1.0 - share) * grad + logit_grad * halt_weight[...]


def write_rms(vec_ref, total_ref):
    lane = lax.broadcasted_iota(jnp.int32, (1, D), 1)
    vec_ref[V_RMS : V_RMS + 1, :] = jnp.where(lane == 0, total_ref[0], total_ref[1])


class Copies:
    def __init__(self, sems, pairs):
        self.made = {
            name: pltpu.make_async_copy(source, target, sems.at[index])
            for index, (name, source, target) in enumerate(pairs)
        }

    def start(self, *names):
        for name in names:
            self.made[name].start()

    def wait(self, *names):
        for name in names:
            self.made[name].wait()


def kernel_a(
    row,
    sec_ref, len_ref, hb_ref, run_ref, ng_ref, ns_ref, ub_ref, db_ref, hw_ref, cg_ref, cs_ref,
    x_hbm, wqkv_hbm, wout_hbm, wup_hbm, wdn_hbm, wcq_hbm,
    vec_ref, out_hbm, after_hbm, packed_hbm, att_hbm, stat_hbm, normed_hbm, n2_hbm, act_hbm, slope_hbm, change_hbm,
    x, wqkv, wout, wup, wdn, wcq, out, after, packed, att, stat, normed, n2, act, slope, change, bias, total, sems,
):
    encoding = sec_ref[0] == 0
    copies = Copies(
        sems,
        [
            ("x", x_hbm.at[0, row], x),
            ("wqkv", wqkv_hbm.at[0], wqkv),
            ("wout", wout_hbm.at[0], wout),
            ("wup", wup_hbm.at[0], wup),
            ("wdn", wdn_hbm.at[0], wdn),
            ("wcq", wcq_hbm, wcq),
            ("out", out, out_hbm),
            ("after", after, after_hbm),
            ("packed", packed, packed_hbm),
            ("att", att, att_hbm),
            ("stat", stat, stat_hbm),
            ("normed", normed, normed_hbm),
            ("n2", n2, n2_hbm),
            ("act", act, act_hbm),
            ("slope", slope, slope_hbm),
            ("change", change, change_hbm),
        ],
    )
    copies.start("x", "wqkv", "wout")

    @pl.when(encoding)
    def _():
        copies.start("wup", "wdn")

    @pl.when(jnp.logical_not(encoding))
    def _():
        copies.start("wcq")

    vec_ref[...] = jnp.zeros_like(vec_ref)
    side = sec_ref[0]
    write_bias(bias, len_ref, row, side, side, 1, jnp.logical_not(encoding))
    copies.wait("x", "wqkv")
    for part in row_chunks():
        current = x[part, :].astype(F32)
        value = (normalize(current)[0] * ng_ref[0:1] + ns_ref[0:1]).astype(BF16)
        normed[part, :] = value
        packed[part, 0:D] = (nn(value, wqkv[:, 0:D]).astype(BF16).astype(F32) * HEAD**-0.5).astype(BF16)
        packed[part, D : 2 * D] = nn(value, wqkv[:, D : 2 * D]).astype(BF16)
        packed[part, 2 * D :] = nn(value, wqkv[:, 2 * D :]).astype(BF16)
    copies.start("normed", "packed")
    attend_forward(
        lambda cols: packed[:, cols],
        lambda cols: packed[:, D + cols.start : D + cols.stop],
        lambda cols: packed[:, 2 * D + cols.start : 2 * D + cols.stop],
        bias, att, stat,
    )
    copies.start("att", "stat")
    copies.wait("wout")
    for part in row_chunks():
        after[part, :] = x[part, :].astype(F32) + nn(att[part, :], wout[...])
    copies.start("after")

    @pl.when(encoding)
    def _():
        copies.wait("wup", "wdn")
        total[0] = 0.0
        total[1] = 0.0
        for part in row_chunks():
            updated = feed_forward(after, ng_ref, ns_ref, wup, ub_ref, wdn, db_ref, n2, act, slope, part)
            current = x[part, :].astype(F32)
            share, _ = halting_share(current, run_ref, hw_ref, hb_ref, part)
            moved = updated - current
            change[part, :] = moved.astype(BF16)
            moved = share * moved
            result = current + moved
            out[part, :] = result.astype(BF16)
            total[0] += jnp.sum(result * result)
            total[1] += jnp.sum(moved * moved)
        copies.start("out", "n2", "act", "slope", "change")
        write_rms(vec_ref, total)
        copies.wait("n2", "act", "slope", "change")

    @pl.when(jnp.logical_not(encoding))
    def _():
        copies.wait("wcq")
        for part in row_chunks():
            value = (normalize(after[part, :])[0] * cg_ref[...] + cs_ref[...]).astype(BF16)
            change[part, :] = value
            out[part, :] = (nn(value, wcq[...]).astype(BF16).astype(F32) * HEAD**-0.5).astype(BF16)
        copies.start("out", "change")
        copies.wait("change")

    copies.wait("normed", "packed", "att", "stat", "after", "out")


def kernel_b(
    row,
    sec_ref, len_ref, hb_ref, run_ref, ng_ref, ns_ref, ub_ref, db_ref, hw_ref, cg_ref, cs_ref,
    x_hbm, cot_hbm, wup_hbm, wdn_hbm, wcq_hbm, wkv_hbm, wco_hbm, mem_hbm, cq_hbm, after_hbm, _n2_hbm, _act_hbm,
    vec_ref, n2_hbm, act_hbm, gb_hbm, gp_hbm, att_hbm, gc_hbm, gq_hbm, gkv_hbm, back_hbm, result_hbm, ga_hbm, gx_hbm,
    x, cot, wup, wdn, wcq, wkv, wco, mem, cq, after, n2, act, gb, gp, att, gc, gq, gkv, back, result, gaf, gx,
    kv, slope, across, gatt, bias, stat, turned, dq, total, sems,
):
    vec_ref[...] = jnp.zeros_like(vec_ref)
    copies = Copies(
        sems,
        [
            ("x", x_hbm.at[0, row], x),
            ("cot", cot_hbm.at[0, row], cot),
            ("wup", wup_hbm.at[0], wup),
            ("wdn", wdn_hbm.at[0], wdn),
            ("wcq", wcq_hbm, wcq),
            ("wkv", wkv_hbm, wkv),
            ("wco", wco_hbm, wco),
            ("mem", mem_hbm, mem),
            ("cq", cq_hbm, cq),
            ("after", after_hbm, after),
            ("n2", n2, n2_hbm),
            ("act", act, act_hbm),
            ("gb", gb, gb_hbm),
            ("gp", gp, gp_hbm),
            ("att", att, att_hbm),
            ("gc", gc, gc_hbm),
            ("gq", gq, gq_hbm),
            ("gkv", gkv, gkv_hbm),
            ("back", back, back_hbm),
            ("result", result, result_hbm),
            ("ga", gaf, ga_hbm),
            ("gx", gx, gx_hbm),
        ],
    )

    @pl.when(sec_ref[0] == 1)
    def _():
        copies.start("mem", "wkv", "cq", "after", "wco", "wup", "wdn", "x", "cot", "wcq")
        write_bias(bias, len_ref, row, 1, 0, 1, None)
        copies.wait("mem", "wkv")
        for part in row_chunks():
            kv[part, 0:D] = nn(mem[part, :], wkv[:, 0:D]).astype(BF16)
            kv[part, D:] = nn(mem[part, :], wkv[:, D:]).astype(BF16)
        copies.wait("cq")
        attend_forward(
            lambda cols: cq[:, cols],
            lambda cols: kv[:, cols],
            lambda cols: kv[:, D + cols.start : D + cols.stop],
            bias, att, stat,
        )
        copies.start("att")
        copies.wait("after", "wco", "wup", "wdn", "x", "cot")
        total[0] = 0.0
        total[1] = 0.0
        for part in row_chunks():
            across[part, :] = after[part, :] + nn(att[part, :], wco[...])
            updated = feed_forward(across, ng_ref, ns_ref, wup, ub_ref, wdn, db_ref, n2, act, slope, part)
            current = x[part, :].astype(F32)
            share, rate = halting_share(current, run_ref, hw_ref, hb_ref, part)
            change = updated - current
            moved = share * change
            value = current + moved
            result[part, :] = value.astype(BF16)
            total[0] += jnp.sum(value * value)
            total[1] += jnp.sum(moved * moved)
            grad, own = halting_backward(
                cot[part, :].astype(F32), change, current, share, rate, run_ref, hw_ref, vec_ref, part
            )
            gx[part, :] = own
            grad = feed_backward(across, grad, ng_ref, wup, wdn, slope, gb, gp, vec_ref, part)
            gaf[part, :] = grad
            branch = grad.astype(BF16)
            gc[part, :] = branch
            gatt[part, :] = nt(branch, wco[...]).astype(BF16)
        copies.start("n2", "act", "gb", "gp", "gc", "result", "gx")
        write_rms(vec_ref, total)
        write_bias(bias, len_ref, row, 0, 1, 1, None)

        def store(kind, cols, value):
            start = (kind - 1) * D
            gkv[:, start + cols.start : start + cols.stop] = value

        attend_backward(
            lambda cols: cq[:, cols],
            lambda cols: kv[:, cols],
            lambda cols: kv[:, D + cols.start : D + cols.stop],
            lambda cols: gatt[:, cols],
            bias, stat, turned, dq, store,
        )
        copies.start("gkv")
        for part in row_chunks():
            back[part, :] = (
                nt(gkv[part, 0:D], wkv[:, 0:D]) + nt(gkv[part, D:], wkv[:, D:])
            ).astype(BF16)
        copies.start("back")
        gq[...] = (dq[...] * HEAD**-0.5).astype(BF16).T
        copies.start("gq")
        copies.wait("wcq")
        for part in row_chunks():
            grad = nt(gq[part, :], wcq[...])
            xhat, scale = normalize(after[part, :])
            vec_ref[V_GAINC : V_GAINC + 1, :] += col_sum(grad * xhat)
            vec_ref[V_SHIFTC : V_SHIFTC + 1, :] += col_sum(grad)
            gaf[part, :] += norm_input_grad(grad, cg_ref[...], xhat, scale)
        copies.start("ga")
        copies.wait(
            "att", "n2", "act", "gb", "gp", "gc", "result", "gx", "gkv", "back", "gq", "ga"
        )


def kernel_c(
    row,
    sec_ref, len_ref, hb_ref, run_ref, ng_ref, ub_ref, hw_ref,
    x_hbm, cot_hbm, wqkv_hbm, wout_hbm, wup_hbm, wdn_hbm, back_hbm, after_hbm, packed_hbm, stat_hbm, slope_hbm,
    change_hbm, ga_hbm, gx_hbm, _gb_hbm, _gp_hbm,
    vec_ref, gb_hbm, gp_hbm, gs_hbm, gpack_hbm, grad_hbm,
    x, cot, wqkv, wout, wup, wdn, back, after, packed, stat, slope, change, gaf, gx, gb, gp, gs, gpack, grad_out,
    gatt, bias, turned, dq, sems,
):
    encoding = sec_ref[0] == 0
    vec_ref[...] = jnp.zeros_like(vec_ref)
    copies = Copies(
        sems,
        [
            ("x", x_hbm.at[0, row], x),
            ("cot", cot_hbm.at[0, row], cot),
            ("wqkv", wqkv_hbm.at[0], wqkv),
            ("wout", wout_hbm.at[0], wout),
            ("wup", wup_hbm.at[0], wup),
            ("wdn", wdn_hbm.at[0], wdn),
            ("back", back_hbm, back),
            ("after", after_hbm, after),
            ("packed", packed_hbm, packed),
            ("stat", stat_hbm, stat),
            ("slope", slope_hbm, slope),
            ("change", change_hbm, change),
            ("ga", ga_hbm, gaf),
            ("gx", gx_hbm, gx),
            ("gb", gb, gb_hbm),
            ("gp", gp, gp_hbm),
            ("gs", gs, gs_hbm),
            ("gpack", gpack, gpack_hbm),
            ("grad", grad_out, grad_hbm),
        ],
    )

    @pl.when(encoding)
    def _():
        copies.start("cot", "back", "change", "after", "wdn", "slope", "wup")

    @pl.when(jnp.logical_not(encoding))
    def _():
        copies.start("ga", "gx")

    copies.start("x", "wout", "packed", "stat", "wqkv")
    side = sec_ref[0]
    write_bias(bias, len_ref, row, side, side, -1, jnp.logical_not(encoding))
    copies.wait("x")

    @pl.when(encoding)
    def _():
        copies.wait("cot", "back", "change", "after", "wdn", "slope", "wup")
        for part in row_chunks():
            grad = cot[part, :].astype(F32) + back[part, :].astype(F32)
            current = x[part, :].astype(F32)
            share, rate = halting_share(current, run_ref, hw_ref, hb_ref, part)
            grad, own = halting_backward(
                grad, change[part, :].astype(F32), current, share, rate, run_ref, hw_ref, vec_ref, part
            )
            gx[part, :] = own
            gaf[part, :] = feed_backward(after, grad, ng_ref, wup, wdn, slope, gb, gp, vec_ref, part)
        copies.start("gb", "gp")

    @pl.when(jnp.logical_not(encoding))
    def _():
        copies.wait("ga", "gx")

    copies.wait("wout")
    for part in row_chunks():
        branch = gaf[part, :].astype(BF16)
        gs[part, :] = branch
        gatt[part, :] = nt(branch, wout[...]).astype(BF16)
    copies.start("gs")
    copies.wait("packed", "stat")

    def store(kind, cols, value):
        gpack[:, kind * D + cols.start : kind * D + cols.stop] = value

    attend_backward(
        lambda cols: packed[:, cols],
        lambda cols: packed[:, D + cols.start : D + cols.stop],
        lambda cols: packed[:, 2 * D + cols.start : 2 * D + cols.stop],
        lambda cols: gatt[:, cols],
        bias, stat, turned, dq, store,
    )
    gpack[:, 0:D] = (dq[...] * HEAD**-0.5).astype(BF16).T
    copies.start("gpack")
    copies.wait("wqkv")
    for part in row_chunks():
        grad = nt(gpack[part, 0:D], wqkv[:, 0:D])
        grad += nt(gpack[part, D : 2 * D], wqkv[:, D : 2 * D])
        grad += nt(gpack[part, 2 * D :], wqkv[:, 2 * D :])
        xhat, scale = normalize(x[part, :].astype(F32))
        vec_ref[V_GAIN1 : V_GAIN1 + 1, :] += col_sum(grad * xhat)
        vec_ref[V_SHIFT1 : V_SHIFT1 + 1, :] += col_sum(grad)
        grad_out[part, :] = gaf[part, :] + gx[part, :] + norm_input_grad(grad, ng_ref[0:1], xhat, scale)
    copies.start("grad")

    @pl.when(encoding)
    def _():
        copies.wait("gb", "gp")

    copies.wait("gs", "gpack", "grad")


def any_spec():
    return pl.BlockSpec(memory_space=pl.ANY)


def vmem_spec():
    return pl.BlockSpec(memory_space=pltpu.VMEM)


def smem_spec():
    return pl.BlockSpec(memory_space=pltpu.SMEM)


def shape(*dims, dtype=BF16):
    return jax.ShapeDtypeStruct(dims, dtype)


def scratch_of(shapes):
    return [pltpu.VMEM(item.shape, item.dtype) for item in shapes]


PARAMS = pltpu.CompilerParams(vmem_limit_bytes=60 * 1024 * 1024)


def call_a(row, scalars, vectors, arrays):
    x, wqkv, wout, wup, wdn, wcq = arrays
    outs = [
        shape(L, D), shape(L, D, dtype=F32), shape(L, 3 * D), shape(L, D), shape(128, L, dtype=F32), shape(L, D),
        shape(L, D), shape(L, FF), shape(L, FF), shape(L, D),
    ]
    return pl.pallas_call(
        functools.partial(kernel_a, row),
        out_shape=[shape(V_ROWS, D, dtype=F32)] + outs,
        in_specs=[smem_spec()] * 3 + [vmem_spec()] * len(vectors) + [any_spec()] * len(arrays),
        out_specs=[vmem_spec()] + [any_spec()] * len(outs),
        scratch_shapes=scratch_of(
            [shape(L, D), shape(D, 3 * D), shape(D, D), shape(D, FF), shape(FF, D), shape(D, D)]
            + outs
            + [shape(L, L, dtype=F32)]
        )
        + [pltpu.SMEM((2,), F32), pltpu.SemaphoreType.DMA((16,))],
        compiler_params=PARAMS,
        name="forward_a",
    )(*scalars, *vectors, *arrays)


def call_b(row, scalars, vectors, arrays):
    outs = [
        shape(L, D), shape(L, FF), shape(L, D), shape(L, FF), shape(L, D), shape(L, D), shape(L, D), shape(L, 2 * D),
        shape(L, D), shape(L, D), shape(L, D, dtype=F32), shape(L, D, dtype=F32),
    ]
    before = 3 + len(vectors)
    return pl.pallas_call(
        functools.partial(kernel_b, row),
        out_shape=[shape(V_ROWS, D, dtype=F32)] + outs,
        in_specs=[smem_spec()] * 3 + [vmem_spec()] * len(vectors) + [any_spec()] * len(arrays),
        out_specs=[vmem_spec()] + [any_spec()] * len(outs),
        scratch_shapes=scratch_of(
            [
                shape(L, D), shape(L, D), shape(D, FF), shape(FF, D), shape(D, D), shape(D, 2 * D), shape(D, D),
                shape(L, D), shape(L, D), shape(L, D, dtype=F32),
            ]
            + outs
            + [
                shape(L, 2 * D), shape(L, FF), shape(L, D, dtype=F32), shape(L, D), shape(L, L, dtype=F32),
                shape(128, L, dtype=F32), shape(D, L), shape(D, L, dtype=F32),
            ]
        )
        + [pltpu.SMEM((2,), F32), pltpu.SemaphoreType.DMA((22,))],
        input_output_aliases={before + len(arrays) - 2: 1, before + len(arrays) - 1: 2},
        compiler_params=PARAMS,
        name="decoder_b",
    )(*scalars, *vectors, *arrays)


def call_c(row, scalars, vectors, arrays):
    outs = [shape(L, D), shape(L, FF), shape(L, D), shape(L, 3 * D), shape(L, D, dtype=F32)]
    before = 3 + len(vectors)
    return pl.pallas_call(
        functools.partial(kernel_c, row),
        out_shape=[shape(V_ROWS, D, dtype=F32)] + outs,
        in_specs=[smem_spec()] * 3 + [vmem_spec()] * len(vectors) + [any_spec()] * len(arrays),
        out_specs=[vmem_spec()] + [any_spec()] * len(outs),
        scratch_shapes=scratch_of(
            [
                shape(L, D), shape(L, D), shape(D, 3 * D), shape(D, D), shape(D, FF), shape(FF, D),
                shape(L, D), shape(L, D, dtype=F32), shape(L, 3 * D), shape(128, L, dtype=F32), shape(L, FF),
                shape(L, D), shape(L, D, dtype=F32), shape(L, D, dtype=F32),
            ]
            + outs
            + [shape(L, D), shape(L, L, dtype=F32), shape(D, L), shape(D, L, dtype=F32)]
        )
        + [pltpu.SemaphoreType.DMA((19,))],
        input_output_aliases={before + len(arrays) - 2: 1, before + len(arrays) - 1: 2},
        compiler_params=PARAMS,
        name="backward_c",
    )(*scalars, *vectors, *arrays)


def weight_kernel(pairs, only, *refs):
    sec_ref, refs = refs[0], refs[1:]
    count = len(pairs)
    operands, outs = refs[: 4 * count], refs[4 * count : 5 * count]

    def work():
        for index in range(count):
            left0, left1, right0, right1 = operands[4 * index : 4 * index + 4]
            for lcol in range(0, left0.shape[1], D):
                for rcol in range(0, right0.shape[1], D):
                    value = tn(left0[:, lcol : lcol + D], right0[:, rcol : rcol + D])
                    value += tn(left1[:, lcol : lcol + D], right1[:, rcol : rcol + D])
                    outs[index][lcol + rcol : lcol + rcol + D, :] = value.astype(BF16)

    if only is None:
        work()
    else:
        pl.when(sec_ref[0] == only)(work)

        @pl.when(sec_ref[0] != only)
        def _():
            for out in outs:
                out[...] = jnp.zeros_like(out)


def weight_grads(sec, only, groups, name):
    flat, outs = [], []
    for lefts, rights in groups:
        flat += [*lefts, *rights]
        blocks = (lefts[0].shape[1] // D) * (rights[0].shape[1] // D)
        outs.append(shape(blocks * D, D))
    return pl.pallas_call(
        functools.partial(weight_kernel, groups, only),
        out_shape=outs,
        in_specs=[smem_spec()] + [vmem_spec()] * len(flat),
        out_specs=[vmem_spec()] * len(outs),
        compiler_params=PARAMS,
        name=name,
    )(sec, *flat)


def side_by_side(blocks):
    count = blocks.shape[0] // D
    return jnp.concatenate([blocks[i * D : (i + 1) * D] for i in range(count)], axis=1)


def gather_sums(own, crossing):
    count = lax.axis_size("dp")

    def laid_out(arrays):
        return [array.reshape(count, -1, D) for array in arrays]

    held = jnp.concatenate(laid_out(own) + laid_out(crossing), axis=1)
    own_rows = sum(array.shape[0] for array in own) // count
    share = lax.psum_scatter(held.reshape(-1, D), "dp", tiled=True)
    swapped = lax.ppermute(share[own_rows:], "section", [(0, 1), (1, 0)])
    share = jnp.concatenate([share[:own_rows], share[own_rows:] + swapped])
    gathered = lax.all_gather(share, "dp")
    parts, place = [], 0
    for array in own + crossing:
        rows = array.shape[0] // count
        parts.append(gathered[:, place : place + rows].reshape(array.shape).astype(F32))
        place += rows
    return parts


def shards(
    inputs, cotangent, lengths, running, norm_gain, norm_shift, qkv_weight, out_weight, up_weight, up_bias,
    down_weight, down_bias, halt_weight, halt_bias, cross_gain, cross_shift, cross_query, cross_kv, cross_out,
):
    section = lax.axis_index("section").astype(jnp.int32)
    decoding = section == 1
    sec = section.reshape(1)
    scalars = (sec, lengths, halt_bias)
    runs = running[0].astype(F32)[..., None]
    rows = range(inputs.shape[1])
    vectors = (norm_gain[0], norm_shift[0], up_bias, down_bias, halt_weight, cross_gain[None], cross_shift[None])
    firsts, received = [], []
    for row in rows:
        firsts.append(
            call_a(
                row, scalars, (runs[row],) + vectors,
                (inputs, qkv_weight, out_weight, up_weight, down_weight, cross_query),
            )
        )
        received.append(lax.ppermute(firsts[row][1], "section", [(0, 1)]))
    middles, returned = [], []
    for row in rows:
        _, out, after, _, _, _, _, n2, act, _, _ = firsts[row]
        middles.append(
            call_b(
                row, scalars, (runs[row],) + vectors,
                (
                    inputs, cotangent, up_weight, down_weight, cross_query, cross_kv, cross_out, received[row], out,
                    after, n2, act,
                ),
            )
        )
        returned.append(lax.ppermute(middles[row][9], "section", [(1, 0)]))
    lasts = []
    for row in rows:
        _, _, after, packed, _, stat, _, _, _, slope, change = firsts[row]
        middle = middles[row]
        lasts.append(
            call_c(
                row, scalars, (runs[row], norm_gain[0], up_bias, halt_weight),
                (
                    inputs, cotangent, qkv_weight, out_weight, up_weight, down_weight, returned[row], after, packed,
                    stat, slope, change, middle[11], middle[12], middle[3], middle[4],
                ),
            )
        )

    def both(items, index):
        return [item[index] for item in items]

    cross_out_grad, cross_query_grad, cross_kv_grad = weight_grads(
        sec, 1,
        [
            (both(middles, 5), both(middles, 6)),
            (both(firsts, 10), both(middles, 7)),
            (received, both(middles, 8)),
        ],
        "cross_weights",
    )
    up_grad, down_grad = weight_grads(
        sec, None,
        [(both(middles, 1), both(lasts, 2)), (both(middles, 2), both(lasts, 1))],
        "feed_weights",
    )
    qkv_grad, out_grad = weight_grads(
        sec, None,
        [(both(firsts, 6), both(lasts, 4)), (both(firsts, 4), both(lasts, 3))],
        "self_weights",
    )
    own = (qkv_grad, out_grad, up_grad, down_grad)
    crossing = (cross_query_grad, cross_kv_grad, cross_out_grad)
    sums = gather_sums(own, crossing)
    vec = sum(both(middles, 0)) + sum(both(lasts, 0))
    vec = jnp.sum(lax.all_gather(vec[:V_RMS], "dp"), axis=0)
    cross_vec = vec[V_GAINC : V_SHIFTC + 1]
    cross_vec = cross_vec + lax.ppermute(cross_vec, "section", [(0, 1), (1, 0)])
    stats = jnp.stack(
        [jnp.where(decoding, middles[row][0], firsts[row][0])[V_RMS, :2] for row in rows]
    )
    row_rms = jnp.sqrt(stats / (L * D) + 1e-06)
    final = jnp.stack([jnp.where(decoding, middles[row][10], firsts[row][1]) for row in rows])
    input_grad = jnp.stack(both(lasts, 5))
    return (
        final[None],
        input_grad[None],
        row_rms[None],
        jnp.stack([vec[V_GAIN1], vec[V_GAIN2]])[None],
        jnp.stack([vec[V_SHIFT1], vec[V_SHIFT2]])[None],
        side_by_side(sums[0])[None],
        sums[1][None],
        side_by_side(sums[2])[None],
        vec[V_UPB : V_UPB + 4].reshape(1, FF),
        sums[3][None],
        vec[V_DOWNB][None],
        vec[V_HW][None],
        vec[V_HB, :1],
        cross_vec[0],
        cross_vec[1],
        sums[4],
        side_by_side(sums[5]),
        sums[6],
    )


def solution(mesh):
    in_specs = (
        P("section", "dp", None, None),
        P("section", "dp", None, None),
        P(None, "dp", None),
        P("section", "dp", None),
        P("section", None, None),
        P("section", None, None),
        P("section", None, None),
        P("section", None, None),
        P("section", None, None),
        P("section", None),
        P("section", None, None),
        P("section", None),
        P("section", None),
        P("section"),
        P(),
        P(),
        P(),
        P(),
        P(),
    )
    out_specs = (
        P("section", "dp", None, None),
        P("section", "dp", None, None),
        P("section", "dp", None),
        P("section", None, None),
        P("section", None, None),
        P("section", None, None),
        P("section", None, None),
        P("section", None, None),
        P("section", None),
        P("section", None, None),
        P("section", None),
        P("section", None),
        P("section"),
        P(),
        P(),
        P(),
        P(),
        P(),
    )
    return jax.shard_map(shards, mesh=mesh, in_specs=in_specs, out_specs=out_specs, check_vma=False)
```

```python
import functools

import jax
import jax.numpy as jnp
from jax import lax
from jax.experimental import pallas as pl
from jax.experimental.pallas import tpu as pltpu
from jax.sharding import PartitionSpec as P

L = 512
D = 512
FF = 2048
HEADS = 8
HEAD = D // HEADS
GROUP = 256
PER = GROUP // HEAD
RC = 256
EPS = 1e-05
MASKED = -1000000000.0
GELU_A = 0.7978845608028654
GELU_B = 0.044715
F32 = jnp.float32
BF16 = jnp.bfloat16

V_GAIN2, V_SHIFT2, V_UPB, V_DOWNB, V_HW, V_HB = 0, 1, 2, 6, 7, 8
V_GAINC, V_SHIFTC, V_GAIN1, V_SHIFT1, V_RMS = 9, 10, 11, 12, 13
V_ROWS = 16


def nn(left, right):
    return lax.dot_general(left, right, (((1,), (0,)), ((), ())), preferred_element_type=F32)


def nt(left, right):
    return lax.dot_general(left, right, (((1,), (1,)), ((), ())), preferred_element_type=F32)


def tn(left, right):
    return lax.dot_general(left, right, (((0,), (0,)), ((), ())), preferred_element_type=F32)


def col_sum(value):
    return jnp.sum(value, axis=0, keepdims=True)


def row_mean(value):
    return jnp.mean(value, axis=1, keepdims=True)


def normalize(value):
    centered = value - row_mean(value)
    scale = lax.rsqrt(row_mean(centered * centered) + EPS)
    return centered * scale, scale


def norm_input_grad(grad, gain, xhat, scale):
    scaled = grad * gain
    return scale * (scaled - row_mean(scaled) - xhat * row_mean(scaled * xhat))


def row_chunks():
    return [slice(place, place + RC) for place in range(0, L, RC)]


def head_masks():
    lane = lax.broadcasted_iota(jnp.int32, (1, GROUP), 1)
    return [(lane // HEAD) == place for place in range(PER)]


def keep(mask, value):
    return jnp.where(mask, value, jnp.zeros_like(value))


def segments(len_ref, side, row, shape, dim):
    place = lax.broadcasted_iota(jnp.int32, shape, dim)
    total = jnp.int32(0)
    found = jnp.zeros(shape, jnp.int32)
    for index in range(len_ref.shape[2]):
        total = total + len_ref[side, row, index]
        found = found + (place >= total).astype(jnp.int32)
    return found


def write_bias(bias_ref, len_ref, row, row_side, col_side, causal_sign, causal):
    down = segments(len_ref, row_side, row, (L, 1), 0)
    across = segments(len_ref, col_side, row, (1, L), 1)
    for part in row_chunks():
        allowed = down[part] == across
        if causal is not None:
            row_place = lax.broadcasted_iota(jnp.int32, (RC, L), 0) + part.start
            col_place = lax.broadcasted_iota(jnp.int32, (RC, L), 1)
            ordered = (row_place - col_place) * causal_sign >= 0
            allowed = allowed & (ordered | jnp.logical_not(causal))
        bias_ref[part, :] = jnp.where(allowed, 0.0, MASKED)


def attend_forward(queries, keys, values, bias_ref, out_ref, stat_ref):
    masks = head_masks()
    lane = lax.broadcasted_iota(jnp.int32, (1, 128), 1)
    stats = jnp.zeros((L, 128), F32)
    for group in range(HEADS // PER):
        cols = slice(group * GROUP, (group + 1) * GROUP)
        weights = []
        for place in range(PER):
            scores = nt(keep(masks[place], queries(cols)), keys(cols)) + bias_ref[...]
            top = jnp.max(scores, axis=1, keepdims=True)
            expanded = jnp.exp(scores - top)
            total = jnp.sum(expanded, axis=1, keepdims=True)
            weights.append((expanded * (1.0 / total)).astype(BF16))
            stats = jnp.where(lane == group * PER + place, top + jnp.log(total), stats)
        stacked = jnp.concatenate([keep(mask, values(cols)) for mask in masks], axis=0)
        out_ref[:, cols] = nn(jnp.concatenate(weights, axis=1), stacked).astype(BF16)
    stat_ref[...] = stats.T


def attend_backward(queries, keys, values, grads, bias_ref, stat_ref, turned_ref, dq_ref, out):
    masks = head_masks()
    for group in range(HEADS // PER):
        cols = slice(group * GROUP, (group + 1) * GROUP)
        turned_ref[cols, :] = keys(cols).T
        grad_scores, weights = [], []
        for place in range(PER):
            head = group * PER + place
            rows = slice(head * HEAD, (head + 1) * HEAD)
            scores = nt(keep(masks[place], keys(cols)), queries(cols)) + bias_ref[...]
            probs = jnp.exp(scores - stat_ref[head : head + 1, :])
            grad_weights = nt(keep(masks[place], values(cols)), grads(cols))
            inner = col_sum(probs * grad_weights)
            grad_score = (probs * (grad_weights - inner)).astype(BF16)
            dq_ref[rows, :] = nn(turned_ref[rows, :], grad_score)
            grad_scores.append(grad_score)
            weights.append(probs.astype(BF16))
        stacked = jnp.concatenate([keep(mask, queries(cols)) for mask in masks], axis=0)
        out(1, cols, nn(jnp.concatenate(grad_scores, axis=1), stacked).astype(BF16))
        stacked = jnp.concatenate([keep(mask, grads(cols)) for mask in masks], axis=0)
        out(2, cols, nn(jnp.concatenate(weights, axis=1), stacked).astype(BF16))


def gelu_parts(pre):
    square = pre * pre
    inner = jnp.tanh(GELU_A * pre * (1.0 + GELU_B * square))
    half = 0.5 * (1.0 + inner)
    slope = half + 0.5 * pre * (1.0 - inner * inner) * (GELU_A * (1.0 + 3.0 * GELU_B * square))
    return pre * half, slope


def feed_forward(after_ref, norm_gain, norm_shift, w_up, up_bias, w_down, down_bias, n2_ref, act_ref, slope_ref, part):
    after = after_ref[part, :]
    normed = (normalize(after)[0] * norm_gain[1:2] + norm_shift[1:2]).astype(BF16)
    n2_ref[part, :] = normed
    total = after + down_bias[...]
    for start in range(0, FF, D):
        cols = slice(start, start + D)
        activated, slope = gelu_parts(nn(normed, w_up[:, cols]) + up_bias[:, cols])
        activated = activated.astype(BF16)
        act_ref[part, cols] = activated
        slope_ref[part, cols] = slope.astype(BF16)
        total = total + nn(activated, w_down[cols, :])
    return total


def feed_backward(after_ref, grad, norm_gain, w_up, w_down, slope_ref, gb_ref, gp_ref, vec_ref, part):
    branch = grad.astype(BF16)
    gb_ref[part, :] = branch
    vec_ref[V_DOWNB : V_DOWNB + 1, :] += col_sum(branch.astype(F32))
    back = jnp.zeros((RC, D), F32)
    for index, start in enumerate(range(0, FF, D)):
        cols = slice(start, start + D)
        pre_grad = (nt(branch, w_down[cols, :]) * slope_ref[part, cols].astype(F32)).astype(BF16)
        gp_ref[part, cols] = pre_grad
        vec_ref[V_UPB + index : V_UPB + index + 1, :] += col_sum(pre_grad.astype(F32))
        back = back + nt(pre_grad, w_up[:, cols])
    xhat, scale = normalize(after_ref[part, :])
    vec_ref[V_GAIN2 : V_GAIN2 + 1, :] += col_sum(back * xhat)
    vec_ref[V_SHIFT2 : V_SHIFT2 + 1, :] += col_sum(back)
    return grad + norm_input_grad(back, norm_gain[1:2], xhat, scale)


def running_column(run_ref, row):
    line = run_ref[0, row : row + 1, :].astype(F32)
    return jnp.broadcast_to(line, (128, L)).T[:, :1]


def halting_share(current, run, halt_weight, halt_bias):
    logit = jnp.sum(current * halt_weight[...], axis=1, keepdims=True) + halt_bias[0]
    rate = jax.nn.sigmoid(logit)
    return run * rate, rate


def halting_backward(grad, change, current, share, rate, run, halt_weight, vec_ref):
    logit_grad = (
        run * jnp.sum(grad * change, axis=1, keepdims=True) * rate * (1.0 - rate)
    )
    vec_ref[V_HW : V_HW + 1, :] += col_sum(logit_grad * current)
    vec_ref[V_HB : V_HB + 1, :] += jnp.broadcast_to(col_sum(logit_grad), (1, D))
    return share * grad, (1.0 - share) * grad + logit_grad * halt_weight[...]


def write_rms(vec_ref, total_ref):
    lane = lax.broadcasted_iota(jnp.int32, (1, D), 1)
    vec_ref[V_RMS : V_RMS + 1, :] = jnp.where(lane == 0, total_ref[0], total_ref[1])


class Copies:
    def __init__(self, sems, pairs):
        self.made = {
            name: pltpu.make_async_copy(source, target, sems.at[index])
            for index, (name, source, target) in enumerate(pairs)
        }

    def start(self, *names):
        for name in names:
            self.made[name].start()

    def wait(self, *names):
        for name in names:
            self.made[name].wait()


def kernel_a(
    row,
    sec_ref, len_ref, hb_ref, run_ref, ng_ref, ns_ref, ub_ref, db_ref, hw_ref, cg_ref, cs_ref,
    x_hbm, wqkv_hbm, wout_hbm, wup_hbm, wdn_hbm, wcq_hbm,
    vec_ref, out_hbm, after_hbm, packed_hbm, att_hbm, stat_hbm, normed_hbm, n2_hbm, act_hbm, slope_hbm, change_hbm,
    x, wqkv, wout, wup, wdn, wcq, out, after, packed, att, stat, normed, n2, act, slope, change, bias, total, sems,
):
    encoding = sec_ref[0] == 0
    copies = Copies(
        sems,
        [
            ("x", x_hbm.at[0, row], x),
            ("wqkv", wqkv_hbm.at[0], wqkv),
            ("wout", wout_hbm.at[0], wout),
            ("wup", wup_hbm.at[0], wup),
            ("wdn", wdn_hbm.at[0], wdn),
            ("wcq", wcq_hbm, wcq),
            ("out", out, out_hbm),
            ("after", after, after_hbm),
            ("packed", packed, packed_hbm),
            ("att", att, att_hbm),
            ("stat", stat, stat_hbm),
            ("normed", normed, normed_hbm),
            ("n2", n2, n2_hbm),
            ("act", act, act_hbm),
            ("slope", slope, slope_hbm),
            ("change", change, change_hbm),
        ],
    )
    copies.start("x", "wqkv", "wout")

    @pl.when(encoding)
    def _():
        copies.start("wup", "wdn")

    @pl.when(jnp.logical_not(encoding))
    def _():
        copies.start("wcq")

    vec_ref[...] = jnp.zeros_like(vec_ref)
    side = sec_ref[0]
    write_bias(bias, len_ref, row, side, side, 1, jnp.logical_not(encoding))
    copies.wait("x", "wqkv")
    for part in row_chunks():
        current = x[part, :].astype(F32)
        value = (normalize(current)[0] * ng_ref[0:1] + ns_ref[0:1]).astype(BF16)
        normed[part, :] = value
        packed[part, 0:D] = (nn(value, wqkv[:, 0:D]).astype(BF16).astype(F32) * HEAD**-0.5).astype(BF16)
        packed[part, D : 2 * D] = nn(value, wqkv[:, D : 2 * D]).astype(BF16)
        packed[part, 2 * D :] = nn(value, wqkv[:, 2 * D :]).astype(BF16)
    copies.start("normed", "packed")
    attend_forward(
        lambda cols: packed[:, cols],
        lambda cols: packed[:, D + cols.start : D + cols.stop],
        lambda cols: packed[:, 2 * D + cols.start : 2 * D + cols.stop],
        bias, att, stat,
    )
    copies.start("att", "stat")
    copies.wait("wout")
    for part in row_chunks():
        after[part, :] = x[part, :].astype(F32) + nn(att[part, :], wout[...])
    copies.start("after")

    @pl.when(encoding)
    def _():
        copies.wait("wup", "wdn")
        runs = running_column(run_ref, row)
        total[0] = 0.0
        total[1] = 0.0
        for part in row_chunks():
            updated = feed_forward(after, ng_ref, ns_ref, wup, ub_ref, wdn, db_ref, n2, act, slope, part)
            current = x[part, :].astype(F32)
            share, _ = halting_share(current, runs[part], hw_ref, hb_ref)
            moved = updated - current
            change[part, :] = moved.astype(BF16)
            moved = share * moved
            result = current + moved
            out[part, :] = result.astype(BF16)
            total[0] += jnp.sum(result * result)
            total[1] += jnp.sum(moved * moved)
        copies.start("out", "n2", "act", "slope", "change")
        write_rms(vec_ref, total)
        copies.wait("n2", "act", "slope", "change")

    @pl.when(jnp.logical_not(encoding))
    def _():
        copies.wait("wcq")
        for part in row_chunks():
            value = (normalize(after[part, :])[0] * cg_ref[...] + cs_ref[...]).astype(BF16)
            change[part, :] = value
            out[part, :] = (nn(value, wcq[...]).astype(BF16).astype(F32) * HEAD**-0.5).astype(BF16)
        copies.start("out", "change")
        copies.wait("change")

    copies.wait("normed", "packed", "att", "stat", "after", "out")


def kernel_b(
    row,
    sec_ref, len_ref, hb_ref, run_ref, ng_ref, ns_ref, ub_ref, db_ref, hw_ref, cg_ref, cs_ref,
    x_hbm, cot_hbm, wup_hbm, wdn_hbm, wcq_hbm, wkv_hbm, wco_hbm, mem_hbm, cq_hbm, after_hbm,
    vec_ref, n2_hbm, act_hbm, gb_hbm, gp_hbm, att_hbm, gc_hbm, gq_hbm, gkv_hbm, back_hbm, result_hbm, ga_hbm, gx_hbm,
    x, cot, wup, wdn, wcq, wkv, wco, mem, cq, after, n2, act, gb, gp, att, gc, gq, gkv, back, result, gaf, gx,
    kv, slope, across, gatt, bias, stat, turned, dq, total, sems,
):
    vec_ref[...] = jnp.zeros_like(vec_ref)
    copies = Copies(
        sems,
        [
            ("x", x_hbm.at[0, row], x),
            ("cot", cot_hbm.at[0, row], cot),
            ("wup", wup_hbm.at[0], wup),
            ("wdn", wdn_hbm.at[0], wdn),
            ("wcq", wcq_hbm, wcq),
            ("wkv", wkv_hbm, wkv),
            ("wco", wco_hbm, wco),
            ("mem", mem_hbm, mem),
            ("cq", cq_hbm, cq),
            ("after", after_hbm, after),
            ("n2", n2, n2_hbm),
            ("act", act, act_hbm),
            ("gb", gb, gb_hbm),
            ("gp", gp, gp_hbm),
            ("att", att, att_hbm),
            ("gc", gc, gc_hbm),
            ("gq", gq, gq_hbm),
            ("gkv", gkv, gkv_hbm),
            ("back", back, back_hbm),
            ("result", result, result_hbm),
            ("ga", gaf, ga_hbm),
            ("gx", gx, gx_hbm),
        ],
    )

    @pl.when(sec_ref[0] == 1)
    def _():
        copies.start("mem", "wkv", "cq", "after", "wco", "wup", "wdn", "x", "cot", "wcq")
        write_bias(bias, len_ref, row, 1, 0, 1, None)
        copies.wait("mem", "wkv")
        for part in row_chunks():
            kv[part, 0:D] = nn(mem[part, :], wkv[:, 0:D]).astype(BF16)
            kv[part, D:] = nn(mem[part, :], wkv[:, D:]).astype(BF16)
        copies.wait("cq")
        attend_forward(
            lambda cols: cq[:, cols],
            lambda cols: kv[:, cols],
            lambda cols: kv[:, D + cols.start : D + cols.stop],
            bias, att, stat,
        )
        copies.start("att")
        copies.wait("after", "wco", "wup", "wdn", "x", "cot")
        runs = running_column(run_ref, row)
        total[0] = 0.0
        total[1] = 0.0
        for part in row_chunks():
            across[part, :] = after[part, :] + nn(att[part, :], wco[...])
            updated = feed_forward(across, ng_ref, ns_ref, wup, ub_ref, wdn, db_ref, n2, act, slope, part)
            current = x[part, :].astype(F32)
            run = runs[part]
            share, rate = halting_share(current, run, hw_ref, hb_ref)
            change = updated - current
            moved = share * change
            value = current + moved
            result[part, :] = value.astype(BF16)
            total[0] += jnp.sum(value * value)
            total[1] += jnp.sum(moved * moved)
            grad, own = halting_backward(
                cot[part, :].astype(F32), change, current, share, rate, run, hw_ref, vec_ref
            )
            gx[part, :] = own
            grad = feed_backward(across, grad, ng_ref, wup, wdn, slope, gb, gp, vec_ref, part)
            gaf[part, :] = grad
            branch = grad.astype(BF16)
            gc[part, :] = branch
            gatt[part, :] = nt(branch, wco[...]).astype(BF16)
        copies.start("n2", "act", "gb", "gp", "gc", "result", "gx")
        write_rms(vec_ref, total)
        write_bias(bias, len_ref, row, 0, 1, 1, None)

        def store(kind, cols, value):
            start = (kind - 1) * D
            gkv[:, start + cols.start : start + cols.stop] = value

        attend_backward(
            lambda cols: cq[:, cols],
            lambda cols: kv[:, cols],
            lambda cols: kv[:, D + cols.start : D + cols.stop],
            lambda cols: gatt[:, cols],
            bias, stat, turned, dq, store,
        )
        copies.start("gkv")
        for part in row_chunks():
            back[part, :] = (
                nt(gkv[part, 0:D], wkv[:, 0:D]) + nt(gkv[part, D:], wkv[:, D:])
            ).astype(BF16)
        copies.start("back")
        gq[...] = (dq[...] * HEAD**-0.5).astype(BF16).T
        copies.start("gq")
        copies.wait("wcq")
        for part in row_chunks():
            grad = nt(gq[part, :], wcq[...])
            xhat, scale = normalize(after[part, :])
            vec_ref[V_GAINC : V_GAINC + 1, :] += col_sum(grad * xhat)
            vec_ref[V_SHIFTC : V_SHIFTC + 1, :] += col_sum(grad)
            gaf[part, :] += norm_input_grad(grad, cg_ref[...], xhat, scale)
        copies.start("ga")
        copies.wait(
            "att", "n2", "act", "gb", "gp", "gc", "result", "gx", "gkv", "back", "gq", "ga"
        )


def kernel_c(
    row,
    sec_ref, hb_ref, run_ref, ng_ref, hw_ref,
    x_hbm, cot_hbm, wup_hbm, wdn_hbm, back_hbm, after_hbm, slope_hbm, change_hbm, n2e_hbm, acte_hbm,
    n2_hbm, act_hbm, gb_hbm, gp_hbm, *rest,
):
    prior_hbm, rest = (rest[0], rest[1:]) if row else (None, rest)
    vec_ref, ga_hbm, gx_hbm, grads_hbm = rest[:4]
    x, cot, wup, wdn, back, after, slope, change, n2, act, gaf, gx, gb, gp, grads, sems = rest[4:]
    encoding = sec_ref[0] == 0
    vec_ref[...] = jnp.zeros_like(vec_ref)
    copies = Copies(
        sems,
        [
            ("x", x_hbm.at[0, row], x),
            ("cot", cot_hbm.at[0, row], cot),
            ("wup", wup_hbm.at[0], wup),
            ("wdn", wdn_hbm.at[0], wdn),
            ("back", back_hbm, back),
            ("after", after_hbm, after),
            ("slope", slope_hbm, slope),
            ("change", change_hbm, change),
            ("n2e", n2e_hbm, n2),
            ("acte", acte_hbm, act),
            ("n2", n2_hbm, n2),
            ("act", act_hbm, act),
            ("gb", gb_hbm, gb),
            ("gp", gp_hbm, gp),
            ("ga", gaf, ga_hbm),
            ("gx", gx, gx_hbm),
            ("grads", grads, grads_hbm),
        ]
        + ([("prior", prior_hbm, grads)] if row else []),
    )
    if row:
        copies.start("prior")

    @pl.when(encoding)
    def _():
        copies.start("cot", "back", "change", "x", "wdn", "slope", "wup", "after", "n2e", "acte")
        copies.wait("cot", "back", "change", "x", "wdn", "slope", "wup", "after")
        runs = running_column(run_ref, row)
        for part in row_chunks():
            grad = cot[part, :].astype(F32) + back[part, :].astype(F32)
            current = x[part, :].astype(F32)
            run = runs[part]
            share, rate = halting_share(current, run, hw_ref, hb_ref)
            grad, own = halting_backward(
                grad, change[part, :].astype(F32), current, share, rate, run, hw_ref, vec_ref
            )
            gx[part, :] = own
            gaf[part, :] = feed_backward(after, grad, ng_ref, wup, wdn, slope, gb, gp, vec_ref, part)
        copies.start("ga", "gx")
        copies.wait("n2e", "acte")

    @pl.when(jnp.logical_not(encoding))
    def _():
        copies.start("n2", "gp", "act", "gb")
        copies.wait("n2", "gp", "act", "gb")

    if row:
        copies.wait("prior")
    turned = n2[...].T
    for start in range(0, FF, D):
        cols = slice(start, start + D)
        add_block(grads, cols, nn(turned, gp[:, cols]), row)
        add_block(grads, slice(FF + start, FF + start + D), tn(act[:, cols], gb[...]), row)
    copies.start("grads")

    @pl.when(encoding)
    def _():
        copies.wait("ga", "gx")

    copies.wait("grads")


def add_block(grads, rows, value, more):
    if more:
        value = value + grads[rows, :].astype(F32)
    grads[rows, :] = value.astype(BF16)


def kernel_s(
    row,
    sec_ref, len_ref, ng_ref,
    x_hbm, wqkv_hbm, wout_hbm, packed_hbm, stat_hbm, normed_hbm, att_hbm, gae_hbm, gxe_hbm, ga_hbm, gx_hbm, *rest,
):
    prior_hbm, rest = (rest[0], rest[1:]) if row else (None, rest)
    vec_ref, grad_hbm, grads_hbm = rest[:3]
    x, wqkv, wout, packed, stat, normed, att, gaf, gx, grad_out, grads, gs, gpack, gatt, bias, turned, dq, sems = rest[3:]
    encoding = sec_ref[0] == 0
    vec_ref[...] = jnp.zeros_like(vec_ref)
    copies = Copies(
        sems,
        [
            ("x", x_hbm.at[0, row], x),
            ("wqkv", wqkv_hbm.at[0], wqkv),
            ("wout", wout_hbm.at[0], wout),
            ("packed", packed_hbm, packed),
            ("stat", stat_hbm, stat),
            ("normed", normed_hbm, normed),
            ("att", att_hbm, att),
            ("gae", gae_hbm, gaf),
            ("gxe", gxe_hbm, gx),
            ("ga", ga_hbm, gaf),
            ("gx", gx_hbm, gx),
            ("grad", grad_out, grad_hbm),
            ("grads", grads, grads_hbm),
        ]
        + ([("prior", prior_hbm, grads)] if row else []),
    )

    @pl.when(encoding)
    def _():
        copies.start("gae", "gxe")

    @pl.when(jnp.logical_not(encoding))
    def _():
        copies.start("ga", "gx")

    copies.start("wout", "packed", "stat", "att", "wqkv", "x", "normed")
    if row:
        copies.start("prior")
    side = sec_ref[0]
    write_bias(bias, len_ref, row, side, side, -1, jnp.logical_not(encoding))

    @pl.when(encoding)
    def _():
        copies.wait("gae", "gxe")

    @pl.when(jnp.logical_not(encoding))
    def _():
        copies.wait("ga", "gx")

    copies.wait("wout")
    for part in row_chunks():
        branch = gaf[part, :].astype(BF16)
        gs[part, :] = branch
        gatt[part, :] = nt(branch, wout[...]).astype(BF16)
    copies.wait("packed", "stat")

    def store(kind, cols, value):
        gpack[:, kind * D + cols.start : kind * D + cols.stop] = value

    attend_backward(
        lambda cols: packed[:, cols],
        lambda cols: packed[:, D + cols.start : D + cols.stop],
        lambda cols: packed[:, 2 * D + cols.start : 2 * D + cols.stop],
        lambda cols: gatt[:, cols],
        bias, stat, turned, dq, store,
    )
    gpack[:, 0:D] = (dq[...] * HEAD**-0.5).astype(BF16).T
    if row:
        copies.wait("prior")
    copies.wait("att", "normed")
    add_block(grads, slice(3 * D, 4 * D), tn(att[...], gs[...]), row)
    flipped = normed[...].T
    for kind in range(3):
        cols = slice(kind * D, (kind + 1) * D)
        add_block(grads, cols, nn(flipped, gpack[:, cols]), row)
    copies.start("grads")
    copies.wait("wqkv", "x")
    for part in row_chunks():
        grad = nt(gpack[part, 0:D], wqkv[:, 0:D])
        grad += nt(gpack[part, D : 2 * D], wqkv[:, D : 2 * D])
        grad += nt(gpack[part, 2 * D :], wqkv[:, 2 * D :])
        xhat, scale = normalize(x[part, :].astype(F32))
        vec_ref[V_GAIN1 : V_GAIN1 + 1, :] += col_sum(grad * xhat)
        vec_ref[V_SHIFT1 : V_SHIFT1 + 1, :] += col_sum(grad)
        grad_out[part, :] = gaf[part, :] + gx[part, :] + norm_input_grad(grad, ng_ref[0:1], xhat, scale)
    copies.start("grad")
    copies.wait("grads", "grad")


def any_spec():
    return pl.BlockSpec(memory_space=pl.ANY)


def vmem_spec():
    return pl.BlockSpec(memory_space=pltpu.VMEM)


def smem_spec():
    return pl.BlockSpec(memory_space=pltpu.SMEM)


def shape(*dims, dtype=BF16):
    return jax.ShapeDtypeStruct(dims, dtype)


def scratch_of(shapes):
    return [pltpu.VMEM(item.shape, item.dtype) for item in shapes]


PARAMS = pltpu.CompilerParams(vmem_limit_bytes=60 * 1024 * 1024)


def call_a(row, scalars, vectors, arrays):
    x, wqkv, wout, wup, wdn, wcq = arrays
    outs = [
        shape(L, D), shape(L, D, dtype=F32), shape(L, 3 * D), shape(L, D), shape(128, L, dtype=F32), shape(L, D),
        shape(L, D), shape(L, FF), shape(L, FF), shape(L, D),
    ]
    return pl.pallas_call(
        functools.partial(kernel_a, row),
        out_shape=[shape(V_ROWS, D, dtype=F32)] + outs,
        in_specs=[smem_spec()] * 3 + [vmem_spec()] * len(vectors) + [any_spec()] * len(arrays),
        out_specs=[vmem_spec()] + [any_spec()] * len(outs),
        scratch_shapes=scratch_of(
            [shape(L, D), shape(D, 3 * D), shape(D, D), shape(D, FF), shape(FF, D), shape(D, D)]
            + outs
            + [shape(L, L, dtype=F32)]
        )
        + [pltpu.SMEM((2,), F32), pltpu.SemaphoreType.DMA((16,))],
        compiler_params=PARAMS,
        name="forward_a",
    )(*scalars, *vectors, *arrays)


def call_b(row, scalars, vectors, arrays):
    outs = [
        shape(L, D), shape(L, FF), shape(L, D), shape(L, FF), shape(L, D), shape(L, D), shape(L, D), shape(L, 2 * D),
        shape(L, D), shape(L, D), shape(L, D, dtype=F32), shape(L, D, dtype=F32),
    ]
    return pl.pallas_call(
        functools.partial(kernel_b, row),
        out_shape=[shape(V_ROWS, D, dtype=F32)] + outs,
        in_specs=[smem_spec()] * 3 + [vmem_spec()] * len(vectors) + [any_spec()] * len(arrays),
        out_specs=[vmem_spec()] + [any_spec()] * len(outs),
        scratch_shapes=scratch_of(
            [
                shape(L, D), shape(L, D), shape(D, FF), shape(FF, D), shape(D, D), shape(D, 2 * D), shape(D, D),
                shape(L, D), shape(L, D), shape(L, D, dtype=F32),
            ]
            + outs
            + [
                shape(L, 2 * D), shape(L, FF), shape(L, D, dtype=F32), shape(L, D), shape(L, L, dtype=F32),
                shape(128, L, dtype=F32), shape(D, L), shape(D, L, dtype=F32),
            ]
        )
        + [pltpu.SMEM((2,), F32), pltpu.SemaphoreType.DMA((22,))],
        compiler_params=PARAMS,
        name="decoder_b",
    )(*scalars, *vectors, *arrays)


def call_c(row, scalars, vectors, arrays):
    outs = [shape(L, D, dtype=F32), shape(L, D, dtype=F32), shape(2 * FF, D)]
    return pl.pallas_call(
        functools.partial(kernel_c, row),
        out_shape=[shape(V_ROWS, D, dtype=F32)] + outs,
        in_specs=[smem_spec()] * len(scalars) + [vmem_spec()] * len(vectors) + [any_spec()] * len(arrays),
        out_specs=[vmem_spec()] + [any_spec()] * len(outs),
        scratch_shapes=scratch_of(
            [
                shape(L, D), shape(L, D), shape(D, FF), shape(FF, D), shape(L, D), shape(L, D, dtype=F32), shape(L, FF),
                shape(L, D), shape(L, D), shape(L, FF), shape(L, D, dtype=F32), shape(L, D, dtype=F32),
                shape(L, D), shape(L, FF), shape(2 * FF, D),
            ]
        )
        + [pltpu.SemaphoreType.DMA((18,))],
        compiler_params=PARAMS,
        name="feed_backward",
    )(*scalars, *vectors, *arrays)


def call_s(row, scalars, vectors, arrays):
    outs = [shape(L, D, dtype=F32), shape(4 * D, D)]
    return pl.pallas_call(
        functools.partial(kernel_s, row),
        out_shape=[shape(V_ROWS, D, dtype=F32)] + outs,
        in_specs=[smem_spec()] * len(scalars) + [vmem_spec()] * len(vectors) + [any_spec()] * len(arrays),
        out_specs=[vmem_spec()] + [any_spec()] * len(outs),
        scratch_shapes=scratch_of(
            [
                shape(L, D), shape(D, 3 * D), shape(D, D), shape(L, 3 * D), shape(128, L, dtype=F32), shape(L, D),
                shape(L, D), shape(L, D, dtype=F32), shape(L, D, dtype=F32), shape(L, D, dtype=F32), shape(4 * D, D),
                shape(L, D), shape(L, 3 * D), shape(L, D), shape(L, L, dtype=F32), shape(D, L), shape(D, L, dtype=F32),
            ]
        )
        + [pltpu.SemaphoreType.DMA((14,))],
        compiler_params=PARAMS,
        name="self_backward",
    )(*scalars, *vectors, *arrays)


def kernel_w(sec_ref, *refs):
    count = (len(refs) - 3) // 2
    sources, out_hbm, held, outs, sems = refs[:count], refs[count], refs[count + 1 : -2], refs[-2], refs[-1]

    @pl.when(sec_ref[0] == 1)
    def _():
        copies = Copies(sems, [(i, sources[i], held[i]) for i in range(count)] + [("out", outs, out_hbm)])
        copies.start(*range(count))
        block = 0
        each = count // 3
        for pair in range(3):
            indices = range(pair * each, (pair + 1) * each)
            copies.wait(*indices)
            lefts, rights = [held[i] for i in indices[: each // 2]], [held[i] for i in indices[each // 2 :]]
            turned = [left[...].T for left in lefts]
            for start in range(0, rights[0].shape[1], D):
                cols = slice(start, start + D)
                value = nn(turned[0], rights[0][:, cols])
                for left, right in zip(turned[1:], rights[1:]):
                    value += nn(left, right[:, cols])
                outs[block * D : (block + 1) * D, :] = value.astype(BF16)
                block += 1
        copies.start("out")
        copies.wait("out")


def call_w(sec, pairs):
    flat = [item for lefts, rights in pairs for item in (*lefts, *rights)]
    return pl.pallas_call(
        kernel_w,
        out_shape=shape(4 * D, D),
        in_specs=[smem_spec()] + [any_spec()] * len(flat),
        out_specs=any_spec(),
        scratch_shapes=scratch_of(flat)
        + [pltpu.VMEM((4 * D, D), BF16), pltpu.SemaphoreType.DMA((len(flat) + 1,))],
        compiler_params=PARAMS,
        name="cross_weights",
    )(sec, *flat)


class Places:
    def __init__(self):
        self.count = lax.axis_size("dp")
        self.far = self.count // 4
        me = lax.axis_index("dp")
        self.core, self.near, self.rest = me % 2, (me // 2) % 2, me // 4

    def swap(self, value, bit, axis="dp", base=0):
        pairs = [(base + i, base + (i ^ bit)) for i in range(self.count)]
        return lax.ppermute(value, axis, pairs)

    def turn(self, value, steps, axis="dp", base=0):
        pairs = [(base + i, base + (i + 4 * steps) % self.count) for i in range(self.count)]
        return lax.ppermute(value, axis, pairs)


def halves(value, bit):
    half = value.shape[0] // 2
    mine = lax.dynamic_slice_in_dim(value, bit * half, half, 0)
    other = lax.dynamic_slice_in_dim(value, (1 - bit) * half, half, 0)
    return mine, other


def plus(left, right):
    return (left.astype(F32) + right.astype(F32)).astype(BF16)


def scatter_steps(places, value, axis="dp", base=0):
    mine, other = halves(value, places.core)
    value = plus(mine, (yield places.swap(other, 1, axis, base)))
    mine, other = halves(value, places.near)
    value = plus(mine, (yield places.swap(other, 2, axis, base)))
    parts = value.reshape(places.far, -1, D)
    total = lax.dynamic_index_in_dim(parts, places.rest, 0, keepdims=False).astype(F32)
    sent = []
    for step in range(1, places.far):
        part = lax.dynamic_index_in_dim(parts, (places.rest + step) % places.far, 0, keepdims=False)
        sent.append(places.turn(part, step, axis, base))
    for part in (yield sent):
        total = total + part.astype(F32)
    yield total.astype(BF16)


def gather_steps(places, share):
    parts = jnp.stack([share] + (yield [places.turn(share, step) for step in range(1, places.far)]))
    parts = jnp.stack([parts, (yield places.swap(parts, 2))])
    yield parts, (yield places.swap(parts, 1))


def vector_steps(places, value):
    bit = 1
    while bit < places.count:
        value = value + (yield places.swap(value, bit))
        bit *= 2
    cross = value[V_GAINC : V_SHIFTC + 1]
    yield value, cross + (yield lax.ppermute(cross, "section", [(0, 1), (1, 0)]))


def advance(steps, arrived):
    arrived = lax.optimization_barrier(arrived)
    return [step.send(item) for step, item in zip(steps, arrived)]


def place_kernel(far, groups, where_ref, *refs):
    outs = refs[2 * len(groups) :]
    core, near, rest = where_ref[0], where_ref[1], where_ref[2]
    for index, blocks in enumerate(groups):
        own_ref, other_ref = refs[2 * index : 2 * index + 2]
        rows = own_ref.shape[2]
        for share in range(4 * far):
            c, n, q = share // (2 * far), share // far % 2, share % far
            out, col = blocks[share * rows // D]
            start = share * rows % D
            step = lax.rem(rest - q + far, far)
            which = lax.rem(near + n, 2)
            target = (out, slice(start, start + rows), slice(col * D, (col + 1) * D))

            @pl.when(core == c)
            def _(target=target, source=own_ref):
                outs[target[0]][target[1], target[2]] = source[which, step].astype(F32)

            @pl.when(core != c)
            def _(target=target, source=other_ref):
                outs[target[0]][target[1], target[2]] = source[which, step].astype(F32)


def put_in_place(places, gathered, groups, widths):
    where = jnp.stack([places.core, places.near, places.rest]).astype(jnp.int32)
    flat = [item for pair in gathered for item in pair]
    return pl.pallas_call(
        functools.partial(place_kernel, places.far, groups),
        out_shape=[shape(D, width, dtype=F32) for width in widths],
        in_specs=[smem_spec()] + [vmem_spec()] * len(flat),
        out_specs=[vmem_spec()] * len(widths),
        compiler_params=PARAMS,
        name="place_sums",
    )(where, *flat)


def widen_kernel(up_in, down_in, up_out, down_out):
    up_out[...] = up_in[...].astype(F32)
    down_out[...] = down_in[...].astype(F32)


def widen(grads):
    count = FF // D
    return pl.pallas_call(
        widen_kernel,
        grid=(count,),
        out_shape=[shape(D, FF, dtype=F32), shape(FF, D, dtype=F32)],
        in_specs=[pl.BlockSpec((D, D), lambda i: (i, 0)), pl.BlockSpec((D, D), lambda i: (count + i, 0))],
        out_specs=[pl.BlockSpec((D, D), lambda i: (0, i)), pl.BlockSpec((D, D), lambda i: (i, 0))],
        compiler_params=PARAMS,
        name="widen",
    )(grads, grads)


def shards(
    inputs, cotangent, lengths, running, norm_gain, norm_shift, qkv_weight, out_weight, up_weight, up_bias,
    down_weight, down_bias, halt_weight, halt_bias, cross_gain, cross_shift, cross_query, cross_kv, cross_out,
):
    section = lax.axis_index("section").astype(jnp.int32)
    decoding = section == 1
    sec = section.reshape(1)
    places = Places()
    scalars = (sec, lengths, halt_bias)
    rows = range(inputs.shape[1])
    vectors = (running, norm_gain[0], norm_shift[0], up_bias, down_bias, halt_weight, cross_gain[None], cross_shift[None])
    firsts, received = [], []
    for row in rows:
        firsts.append(
            call_a(
                row, scalars, vectors,
                (inputs, qkv_weight, out_weight, up_weight, down_weight, cross_query),
            )
        )
        received.append(lax.ppermute(firsts[row][1], "section", [(0, 1)]))
    middles, returned = [], []
    for row in rows:
        _, out, after = firsts[row][:3]
        middles.append(
            call_b(
                row, scalars, vectors,
                (inputs, cotangent, up_weight, down_weight, cross_query, cross_kv, cross_out, received[row], out, after),
            )
        )
        returned.append(lax.ppermute(middles[row][9], "section", [(1, 0)]))

    def both(items, index):
        return [item[index] for item in items]

    feeds, selves = [], []
    for row in rows:
        _, _, after, packed, att, stat, normed, n2, act, slope, change = firsts[row]
        middle = middles[row]
        prior = lax.optimization_barrier((feeds[row - 1][3], selves[row - 1][0]))[:1] if row else ()
        feeds.append(
            call_c(
                row, (sec, halt_bias), (running, norm_gain[0], halt_weight),
                (
                    inputs, cotangent, up_weight, down_weight, returned[row], after, slope, change, n2, act,
                    middle[1], middle[2], middle[3], middle[4],
                )
                + tuple(prior),
            )
        )
        selves.append(
            call_s(
                row, (sec, lengths), (norm_gain[0],),
                (
                    inputs, qkv_weight, out_weight, packed, stat, normed, att, feeds[row][1], feeds[row][2],
                    middle[11], middle[12],
                )
                + ((selves[row - 1][2],) if row else ()),
            )
        )
    *arrived, _ = lax.optimization_barrier((*received, feeds[-1][0]))
    cross_grads = call_w(
        sec,
        [
            (both(firsts, 10), both(middles, 7)),
            (arrived, both(middles, 8)),
            (both(middles, 5), both(middles, 6)),
        ],
    )
    feed_sum = lax.psum(feeds[-1][3], "dp")
    vec = sum(both(middles, 0)) + sum(both(feeds, 0)) + sum(both(selves, 0))

    def sum_rest(operands):
        self_grads, cross_grads, vec = operands
        scatters = [
            scatter_steps(places, self_grads),
            scatter_steps(places, cross_grads, ("section", "dp"), places.count),
        ]
        small = vector_steps(places, vec)
        sent = [next(step) for step in (*scatters, small)]
        sent = advance((*scatters, small), sent)
        sent = advance((*scatters, small), sent)
        self_share, cross_share, vec_sent = advance((*scatters, small), sent)
        cross_share = jnp.where(decoding, cross_share, lax.ppermute(cross_share, "section", [(1, 0)]))
        gathers = [gather_steps(places, self_share), gather_steps(places, cross_share)]
        sent = [next(step) for step in gathers]
        for _ in range(2):
            arrived = lax.optimization_barrier((sent[0], vec_sent))
            sent = [gathers[0].send(arrived[0]), gathers[1].send(sent[1])]
            vec_sent = small.send(arrived[1])
        own = [gather.send(item) for gather, item in zip(gathers, sent)]
        while not isinstance(vec_sent, tuple):
            vec_sent = small.send(vec_sent)
        return *own, *vec_sent

    operands = (selves[-1][2], cross_grads, vec)
    *gathered, vec, cross_vec = lax.cond(
        lengths[0, 0, 0] > 0,
        sum_rest,
        lambda operands: jax.tree.map(
            lambda item: jnp.zeros(item.shape, item.dtype), jax.eval_shape(sum_rest, operands)
        ),
        operands,
    )
    groups = [[(0, 0), (0, 1), (0, 2), (1, 0)], [(2, 0), (3, 0), (3, 1), (4, 0)]]
    qkv_sum, out_sum, query_sum, kv_sum, cross_out_sum = put_in_place(
        places, gathered, groups, [3 * D, D, D, 2 * D, D]
    )
    up_sum, down_sum = widen(feed_sum)
    stats = jnp.stack(
        [jnp.where(decoding, middles[row][0], firsts[row][0])[V_RMS, :2] for row in rows]
    )
    row_rms = jnp.sqrt(stats / (L * D) + 1e-06)
    final = jnp.stack([jnp.where(decoding, middles[row][10], firsts[row][1]) for row in rows])
    input_grad = jnp.stack(both(selves, 1))
    return (
        final[None],
        input_grad[None],
        row_rms[None],
        jnp.stack([vec[V_GAIN1], vec[V_GAIN2]])[None],
        jnp.stack([vec[V_SHIFT1], vec[V_SHIFT2]])[None],
        qkv_sum[None],
        out_sum[None],
        up_sum[None],
        vec[V_UPB : V_UPB + 4].reshape(1, FF),
        down_sum[None],
        vec[V_DOWNB][None],
        vec[V_HW][None],
        vec[V_HB, :1],
        cross_vec[0],
        cross_vec[1],
        query_sum,
        kv_sum,
        cross_out_sum,
    )


def solution(mesh):
    in_specs = (
        P("section", "dp", None, None),
        P("section", "dp", None, None),
        P(None, "dp", None),
        P("section", "dp", None),
        P("section", None, None),
        P("section", None, None),
        P("section", None, None),
        P("section", None, None),
        P("section", None, None),
        P("section", None),
        P("section", None, None),
        P("section", None),
        P("section", None),
        P("section"),
        P(),
        P(),
        P(),
        P(),
        P(),
    )
    out_specs = (
        P("section", "dp", None, None),
        P("section", "dp", None, None),
        P("section", "dp", None),
        P("section", None, None),
        P("section", None, None),
        P("section", None, None),
        P("section", None, None),
        P("section", None, None),
        P("section", None),
        P("section", None, None),
        P("section", None),
        P("section", None),
        P("section"),
        P(),
        P(),
        P(),
        P(),
        P(),
    )
    return jax.shard_map(shards, mesh=mesh, in_specs=in_specs, out_specs=out_specs, check_vma=False)
```

```python
import functools

import jax
import jax.numpy as jnp
from jax import lax
from jax.experimental import pallas as pl
from jax.experimental.pallas import tpu as pltpu
from jax.sharding import PartitionSpec as P

L = 512
D = 512
FF = 2048
HEADS = 8
SECTION, DP = "section", "dp"
HEAD = D // HEADS
GROUP = 256
PER = GROUP // HEAD
RC = 512
EPS = 1e-05
MASKED = -1000000000.0
GELU_A = 0.7978845608028654
GELU_B = 0.044715
F32 = jnp.float32
BF16 = jnp.bfloat16

V_GAIN2, V_SHIFT2, V_UPB, V_DOWNB, V_HW, V_HB = 0, 1, 2, 6, 7, 8
V_GAINC, V_SHIFTC, V_GAIN1, V_SHIFT1, V_RMS = 9, 10, 11, 12, 13
V_ROWS = 16


def nn(left, right):
    return lax.dot_general(left, right, (((1,), (0,)), ((), ())), preferred_element_type=F32)


def nt(left, right):
    return lax.dot_general(left, right, (((1,), (1,)), ((), ())), preferred_element_type=F32)


def tn(left, right):
    return lax.dot_general(left, right, (((0,), (0,)), ((), ())), preferred_element_type=F32)


def col_sum(value):
    return jnp.sum(value, axis=0, keepdims=True)


def row_mean(value):
    return jnp.mean(value, axis=1, keepdims=True)


def normalize(value):
    centered = value - row_mean(value)
    scale = lax.rsqrt(row_mean(centered * centered) + EPS)
    return centered * scale, scale


def norm_input_grad(grad, gain, xhat, scale):
    scaled = grad * gain
    return scale * (scaled - row_mean(scaled) - xhat * row_mean(scaled * xhat))


def each(count, size, body):
    def step(index, carry):
        body(index, pl.ds(pl.multiple_of(index * size, size), size))
        return carry

    lax.fori_loop(0, count, step, 0)


def for_rows(body):
    for first in range(0, L, RC):
        body(slice(first, first + RC))


def head_masks():
    lane = lax.broadcasted_iota(jnp.int32, (1, GROUP), 1)
    return [(lane // HEAD) == place for place in range(PER)]


def keep(mask, value):
    return jnp.where(mask, value, jnp.zeros_like(value))


def segments(len_ref, side, row, shape, dim, first):
    place = lax.broadcasted_iota(jnp.int32, shape, dim) + first
    total = jnp.int32(0)
    found = jnp.zeros(shape, jnp.int32)
    for index in range(len_ref.shape[2]):
        total = total + len_ref[side, row, index]
        found = found + (place >= total).astype(jnp.int32)
    return found


def write_bias(bias_ref, len_ref, row, row_side, col_side, causal_sign, causal):
    across = segments(len_ref, col_side, row, (1, L), 1, 0)

    def some(part):
        allowed = segments(len_ref, row_side, row, (RC, 1), 0, part.start) == across
        if causal is not None:
            row_place = lax.broadcasted_iota(jnp.int32, (RC, L), 0) + part.start
            col_place = lax.broadcasted_iota(jnp.int32, (RC, L), 1)
            ordered = (row_place - col_place) * causal_sign >= 0
            allowed = allowed & (ordered | jnp.logical_not(causal))
        bias_ref[part, :] = jnp.where(allowed, 0.0, MASKED)

    for_rows(some)


def attend_forward(queries, q0, keys, k0, values, v0, bias_ref, out_ref, stat_ref, column_ref):
    masks = head_masks()
    lane = lax.broadcasted_iota(jnp.int32, (1, 128), 1)
    column_ref[...] = jnp.zeros_like(column_ref)

    def of_group(index, cols):
        own_q, own_k, own_v = (ref[:, moved(cols, first)] for ref, first in ((queries, q0), (keys, k0), (values, v0)))
        stats = column_ref[...]
        weights = []
        for place in range(PER):
            scores = nt(keep(masks[place], own_q), own_k) + bias_ref[...]
            top = jnp.max(scores, axis=1, keepdims=True)
            expanded = jnp.exp(scores - top)
            total = jnp.sum(expanded, axis=1, keepdims=True)
            weights.append((expanded * (1.0 / total)).astype(BF16))
            stats = jnp.where(lane == index * PER + place, top + jnp.log(total), stats)
        column_ref[...] = stats
        stacked = jnp.concatenate([keep(mask, own_v) for mask in masks], axis=0)
        out_ref[:, cols] = nn(jnp.concatenate(weights, axis=1), stacked).astype(BF16)

    for index in range(D // GROUP):
        of_group(index, pl.ds(index * GROUP, GROUP))
    turned = column_ref[...].T
    for head in range(HEADS):
        stat_ref[head] = turned[head : head + 1, :]


def moved(cols, first):
    place = cols.start + first
    return pl.ds(place if isinstance(place, int) else pl.multiple_of(place, GROUP), cols.size)


def write_inner(inner_ref, grads, out_ref):
    product = grads[...].astype(F32) * out_ref[...].astype(F32)
    high = product.astype(BF16)
    low = (product - high.astype(F32)).astype(BF16)
    head = lax.broadcasted_iota(jnp.int32, (128, D), 0)
    feature = lax.broadcasted_iota(jnp.int32, (128, D), 1)
    members = jnp.where(feature // HEAD == head, 1.0, 0.0).astype(BF16)
    inner = nt(members, high) + nt(members, low)
    for index in range(HEADS):
        inner_ref[index] = inner[index : index + 1, :]


def attend_backward(
    queries, q0, keys, k0, values, v0, grads, out_ref, bias_ref, stat_ref,
    turned_ref, dq_ref, inner_ref, scores_ref, drops_ref, probs_ref, slants_ref, target, t0,
):
    masks = head_masks()
    write_inner(inner_ref, grads, out_ref)

    def of_group(index, cols):
        own_q, own_k, own_v = (ref[:, moved(cols, first)] for ref, first in ((queries, q0), (keys, k0), (values, v0)))
        own_g = grads[:, cols]
        turned_ref[cols, :] = own_k.T
        for place in range(PER):
            head, slot = index * PER + place, place % 2
            rows, across = pl.ds(pl.multiple_of(head * HEAD, HEAD), HEAD), slice(place * L, (place + 1) * L)
            scores_ref[slot] = nt(keep(masks[place], own_k), own_q)
            drops_ref[slot] = nt(keep(masks[place], own_v), own_g)
            log_total, inner = stat_ref[head], inner_ref[head]
            for part in range(0, L, 64):
                lines = slice(part, part + 64)
                probs = jnp.exp(scores_ref[slot, lines, :] + bias_ref[lines, :] - log_total)
                probs_ref[lines, across] = probs.astype(BF16)
                slants_ref[lines, across] = (probs * (drops_ref[slot, lines, :] - inner)).astype(BF16)
            dq_ref[rows, :] = nn(turned_ref[rows, :], slants_ref[:, across])
        stacked = jnp.concatenate([keep(mask, own_q) for mask in masks], axis=0)
        target[:, moved(cols, t0)] = nn(slants_ref[...], stacked).astype(BF16)
        stacked = jnp.concatenate([keep(mask, own_g) for mask in masks], axis=0)
        target[:, moved(cols, t0 + D)] = nn(probs_ref[...], stacked).astype(BF16)

    each(D // GROUP, GROUP, of_group)


def gelu_parts(pre):
    square = pre * pre
    half = 0.5 + 0.5 * jnp.tanh(pre * (GELU_A + GELU_A * GELU_B * square))
    slope = half + half * (1.0 - half) * pre * (2.0 * GELU_A + 6.0 * GELU_A * GELU_B * square)
    return pre * half, slope


def feed_forward(after_ref, norm_gain, norm_shift, w_up, up_bias, w_down, down_bias, n2_ref, act_ref, slope_ref, part):
    after = after_ref[part, :]
    normed = (normalize(after)[0] * norm_gain[1:2] + norm_shift[1:2]).astype(BF16)
    n2_ref[part, :] = normed
    total = after + down_bias[...]
    for cols in blocks_of(FF):
        activated, slope = gelu_parts(nn(normed, w_up[:, cols]) + up_bias[:, cols])
        activated = activated.astype(BF16)
        act_ref[part, cols] = activated
        slope_ref[part, cols] = slope.astype(BF16)
        total = total + nn(activated, w_down[cols, :])
    return total


def feed_slope(gb_ref, w_down, slope_ref, gp_ref, vec, part, index, cols):
    value = (nt(gb_ref[part, :], w_down[cols, :]) * slope_ref[part, cols].astype(F32)).astype(BF16)
    gp_ref[part, cols] = value
    add_row(vec, V_UPB + index, col_sum(value.astype(F32)))
    return value


def feed_input_grad(after_ref, back, grad_ref, gb_ref, norm_gain, vec, part):
    add_row(vec, V_DOWNB, col_sum(gb_ref[part, :].astype(F32)))
    xhat, scale = normalize(after_ref[part, :])
    add_row(vec, V_GAIN2, col_sum(back * xhat))
    add_row(vec, V_SHIFT2, col_sum(back))
    return grad_ref[part, :] + norm_input_grad(back, norm_gain[1:2], xhat, scale)


def write_running(column_ref, run_ref, row):
    line = run_ref[0, row : row + 1, :].astype(F32)
    column_ref[...] = jnp.broadcast_to(line, (128, L)).T


def halting_share(current, run, halt_weight, halt_bias):
    logit = jnp.sum(current * halt_weight[...], axis=1, keepdims=True) + halt_bias[0]
    rate = jax.nn.sigmoid(logit)
    return run * rate, rate


def halting_backward(grad, change, current, share, rate, run, halt_weight, vec_ref):
    logit_grad = (
        run * jnp.sum(grad * change, axis=1, keepdims=True) * rate * (1.0 - rate)
    )
    vec_ref[V_HW : V_HW + 1, :] += col_sum(logit_grad * current)
    vec_ref[V_HB : V_HB + 1, :] += jnp.broadcast_to(col_sum(logit_grad), (1, D))
    return share * grad, (1.0 - share) * grad + logit_grad * halt_weight[...]


def write_rms(vec_ref, total_ref):
    lane = lax.broadcasted_iota(jnp.int32, (1, D), 1)
    vec_ref[V_RMS : V_RMS + 1, :] = jnp.where(lane == 0, total_ref[0], total_ref[1])


class Copies:
    def __init__(self, sems, **pairs):
        for index, (name, (source, target)) in enumerate(pairs.items()):
            setattr(self, name, pltpu.make_async_copy(source, target, sems.at[index]))


def start(*copies):
    for copy in copies:
        copy.start()


def wait(*copies):
    for copy in copies:
        copy.wait()


def blocks_of(width):
    return [slice(place, place + D) for place in range(0, width, D)]


def on_decoder():
    return lax.axis_index(SECTION) == 1


def add_row(vec, row, value):
    vec[row : row + 1, :] += value


def kernel_a(
    row,
    x_hbm, ng_hbm, ns_hbm, len_hbm, run_hbm, ub_hbm, db_hbm, hw_hbm, hb_hbm, cg_hbm, cs_hbm,
    wqkv_hbm, wout_hbm, wup_hbm, wdn_hbm, wcq_hbm,
    *rest,
):
    (
        vec_hbm, out_hbm, after_hbm, packed_hbm, att_hbm, stat_hbm, normed_hbm, n2_hbm, act_hbm, slope_hbm, change_hbm,
        result_hbm, x, ng, ns, lens, run, ub, db, hw, hb, cg, cs, wqkv, wout, wup, wdn, wcq,
        vec, out, after, packed, att, stat, normed, n2, act, slope, change, bias, column, total, sems,
    ) = rest[row > 0 :]
    decoding = on_decoder()
    encoding = jnp.logical_not(decoding)
    first, second = slice(0, L // 2), slice(L // 2, L)
    c = Copies(
        sems,
        x=(x_hbm.at[0, row], x), ng=(ng_hbm.at[0], ng), ns=(ns_hbm.at[0], ns), lens=(len_hbm, lens), run=(run_hbm, run),
        ub=(ub_hbm, ub), db=(db_hbm, db), hw=(hw_hbm, hw), hb=(hb_hbm, hb), cg=(cg_hbm, cg), cs=(cs_hbm, cs),
        wqkv=(wqkv_hbm.at[0], wqkv), wout=(wout_hbm.at[0], wout), wup=(wup_hbm.at[0], wup), wdn=(wdn_hbm.at[0], wdn),
        wcq=(wcq_hbm, wcq),
        vec=(vec, vec_hbm), out=(out, out_hbm), after=(after, after_hbm), packed=(packed, packed_hbm),
        att=(att, att_hbm), stat=(stat, stat_hbm), normed=(normed, normed_hbm), change=(change, change_hbm),
        n20=(n2.at[first], n2_hbm.at[first]), act0=(act.at[first], act_hbm.at[first]),
        slope0=(slope.at[first], slope_hbm.at[first]), change0=(change.at[first], change_hbm.at[first]),
        n21=(n2.at[second], n2_hbm.at[second]), act1=(act.at[second], act_hbm.at[second]),
        slope1=(slope.at[second], slope_hbm.at[second]), change1=(change.at[second], change_hbm.at[second]),
        result=(out, result_hbm.at[0, row]),
    )
    firsts, seconds = (c.n20, c.act0, c.slope0, c.change0), (c.n21, c.act1, c.slope1, c.change1)
    start(c.x, c.ng, c.ns, c.lens, c.wqkv, c.wout)

    @pl.when(encoding)
    def _():
        start(c.run, c.ub, c.db, c.hw, c.hb, c.wup, c.wdn)

    @pl.when(decoding)
    def _():
        start(c.cg, c.cs, c.wcq)

    wait(c.lens)
    side = decoding.astype(jnp.int32)
    write_bias(bias, lens, row, side, side, 1, decoding)
    wait(c.x, c.ng, c.ns)

    @for_rows
    def _(part):
        normed[part, :] = (normalize(x[part, :].astype(F32))[0] * ng[0:1] + ns[0:1]).astype(BF16)

    start(c.normed)
    wait(c.wqkv)
    for index, cols in enumerate(blocks_of(3 * D)):
        value = nn(normed[...], wqkv[:, cols]).astype(BF16)
        if index == 0:
            value = (value.astype(F32) * HEAD**-0.5).astype(BF16)
        packed[:, cols] = value
    start(c.packed)
    attend_forward(packed, 0, packed, D, packed, 2 * D, bias, att, stat, column)
    start(c.att, c.stat)
    wait(c.wout)
    after[...] = x[...].astype(F32) + nn(att[...], wout[...])
    start(c.after)

    @pl.when(encoding)
    def _():
        wait(c.run, c.ub, c.db, c.hw, c.hb, c.wup, c.wdn)
        write_running(column, run, row)
        total[0] = 0.0
        total[1] = 0.0

        @for_rows
        def _(part):
            updated = feed_forward(after, ng, ns, wup, ub, wdn, db, n2, act, slope, part)
            current = x[part, :].astype(F32)
            share, _ = halting_share(current, column[part, :1], hw, hb)
            moved = updated - current
            change[part, :] = moved.astype(BF16)
            moved = share * moved
            result = current + moved
            out[part, :] = result.astype(BF16)
            total[0] += jnp.sum(result * result)
            total[1] += jnp.sum(moved * moved)
            if part.start == 0:
                start(*firsts)

        start(c.out, *seconds, c.result)
        vec[...] = jnp.zeros_like(vec)
        write_rms(vec, total)
        start(c.vec)
        wait(*firsts, *seconds, c.vec, c.result)

    @pl.when(decoding)
    def _():
        wait(c.cg, c.cs, c.wcq)

        @for_rows
        def _(part):
            change[part, :] = (normalize(after[part, :])[0] * cg[...] + cs[...]).astype(BF16)

        value = nn(change[...], wcq[...]).astype(BF16)
        out[...] = (value.astype(F32) * HEAD**-0.5).astype(BF16)
        start(c.out, c.change)
        vec[...] = jnp.zeros_like(vec)
        start(c.vec)
        wait(c.change, c.vec)

    wait(c.normed, c.packed, c.att, c.stat, c.after, c.out)


def kernel_b(
    row,
    x_hbm, cot_hbm, ng_hbm, ns_hbm, len_hbm, run_hbm, ub_hbm, db_hbm, hw_hbm, hb_hbm,
    wup_hbm, wdn_hbm, wkv_hbm, wco_hbm, mem_hbm, cq_hbm, after_hbm, _,
    vec_hbm, n2_hbm, act_hbm, gb_hbm, gp_hbm, att_hbm, gc_hbm, dq_hbm, gkv_hbm, back_hbm, ga_hbm, gx_hbm, result_hbm,
    x, cot, ng, ns, lens, run, ub, db, hw, hb, wup, wdn, wkv, wco, mem, cq, after,
    vec, n2, act, gb, gp, att, gc, dqb, gkv, back, gaf, gx,
    result, kv, slope, across, gatt, bias, stat, column, turned, dq, inner, scores, drops, probs, slants, total, sems,
):
    c = Copies(
        sems,
        x=(x_hbm.at[0, row], x), cot=(cot_hbm.at[0, row], cot), ng=(ng_hbm.at[0], ng), ns=(ns_hbm.at[0], ns),
        lens=(len_hbm, lens), run=(run_hbm, run), ub=(ub_hbm, ub), db=(db_hbm, db), hw=(hw_hbm, hw), hb=(hb_hbm, hb),
        wup=(wup_hbm.at[0], wup), wdn=(wdn_hbm.at[0], wdn), wkv=(wkv_hbm, wkv),
        wco=(wco_hbm, wco), mem=(mem_hbm, mem), cq=(cq_hbm, cq), after=(after_hbm, after),
        vec=(vec, vec_hbm), n2=(n2, n2_hbm), act=(act, act_hbm), gb=(gb, gb_hbm), gp=(gp, gp_hbm), att=(att, att_hbm),
        gc=(gc, gc_hbm), dq=(dqb, dq_hbm), gkv=(gkv, gkv_hbm), back=(back, back_hbm), result=(result, result_hbm.at[0, row]),
        ga=(gaf, ga_hbm), gx=(gx, gx_hbm),
    )
    decoding = on_decoder()

    @pl.when(jnp.logical_not(decoding))
    def _():
        vec[...] = jnp.zeros_like(vec)
        start(c.vec)

    @pl.when(decoding)
    def _():
        start(c.mem, c.wkv, c.lens, c.cq, c.wco, c.after, c.ng, c.ns, c.ub, c.db, c.wup, c.wdn)
        start(c.x, c.cot, c.run, c.hw, c.hb)
        vec[...] = jnp.zeros_like(vec)
        wait(c.lens)
        write_bias(bias, lens, row, 1, 0, 1, None)
        wait(c.mem, c.wkv)
        for cols in blocks_of(2 * D):
            kv[:, cols] = nn(mem[...], wkv[:, cols]).astype(BF16)
        wait(c.cq)
        attend_forward(cq, 0, kv, 0, kv, D, bias, att, stat, column)
        start(c.att)
        wait(c.after, c.wco)
        across[...] = after[...] + nn(att[...], wco[...])
        wait(c.ng, c.ns, c.ub, c.db, c.wup, c.wdn, c.x, c.cot, c.run, c.hw, c.hb)
        write_running(column, run, row)
        total[0] = 0.0
        total[1] = 0.0

        @for_rows
        def _(part):
            updated = feed_forward(across, ng, ns, wup, ub, wdn, db, n2, act, slope, part)
            current = x[part, :].astype(F32)
            share, rate = halting_share(current, column[part, :1], hw, hb)
            moved = updated - current
            grad, own = halting_backward(
                cot[part, :].astype(F32), moved, current, share, rate, column[part, :1], hw, vec
            )
            gx[part, :] = own
            moved = share * moved
            value = current + moved
            result[part, :] = value.astype(BF16)
            total[0] += jnp.sum(value * value)
            total[1] += jnp.sum(moved * moved)
            gaf[part, :] = grad
            gb[part, :] = grad.astype(BF16)

        start(c.n2, c.act, c.gb, c.result, c.gx)
        write_bias(bias, lens, row, 0, 1, 1, None)

        @for_rows
        def _(part):
            for index, cols in enumerate(blocks_of(FF)):
                value = feed_slope(gb, wdn, slope, gp, vec, part, index, cols)
                total_back = nt(value, wup[:, cols]) if index == 0 else total_back + nt(value, wup[:, cols])
            grad = feed_input_grad(across, total_back, gaf, gb, ng, vec, part)
            gaf[part, :] = grad
            gc[part, :] = grad.astype(BF16)

        gatt[...] = nt(gc[...], wco[...]).astype(BF16)
        start(c.gp, c.gc, c.ga)
        write_rms(vec, total)
        start(c.vec)
        attend_backward(
            cq, 0, kv, 0, kv, D, gatt, att, bias, stat, turned, dq, inner, scores, drops, probs, slants, gkv, 0
        )
        start(c.gkv)
        dqb[...] = (dq[...] * HEAD**-0.5).astype(BF16)
        start(c.dq)
        back[...] = (nt(gkv[:, 0:D], wkv[:, 0:D]) + nt(gkv[:, D:], wkv[:, D:])).astype(BF16)
        start(c.back)
        wait(c.att, c.n2, c.act, c.gb, c.gp, c.gc, c.result, c.gx, c.gkv, c.dq, c.back, c.ga)

    wait(c.vec)


def kernel_c(
    row,
    x_hbm, cot_hbm, ng_hbm, run_hbm, hw_hbm, hb_hbm, wup_hbm, wdn_hbm, back_hbm, after_hbm, slope_hbm, change_hbm,
    n2e_hbm, acte_hbm, n2_hbm, act_hbm, gb_hbm, gp_hbm, cg_hbm, wcq_hbm, dq_hbm, gad_hbm, *rest,
):
    prior_hbm, rest = (rest[0], rest[1:]) if row else (None, rest)
    vec_hbm, ga_hbm, gx_hbm, grads_hbm, gq_hbm = rest[:5]
    (
        x, cot, ng, run, hw, hb, wup, wdn, back, after, slope, change, n2, act, cg, wcq, dq, vec, gaf, gx, gb, gp, grads, gq,
        column, sems,
    ) = rest[5:]
    decoding = on_decoder()
    encoding = jnp.logical_not(decoding)
    ups, downs = blocks_of(FF), [slice(FF + cols.start, FF + cols.stop) for cols in blocks_of(FF)]
    c = Copies(
        sems,
        x=(x_hbm.at[0, row], x), cot=(cot_hbm.at[0, row], cot), ng=(ng_hbm.at[0], ng), run=(run_hbm, run),
        hw=(hw_hbm, hw), hb=(hb_hbm, hb), wup=(wup_hbm.at[0], wup), wdn=(wdn_hbm.at[0], wdn), back=(back_hbm, back),
        after=(after_hbm, after), slope=(slope_hbm, slope), change=(change_hbm, change), n2e=(n2e_hbm, n2),
        acte=(acte_hbm, act), n2=(n2_hbm, n2), act=(act_hbm, act), gb=(gb_hbm, gb), gp=(gp_hbm, gp),
        vec=(vec, vec_hbm), ga=(gaf, ga_hbm), gx=(gx, gx_hbm), grads=(grads, grads_hbm), cg=(cg_hbm, cg),
        wcq=(wcq_hbm, wcq), dq=(dq_hbm, dq), gad=(gad_hbm, gaf), gq=(gq, gq_hbm),
        **({"prior": (prior_hbm, grads)} if row else {}),
    )
    vec[...] = jnp.zeros_like(vec)

    @pl.when(encoding)
    def _():
        start(c.back, c.cot, c.x, c.change, c.run, c.hw, c.hb, c.wdn, c.slope, c.n2e, c.acte, c.wup, c.after, c.ng)
        if row:
            start(c.prior)
        wait(c.back, c.cot, c.x, c.change, c.run, c.hw, c.hb)
        write_running(column, run, row)

        @for_rows
        def _(part):
            grad = cot[part, :].astype(F32) + back[part, :].astype(F32)
            current = x[part, :].astype(F32)
            share, rate = halting_share(current, column[part, :1], hw, hb)
            grad, own = halting_backward(
                grad, change[part, :].astype(F32), current, share, rate, column[part, :1], hw, vec
            )
            gx[part, :] = own
            gaf[part, :] = grad
            gb[part, :] = grad.astype(BF16)

        start(c.gx)
        wait(c.wdn, c.slope)
        for index, cols in enumerate(ups):
            feed_slope(gb, wdn, slope, gp, vec, slice(0, L), index, cols)
        wait(c.n2e, c.acte)

    @pl.when(decoding)
    def _():
        start(c.n2, c.gp, c.act, c.gb)
        if row:
            start(c.prior)
        start(c.dq, c.wcq, c.after, c.gad, c.cg)
        wait(c.n2, c.gp, c.act, c.gb)

    if row:
        wait(c.prior)
    turned = n2[...].T
    for up, down in zip(ups, downs):
        add_block(grads, up, nn(turned, gp[:, up]), row)
        add_block(grads, down, tn(act[:, up], gb[...]), row)
    start(c.grads)

    @pl.when(encoding)
    def _():
        wait(c.wup, c.after, c.ng)

        @for_rows
        def _(part):
            for index, cols in enumerate(ups):
                value = nt(gp[part, cols], wup[:, cols])
                total_back = value if index == 0 else total_back + value
            gaf[part, :] = feed_input_grad(after, total_back, gaf, gb, ng, vec, part)

        start(c.ga)
        wait(c.ga, c.gx)

    @pl.when(decoding)
    def _():
        wait(c.dq, c.wcq, c.after, c.gad, c.cg)
        gq[...] = dq[...].T
        start(c.gq)

        @for_rows
        def _(part):
            grad = nt(gq[part, :], wcq[...])
            xhat, scale = normalize(after[part, :])
            add_row(vec, V_GAINC, col_sum(grad * xhat))
            add_row(vec, V_SHIFTC, col_sum(grad))
            gaf[part, :] += norm_input_grad(grad, cg[...], xhat, scale)

        start(c.ga)
        wait(c.gq, c.ga)

    start(c.vec)
    wait(c.grads, c.vec)


def add_block(grads, rows, value, more):
    if more:
        value = value + grads[rows, :].astype(F32)
    grads[rows, :] = value.astype(BF16)


def kernel_s(
    row,
    x_hbm, ng_hbm, len_hbm, wqkv_hbm, wout_hbm, packed_hbm, stat_hbm, normed_hbm, att_hbm,
    ga_hbm, gxe_hbm, gx_hbm, *rest,
):
    prior_hbm, rest = (rest[0], rest[2:]) if row else (None, rest)
    vec_hbm, grads_hbm, grad_hbm = rest[:3]
    (
        x, ng, lens, wqkv, wout, packed, stat, normed, att, gaf, gx, vec, grads, grad_out, gs, gpack, gatt, bias,
        turned, dq, inner, scores, drops, probs, slants, sems,
    ) = rest[3:]
    decoding = on_decoder()
    encoding = jnp.logical_not(decoding)
    c = Copies(
        sems,
        x=(x_hbm.at[0, row], x), ng=(ng_hbm.at[0], ng), lens=(len_hbm, lens), wqkv=(wqkv_hbm.at[0], wqkv),
        wout=(wout_hbm.at[0], wout), packed=(packed_hbm, packed), stat=(stat_hbm, stat), normed=(normed_hbm, normed),
        att=(att_hbm, att), gxe=(gxe_hbm, gx), ga=(ga_hbm, gaf), gx=(gx_hbm, gx),
        vec=(vec, vec_hbm), grad=(grad_out, grad_hbm.at[0, row]), grads=(grads, grads_hbm),
        **({"prior": (prior_hbm, grads)} if row else {}),
    )

    start(c.ga, c.lens, c.wout, c.att, c.packed, c.stat, c.normed, c.wqkv, c.x, c.ng)
    if row:
        start(c.prior)

    @pl.when(encoding)
    def _():
        start(c.gxe)

    @pl.when(decoding)
    def _():
        start(c.gx)

    vec[...] = jnp.zeros_like(vec)
    wait(c.lens)
    side = decoding.astype(jnp.int32)
    write_bias(bias, lens, row, side, side, -1, decoding)

    wait(c.ga)
    gs[...] = gaf[...].astype(BF16)
    wait(c.wout)
    gatt[...] = nt(gs[...], wout[...]).astype(BF16)
    wait(c.att, c.packed, c.stat)
    attend_backward(
        packed, 0, packed, D, packed, 2 * D, gatt, att, bias, stat, turned, dq, inner, scores, drops, probs, slants,
        gpack, D,
    )
    gpack[:, 0:D] = (dq[...] * HEAD**-0.5).astype(BF16).T
    if row:
        wait(c.prior)
    wait(c.normed)
    add_block(grads, slice(3 * D, 4 * D), tn(att[...], gs[...]), row)
    flipped = normed[...].T
    for cols in blocks_of(3 * D):
        add_block(grads, cols, nn(flipped, gpack[:, cols]), row)
    start(c.grads)
    wait(c.wqkv, c.x, c.ng)

    @pl.when(encoding)
    def _():
        wait(c.gxe)

    @pl.when(decoding)
    def _():
        wait(c.gx)

    @for_rows
    def _(part):
        for index, cols in enumerate(blocks_of(3 * D)):
            value = nt(gpack[part, cols], wqkv[:, cols])
            grad = value if index == 0 else grad + value
        xhat, scale = normalize(x[part, :].astype(F32))
        add_row(vec, V_GAIN1, col_sum(grad * xhat))
        add_row(vec, V_SHIFT1, col_sum(grad))
        grad_out[part, :] = gaf[part, :] + gx[part, :] + norm_input_grad(grad, ng[0:1], xhat, scale)

    start(c.grad, c.vec)
    wait(c.grads, c.grad, c.vec)


def any_spec():
    return pl.BlockSpec(memory_space=pl.ANY)


def vmem_spec():
    return pl.BlockSpec(memory_space=pltpu.VMEM)


def smem_spec():
    return pl.BlockSpec(memory_space=pltpu.SMEM)


def shape(*dims, dtype=BF16):
    return jax.ShapeDtypeStruct(dims, dtype)


def scratch_of(shapes):
    return [pltpu.VMEM(item.shape, item.dtype) for item in shapes]


PARAMS = pltpu.CompilerParams(vmem_limit_bytes=63 * 1024 * 1024)


def made(dims, dtype=BF16):
    return pltpu.VMEM(dims, dtype)


def call(kernel, name, arrays, inputs, outs, extra, copies, aliases=None, unheld=()):
    return pl.pallas_call(
        kernel,
        out_shape=[shape(V_ROWS, D, dtype=F32)] + outs + list(unheld),
        in_specs=[any_spec()] * len(arrays),
        out_specs=[any_spec()] * (1 + len(outs) + len(unheld)),
        input_output_aliases=aliases or {},
        scratch_shapes=inputs
        + [made((V_ROWS, D), F32)]
        + scratch_of(outs)
        + extra
        + [pltpu.SemaphoreType.DMA((copies,))],
        compiler_params=PARAMS,
        name=name,
    )(*arrays)


VECTOR = made((1, D), F32)
PAIR = made((2, D), F32)
WIDE = made((1, FF), F32)
ROW = made((L, D))
ROW32 = made((L, D), F32)
WUP, WDN, WSQ = made((D, FF)), made((FF, D)), made((D, D))
STAT = made((HEADS, 1, L), F32)
COLUMN = made((L, 128), F32)
ONE = pltpu.SMEM((1,), F32)


def lens_of(arrays):
    return pltpu.SMEM(arrays.shape, arrays.dtype)


def call_a(row, lengths, running, arrays):
    outs = [
        shape(L, D), shape(L, D, dtype=F32), shape(L, 3 * D), shape(L, D), shape(HEADS, 1, L, dtype=F32), shape(L, D),
        shape(L, D), shape(L, FF), shape(L, FF), shape(L, D),
    ]
    inputs = [
        ROW, PAIR, PAIR, lens_of(lengths), made(running.shape, running.dtype), WIDE, VECTOR, VECTOR, ONE, VECTOR, VECTOR,
        made((D, 3 * D)), WSQ, WUP, WDN, WSQ,
    ]
    extra = [ROW32, COLUMN, pltpu.SMEM((2,), F32)]
    aliases = {len(arrays) - 1: 1 + len(outs)} if row else {}
    kernel = functools.partial(kernel_a, row)
    return call(kernel, "forward_a", arrays, inputs, outs, extra, 34, aliases, [shape(*arrays[0].shape)])


ATTEND_SCRATCH = [
    made((D, L)), ROW32, STAT, made((2, L, L), F32), made((2, L, L), F32), made((L, PER * L)), made((L, PER * L)),
]


def call_b(row, lengths, running, arrays):
    outs = [
        shape(L, D), shape(L, FF), shape(L, D), shape(L, FF), shape(L, D), shape(L, D), shape(D, L), shape(L, 2 * D),
        shape(L, D), shape(L, D, dtype=F32), shape(L, D, dtype=F32),
    ]
    inputs = [
        ROW, ROW, PAIR, PAIR, lens_of(lengths), made(running.shape, running.dtype), WIDE, VECTOR, VECTOR, ONE,
        WUP, WDN, made((D, 2 * D)), WSQ, ROW, ROW, ROW32,
    ]
    extra = [ROW, made((L, 2 * D)), made((L, FF)), ROW32, ROW, ROW32, STAT, COLUMN, *ATTEND_SCRATCH, pltpu.SMEM((2,), F32)]
    aliases = {len(arrays) - 1: 1 + len(outs)}
    kernel = functools.partial(kernel_b, row)
    return call(kernel, "decoder_b", arrays, inputs, outs, extra, 30, aliases, [shape(*arrays[0].shape)])


def call_c(row, running, arrays):
    outs = [shape(L, D, dtype=F32), shape(L, D, dtype=F32), shape(2 * FF, D), shape(L, D)]
    inputs = [
        ROW, ROW, PAIR, made(running.shape, running.dtype), VECTOR, ONE, WUP, WDN, ROW, ROW32, made((L, FF)), ROW, ROW,
        made((L, FF)), VECTOR, WSQ, made((D, L)),
    ]
    held = scratch_of(outs)
    return pl.pallas_call(
        functools.partial(kernel_c, row),
        out_shape=[shape(V_ROWS, D, dtype=F32)] + outs,
        in_specs=[any_spec()] * len(arrays),
        out_specs=[any_spec()] * 5,
        scratch_shapes=inputs
        + [made((V_ROWS, D), F32), held[0], held[1], ROW, made((L, FF)), held[2], held[3], COLUMN]
        + [pltpu.SemaphoreType.DMA((28,))],
        compiler_params=PARAMS,
        name="feed_backward",
    )(*arrays)


def call_s(row, lengths, arrays):
    outs = [shape(4 * D, D)]
    inputs = [ROW, PAIR, lens_of(lengths), made((D, 3 * D)), WSQ, made((L, 3 * D)), STAT, ROW, ROW, ROW32, ROW32]
    extra = [ROW32, ROW, made((L, 3 * D)), ROW, ROW32, *ATTEND_SCRATCH]
    aliases = {len(arrays) - 1: 2} if row else {}
    kernel = functools.partial(kernel_s, row)
    whole = shape(*arrays[0].shape, dtype=F32)
    return call(kernel, "self_backward", arrays, inputs, outs, extra, 17, aliases, [whole])


def kernel_w(*refs):
    count = (len(refs) - 3) // 2
    sources, out_hbm, held, outs, sems = refs[:count], refs[count], refs[count + 1 : -2], refs[-2], refs[-1]

    @pl.when(on_decoder())
    def _():
        copies = [pltpu.make_async_copy(sources[i], held[i], sems.at[i]) for i in range(count)]
        start(*copies)
        block, each = 0, count // 3
        for pair in range(3):
            mine = slice(pair * each, (pair + 1) * each)
            wait(*copies[mine])
            lefts, rights = held[mine][: each // 2], held[mine][each // 2 :]
            turned = [left[...].T for left in lefts]
            for cols in blocks_of(rights[0].shape[1]):
                value = nn(turned[0], rights[0][:, cols])
                for left, right in zip(turned[1:], rights[1:]):
                    value += nn(left, right[:, cols])
                outs[block * D : (block + 1) * D, :] = value.astype(BF16)
                block += 1
        out = pltpu.make_async_copy(outs, out_hbm, sems.at[count])
        start(out)
        wait(out)


def call_w(pairs):
    flat = [item for lefts, rights in pairs for item in (*lefts, *rights)]
    return pl.pallas_call(
        kernel_w,
        out_shape=shape(4 * D, D),
        in_specs=[any_spec()] * len(flat),
        out_specs=any_spec(),
        scratch_shapes=scratch_of(flat) + [made((4 * D, D)), pltpu.SemaphoreType.DMA((len(flat) + 1,))],
        compiler_params=PARAMS,
        name="cross_weights",
    )(*flat)


class Places:
    def __init__(self):
        self.count = lax.axis_size(DP)
        self.far = self.count // 4
        me = lax.axis_index(DP)
        self.core, self.near, self.rest = me % 2, (me // 2) % 2, me // 4

    def swap(self, value, bit, axis=DP, base=0):
        pairs = [(base + i, base + (i ^ bit)) for i in range(self.count)]
        return lax.ppermute(value, axis, pairs)

    def turn(self, value, steps, axis=DP, base=0):
        pairs = [(base + i, base + (i + 4 * steps) % self.count) for i in range(self.count)]
        return lax.ppermute(value, axis, pairs)


def halves(value, bit):
    half = value.shape[0] // 2
    mine = lax.dynamic_slice_in_dim(value, bit * half, half, 0)
    other = lax.dynamic_slice_in_dim(value, (1 - bit) * half, half, 0)
    return mine, other


def plus(left, right):
    return (left.astype(F32) + right.astype(F32)).astype(BF16)


def scatter_steps(places, value, axis=DP, base=0):
    mine, other = halves(value, places.core)
    value = plus(mine, (yield places.swap(other, 1, axis, base)))
    mine, other = halves(value, places.near)
    value = plus(mine, (yield places.swap(other, 2, axis, base)))
    parts = value.reshape(places.far, -1, D)
    total = lax.dynamic_index_in_dim(parts, places.rest, 0, keepdims=False).astype(F32)
    sent = []
    for step in range(1, places.far):
        part = lax.dynamic_index_in_dim(parts, (places.rest + step) % places.far, 0, keepdims=False)
        sent.append(places.turn(part, step, axis, base))
    for part in (yield sent):
        total = total + part.astype(F32)
    yield total.astype(BF16)


def gather_steps(places, share):
    parts = jnp.stack([share] + (yield [places.turn(share, step) for step in range(1, places.far)]))
    yield jnp.stack([parts, (yield places.swap(parts, 2))])


def vector_steps(places, value):
    bit = 1
    while bit < places.count:
        value = value + (yield places.swap(value, bit))
        bit *= 2
    cross = value[V_GAINC : V_SHIFTC + 1]
    yield value, cross + (yield lax.ppermute(cross, SECTION, [(0, 1), (1, 0)]))


def advance(steps, arrived):
    arrived = lax.optimization_barrier(arrived)
    return [step.send(item) for step, item in zip(steps, arrived)]


def place_kernel(far, groups, where_ref, *refs):
    outs = refs[2 * len(groups) :]
    core, near, rest = where_ref[0], where_ref[1], where_ref[2]
    for index, blocks in enumerate(groups):
        own_ref, other_ref = refs[2 * index : 2 * index + 2]
        rows = own_ref.shape[2]
        for share in range(4 * far):
            c, n, q = share // (2 * far), share // far % 2, share % far
            out, col = blocks[share * rows // D]
            start = share * rows % D
            step = lax.rem(rest - q + far, far)
            which = lax.rem(near + n, 2)
            target = (out, slice(start, start + rows), slice(col * D, (col + 1) * D))

            @pl.when(core == c)
            def _(target=target, source=own_ref):
                outs[target[0]][target[1], target[2]] = source[which, step].astype(F32)

            @pl.when(core != c)
            def _(target=target, source=other_ref):
                outs[target[0]][target[1], target[2]] = source[which, step].astype(F32)


def put_in_place(places, gathered, groups, widths):
    where = jnp.stack([places.core, places.near, places.rest]).astype(jnp.int32)
    flat = [item for pair in gathered for item in pair]
    return pl.pallas_call(
        functools.partial(place_kernel, places.far, groups),
        out_shape=[shape(D, width, dtype=F32) for width in widths],
        in_specs=[smem_spec()] + [vmem_spec()] * len(flat),
        out_specs=[vmem_spec()] * len(widths),
        compiler_params=PARAMS,
        name="place_sums",
    )(where, *flat)


def widen_kernel(up_in, down_in, up_out, down_out):
    up_out[...] = up_in[...].astype(F32)
    down_out[...] = down_in[...].astype(F32)


def widen(grads):
    count = FF // D
    return pl.pallas_call(
        widen_kernel,
        grid=(count,),
        out_shape=[shape(D, FF, dtype=F32), shape(FF, D, dtype=F32)],
        in_specs=[pl.BlockSpec((D, D), lambda i: (i, 0)), pl.BlockSpec((D, D), lambda i: (count + i, 0))],
        out_specs=[pl.BlockSpec((D, D), lambda i: (0, i)), pl.BlockSpec((D, D), lambda i: (i, 0))],
        compiler_params=PARAMS,
        name="widen",
    )(grads, grads)


def shards(
    inputs, cotangent, lengths, running, norm_gain, norm_shift, qkv_weight, out_weight, up_weight, up_bias,
    down_weight, down_bias, halt_weight, halt_bias, cross_gain, cross_shift, cross_query, cross_kv, cross_out,
):
    decoding = on_decoder()
    places = Places()
    rows = range(inputs.shape[1])
    vectors = (norm_gain, norm_shift, lengths, running, up_bias, down_bias, halt_weight, halt_bias)
    crosses = (cross_gain[None], cross_shift[None])
    firsts, received = [], []
    for row in rows:
        arrays = (
            inputs, *vectors, *crosses, qkv_weight, out_weight, up_weight, down_weight, cross_query,
            *([firsts[row - 1][11]] if row else []),
        )
        firsts.append(call_a(row, lengths, running, arrays))
        received.append(lax.ppermute(firsts[row][1], SECTION, [(0, 1)]))
    result = firsts[-1][11]
    middles, returned = [], []
    for row in rows:
        _, out, after = firsts[row][:3]
        arrays = (
            inputs, cotangent, *vectors, up_weight, down_weight, cross_kv, cross_out, received[row], out, after, result,
        )
        middles.append(call_b(row, lengths, running, arrays))
        result = middles[row][12]
        returned.append(lax.ppermute(middles[row][9], SECTION, [(1, 0)]))

    def both(items, index):
        return [item[index] for item in items]

    feeds = []
    for row in rows:
        _, _, after, _, _, _, _, n2, act, slope, change, _ = firsts[row]
        arrays = (
            inputs, cotangent, norm_gain, running, halt_weight, halt_bias, up_weight, down_weight, returned[row], after,
            slope, change, n2, act, *middles[row][1:5], crosses[0], cross_query, middles[row][7], middles[row][10],
            *([feeds[row - 1][3]] if row else []),
        )
        feeds.append(call_c(row, running, arrays))
    feed_sum = lax.psum(feeds[-1][3], DP)
    vec_before = sum(both(middles, 0)) + sum(both(feeds, 0))
    groups = [[(0, 0), (0, 1), (0, 2), (1, 0)], [(2, 0), (3, 0), (3, 1), (4, 0)]]
    widths = [3 * D, D, D, 2 * D, D]

    def tail(operands):
        firsts, middles, feeds, received, vec = operands
        cross_grads = call_w(
            [
                (both(firsts, 10), both(feeds, 4)),
                (received, both(middles, 8)),
                (both(middles, 5), both(middles, 6)),
            ]
        )
        crosses = scatter_steps(places, cross_grads, (SECTION, DP), places.count)
        cross_sent = next(crosses)
        selves = []
        for row in rows:
            _, _, _, packed, att, stat, normed, _, _, _, _, _ = firsts[row]
            before = ()
            if row:
                cross_sent, *before = lax.optimization_barrier((cross_sent, *selves[row - 1][1:]))
                cross_sent = crosses.send(cross_sent)
            arrays = (
                inputs, norm_gain, lengths, qkv_weight, out_weight, packed, stat, normed, att, *feeds[row][1:3],
                middles[row][11], *before,
            )
            selves.append(call_s(row, lengths, arrays))
        cross_sent, self_grads = lax.optimization_barrier((cross_sent, selves[-1][1]))
        cross_sent = crosses.send(cross_sent)
        vec = vec + sum(both(selves, 0))
        sums = [scatter_steps(places, self_grads), vector_steps(places, vec)]
        sent = [next(step) for step in sums]
        cross_share = crosses.send(cross_sent)
        cross_share = jnp.where(decoding, cross_share, lax.ppermute(cross_share, SECTION, [(1, 0)]))
        for _ in range(3):
            sent = advance(sums, sent)
        self_share, vec_sent = sent
        small = sums[1]
        gathers = [gather_steps(places, self_share), gather_steps(places, cross_share)]
        sent = [next(step) for step in gathers]
        arrived = lax.optimization_barrier((sent[0], vec_sent))
        sent = [gathers[0].send(arrived[0]), gathers[1].send(sent[1])]
        vec_sent = small.send(arrived[1])
        gathered = [gather.send(item) for gather, item in zip(gathers, sent)]
        while not isinstance(vec_sent, tuple):
            vec_sent = small.send(vec_sent)
        stats = [jnp.where(decoding, middles[row][0], firsts[row][0])[V_RMS, :2] for row in rows]
        row_rms = jnp.sqrt(jnp.stack(stats) / (L * D) + 1e-06)
        return *gathered, *vec_sent, row_rms, selves[-1][2]

    def nothing(operands):
        vec = operands[-1]
        parts = jnp.zeros((2, places.far, 4 * D // places.count, D), BF16)
        return parts, parts, vec, vec[:2], vec[:2, :2], jnp.zeros(inputs.shape, F32)

    *gathered, vec, cross_vec, row_rms, input_grad = lax.cond(
        lengths[0, 0, 0] > 0, tail, nothing, (firsts, middles, feeds, received, vec_before)
    )
    gathered = [(parts, places.swap(parts, 1)) for parts in gathered]
    qkv_sum, out_sum, query_sum, kv_sum, cross_out_sum = put_in_place(places, gathered, groups, widths)
    up_sum, down_sum = widen(feed_sum)
    return (
        result,
        input_grad,
        row_rms[None],
        jnp.stack([vec[V_GAIN1], vec[V_GAIN2]])[None],
        jnp.stack([vec[V_SHIFT1], vec[V_SHIFT2]])[None],
        qkv_sum[None],
        out_sum[None],
        up_sum[None],
        vec[V_UPB : V_UPB + 4].reshape(1, FF),
        down_sum[None],
        vec[V_DOWNB][None],
        vec[V_HW][None],
        vec[V_HB, :1],
        cross_vec[0],
        cross_vec[1],
        query_sum,
        kv_sum,
        cross_out_sum,
    )


def solution(mesh):
    in_specs = (
        P(SECTION, DP, None, None),
        P(SECTION, DP, None, None),
        P(None, DP, None),
        P(SECTION, DP, None),
        P(SECTION, None, None),
        P(SECTION, None, None),
        P(SECTION, None, None),
        P(SECTION, None, None),
        P(SECTION, None, None),
        P(SECTION, None),
        P(SECTION, None, None),
        P(SECTION, None),
        P(SECTION, None),
        P(SECTION),
        P(),
        P(),
        P(),
        P(),
        P(),
    )
    out_specs = (
        P(SECTION, DP, None, None),
        P(SECTION, DP, None, None),
        P(SECTION, DP, None),
        P(SECTION, None, None),
        P(SECTION, None, None),
        P(SECTION, None, None),
        P(SECTION, None, None),
        P(SECTION, None, None),
        P(SECTION, None),
        P(SECTION, None, None),
        P(SECTION, None),
        P(SECTION, None),
        P(SECTION),
        P(),
        P(),
        P(),
        P(),
        P(),
    )
    return jax.shard_map(shards, mesh=mesh, in_specs=in_specs, out_specs=out_specs, check_vma=False)
```

```python
import functools

import jax
import jax.numpy as jnp
from jax import lax
from jax.experimental import pallas as pl
from jax.experimental.pallas import tpu as pltpu
from jax.sharding import PartitionSpec as P

L = 512
D = 512
FF = 2048
HEADS = 8
SECTION, DP = "section", "dp"
HEAD = D // HEADS
GROUP = 256
PER = GROUP // HEAD
RC = 512
EPS = 1e-05
MASKED = -1000000000.0
GELU_A = 0.7978845608028654
GELU_B = 0.044715
F32 = jnp.float32
BF16 = jnp.bfloat16

V_GAIN2, V_SHIFT2, V_UPB, V_DOWNB, V_HW, V_HB = 0, 1, 2, 6, 7, 8
V_GAINC, V_SHIFTC, V_GAIN1, V_SHIFT1, V_RMS = 9, 10, 11, 12, 13
V_ROWS = 16


def nn(left, right):
    return lax.dot_general(left, right, (((1,), (0,)), ((), ())), preferred_element_type=F32)


def nt(left, right):
    return lax.dot_general(left, right, (((1,), (1,)), ((), ())), preferred_element_type=F32)


def tn(left, right):
    return lax.dot_general(left, right, (((0,), (0,)), ((), ())), preferred_element_type=F32)


def col_sum(value):
    return jnp.sum(value, axis=0, keepdims=True)


def row_mean(value):
    return jnp.mean(value, axis=1, keepdims=True)


def normalize(value):
    centered = value - row_mean(value)
    scale = lax.rsqrt(row_mean(centered * centered) + EPS)
    return centered * scale, scale


def norm_input_grad(grad, gain, xhat, scale):
    scaled = grad * gain
    return scale * (scaled - row_mean(scaled) - xhat * row_mean(scaled * xhat))


def each(count, size, body):
    def step(index, carry):
        body(index, pl.ds(pl.multiple_of(index * size, size), size))
        return carry

    lax.fori_loop(0, count, step, 0)


def each_apart(count, size, body):
    for index in range(count):
        body(index, pl.ds(index * size, size))


def for_rows(body):
    for first in range(0, L, RC):
        body(slice(first, first + RC))


def head_masks():
    lane = lax.broadcasted_iota(jnp.int32, (1, GROUP), 1)
    return [(lane // HEAD) == place for place in range(PER)]


def keep(mask, value):
    return jnp.where(mask, value, jnp.zeros_like(value))


def segments(len_ref, side, row, shape, dim, first):
    place = lax.broadcasted_iota(jnp.int32, shape, dim) + first
    total = jnp.int32(0)
    found = jnp.zeros(shape, jnp.int32)
    for index in range(len_ref.shape[2]):
        total = total + len_ref[side, row, index]
        found = found + (place >= total).astype(jnp.int32)
    return found


def write_bias(bias_ref, len_ref, row, row_side, col_side, causal_sign, causal):
    across = segments(len_ref, col_side, row, (1, L), 1, 0)

    def some(part):
        allowed = segments(len_ref, row_side, row, (RC, 1), 0, part.start) == across
        if causal is not None:
            row_place = lax.broadcasted_iota(jnp.int32, (RC, L), 0) + part.start
            col_place = lax.broadcasted_iota(jnp.int32, (RC, L), 1)
            ordered = (row_place - col_place) * causal_sign >= 0
            allowed = allowed & (ordered | jnp.logical_not(causal))
        bias_ref[part, :] = jnp.where(allowed, 0.0, MASKED)

    for_rows(some)


def attend_forward(queries, q0, keys, k0, values, v0, bias_ref, out_ref, stat_ref, column_ref, loop=each):
    masks = head_masks()
    lane = lax.broadcasted_iota(jnp.int32, (1, 128), 1)
    column_ref[...] = jnp.zeros_like(column_ref)

    def of_group(index, cols):
        own_q, own_k, own_v = (ref[:, moved(cols, first)] for ref, first in ((queries, q0), (keys, k0), (values, v0)))
        stats = column_ref[...]
        weights = []
        for place in range(PER):
            scores = nt(keep(masks[place], own_q), own_k) + bias_ref[...]
            top = jnp.max(scores, axis=1, keepdims=True)
            expanded = jnp.exp(scores - top)
            total = jnp.sum(expanded, axis=1, keepdims=True)
            weights.append((expanded * (1.0 / total)).astype(BF16))
            stats = jnp.where(lane == index * PER + place, top + jnp.log(total), stats)
        column_ref[...] = stats
        stacked = jnp.concatenate([keep(mask, own_v) for mask in masks], axis=0)
        out_ref[:, cols] = nn(jnp.concatenate(weights, axis=1), stacked).astype(BF16)

    loop(D // GROUP, GROUP, of_group)
    turned = column_ref[...].T
    for head in range(HEADS):
        stat_ref[head] = turned[head : head + 1, :]


def moved(cols, first):
    place = cols.start + first
    return pl.ds(place if isinstance(place, int) else pl.multiple_of(place, GROUP), cols.size)


def attend_backward(
    queries, q0, keys, k0, values, v0, grads, bias_ref, stat_ref,
    turned_ref, dq_ref, scores_ref, drops_ref, probs_ref, slants_ref, target, t0,
):
    masks = head_masks()

    def of_group(index, cols):
        own_q, own_k, own_v = (ref[:, moved(cols, first)] for ref, first in ((queries, q0), (keys, k0), (values, v0)))
        own_g = grads[:, cols]
        turned_ref[cols, :] = own_k.T
        for place in range(PER):
            head, slot = index * PER + place, place % 2
            rows, across = pl.ds(pl.multiple_of(head * HEAD, HEAD), HEAD), slice(place * L, (place + 1) * L)
            scores_ref[slot] = nt(keep(masks[place], own_k), own_q)
            drops_ref[slot] = nt(keep(masks[place], own_v), own_g)
            log_total, inner = stat_ref[head], jnp.zeros((8, L), F32)
            for part in range(0, L, 64):
                lines = slice(part, part + 64)
                probs = jnp.exp(scores_ref[slot, lines, :] + bias_ref[lines, :] - log_total)
                scores_ref[slot, lines, :] = probs
                probs_ref[lines, across] = probs.astype(BF16)
                inner += jnp.sum((probs * drops_ref[slot, lines, :]).reshape(8, 8, L), axis=0)
            inner = col_sum(inner)
            for part in range(0, L, 64):
                lines = slice(part, part + 64)
                slant = scores_ref[slot, lines, :] * (drops_ref[slot, lines, :] - inner)
                slants_ref[lines, across] = slant.astype(BF16)
            dq_ref[rows, :] = nn(turned_ref[rows, :], slants_ref[:, across])
        stacked = jnp.concatenate([keep(mask, own_q) for mask in masks], axis=0)
        target[:, moved(cols, t0)] = nn(slants_ref[...], stacked).astype(BF16)
        stacked = jnp.concatenate([keep(mask, own_g) for mask in masks], axis=0)
        target[:, moved(cols, t0 + D)] = nn(probs_ref[...], stacked).astype(BF16)

    each(D // GROUP, GROUP, of_group)


def gelu_parts(pre):
    square = pre * pre
    half = 0.5 + 0.5 * jnp.tanh(pre * (GELU_A + GELU_A * GELU_B * square))
    slope = half + half * (1.0 - half) * pre * (2.0 * GELU_A + 6.0 * GELU_A * GELU_B * square)
    return pre * half, slope


def feed_forward(
    after_ref, norm_gain, norm_shift, w_up, up_bias, w_down, down_bias, n2_ref, act_ref, slope_ref, total_ref, loop=each
):
    after = after_ref[...]
    n2_ref[...] = (normalize(after)[0] * norm_gain[1:2] + norm_shift[1:2]).astype(BF16)
    total_ref[...] = after + down_bias[...]

    def of_block(_, cols):
        activated, slope = gelu_parts(nn(n2_ref[...], w_up[:, cols]) + up_bias[:, cols])
        activated = activated.astype(BF16)
        act_ref[:, cols] = activated
        slope_ref[:, cols] = slope.astype(BF16)
        total_ref[...] += nn(activated, w_down[cols, :])

    loop(FF // D, D, of_block)


def feed_slope(gb_ref, w_down, slope_ref, gp_ref, bias_ref, w_up=None, back_ref=None, loop=each):
    def of_block(_, cols):
        value = (nt(gb_ref[...], w_down[cols, :]) * slope_ref[:, cols].astype(F32)).astype(BF16)
        gp_ref[:, cols] = value
        bias_ref[:, cols] = col_sum(value.astype(F32))
        if w_up is not None:
            back_ref[...] += nt(value, w_up[:, cols])

    loop(FF // D, D, of_block)


def add_up_bias(vec, bias_ref):
    for index, cols in enumerate(blocks_of(FF)):
        add_row(vec, V_UPB + index, bias_ref[:, cols])


def feed_input_grad(after_ref, back, grad_ref, gb_ref, norm_gain, vec, part):
    add_row(vec, V_DOWNB, col_sum(gb_ref[part, :].astype(F32)))
    xhat, scale = normalize(after_ref[part, :])
    add_row(vec, V_GAIN2, col_sum(back * xhat))
    add_row(vec, V_SHIFT2, col_sum(back))
    return grad_ref[part, :] + norm_input_grad(back, norm_gain[1:2], xhat, scale)


def write_running(column_ref, run_ref, row):
    line = run_ref[0, row : row + 1, :].astype(F32)
    column_ref[...] = jnp.broadcast_to(line, (128, L)).T


def halting_share(current, run, halt_weight, halt_bias):
    logit = jnp.sum(current * halt_weight[...], axis=1, keepdims=True) + halt_bias[0]
    rate = jax.nn.sigmoid(logit)
    return run * rate, rate


def halting_backward(grad, change, current, share, rate, run, halt_weight, vec_ref):
    logit_grad = (
        run * jnp.sum(grad * change, axis=1, keepdims=True) * rate * (1.0 - rate)
    )
    vec_ref[V_HW : V_HW + 1, :] += col_sum(logit_grad * current)
    vec_ref[V_HB : V_HB + 1, :] += jnp.broadcast_to(col_sum(logit_grad), (1, D))
    return share * grad, (1.0 - share) * grad + logit_grad * halt_weight[...]


def write_rms(vec_ref, total_ref):
    lane = lax.broadcasted_iota(jnp.int32, (1, D), 1)
    vec_ref[V_RMS : V_RMS + 1, :] = jnp.where(lane == 0, total_ref[0], total_ref[1])


class Copies:
    def __init__(self, sems, **pairs):
        for index, (name, (source, target)) in enumerate(pairs.items()):
            setattr(self, name, pltpu.make_async_copy(source, target, sems.at[index]))


def start(*copies):
    for copy in copies:
        copy.start()


def wait(*copies):
    for copy in copies:
        copy.wait()


def blocks_of(width):
    return [slice(place, place + D) for place in range(0, width, D)]


def on_decoder():
    return lax.axis_index(SECTION) == 1


def halves_out(held, mine_hbm, other_hbm, sems):
    half = held.shape[0] // 2
    core = lax.rem(lax.axis_index(DP), 2)
    return [
        pltpu.make_async_copy(held.at[pl.ds(pl.multiple_of(place * half, half), half)], target, sems.at[index])
        for index, (place, target) in enumerate(((core, mine_hbm), (1 - core, other_hbm)))
    ]


def add_row(vec, row, value):
    vec[row : row + 1, :] += value


def kernel_a(
    row,
    x_hbm, ng_hbm, ns_hbm, len_hbm, run_hbm, ub_hbm, db_hbm, hw_hbm, hb_hbm, cg_hbm, cs_hbm,
    wqkv_hbm, wout_hbm, wup_hbm, wdn_hbm, wcq_hbm,
    *rest,
):
    (
        vec_hbm, out_hbm, after_hbm, packed_hbm, att_hbm, stat_hbm, normed_hbm, n2_hbm, act_hbm, slope_hbm, change_hbm,
        normed2_hbm, result_hbm, x, ng, ns, lens, run, ub, db, hw, hb, cg, cs, wqkv, wout, wup, wdn, wcq,
        vec, out, after, packed, att, stat, normed, n2, act, slope, change, normed2, bias, column, total, sems,
    ) = rest[row > 0 :]
    decoding = on_decoder()
    encoding = jnp.logical_not(decoding)
    c = Copies(
        sems,
        x=(x_hbm.at[0, row], x), ng=(ng_hbm.at[0], ng), ns=(ns_hbm.at[0], ns), lens=(len_hbm, lens), run=(run_hbm, run),
        ub=(ub_hbm, ub), db=(db_hbm, db), hw=(hw_hbm, hw), hb=(hb_hbm, hb), cg=(cg_hbm, cg), cs=(cs_hbm, cs),
        wqkv=(wqkv_hbm.at[0], wqkv), wout=(wout_hbm.at[0], wout), wup=(wup_hbm.at[0], wup), wdn=(wdn_hbm.at[0], wdn),
        wcq=(wcq_hbm, wcq),
        vec=(vec, vec_hbm), out=(out, out_hbm), after=(after, after_hbm), packed=(packed, packed_hbm),
        att=(att, att_hbm), stat=(stat, stat_hbm), normed=(normed, normed_hbm), normed2=(normed2, normed2_hbm),
        n2=(n2, n2_hbm), act=(act, act_hbm), slope=(slope, slope_hbm), change=(change, change_hbm),
        result=(out, result_hbm.at[0, row]),
    )
    start(c.x, c.ng, c.ns, c.lens, c.wqkv, c.wout)

    @pl.when(encoding)
    def _():
        start(c.run, c.ub, c.db, c.hw, c.hb, c.wup, c.wdn)

    @pl.when(decoding)
    def _():
        start(c.cg, c.cs, c.wcq)

    wait(c.lens)
    side = decoding.astype(jnp.int32)
    write_bias(bias, lens, row, side, side, 1, decoding)
    wait(c.x, c.ng, c.ns)

    @for_rows
    def _(part):
        normed[part, :] = (normalize(x[part, :].astype(F32))[0] * ng[0:1] + ns[0:1]).astype(BF16)

    start(c.normed)
    wait(c.wqkv)
    for index, cols in enumerate(blocks_of(3 * D)):
        value = nn(normed[...], wqkv[:, cols]).astype(BF16)
        if index == 0:
            value = (value.astype(F32) * HEAD**-0.5).astype(BF16)
        packed[:, cols] = value
    start(c.packed)
    attend_forward(packed, 0, packed, D, packed, 2 * D, bias, att, stat, column, each_apart)
    start(c.att, c.stat)
    wait(c.wout)
    after[...] = x[...].astype(F32) + nn(att[...], wout[...])
    start(c.after)

    @pl.when(encoding)
    def _():
        wait(c.run, c.ub, c.db, c.hw, c.hb, c.wup, c.wdn)
        write_running(column, run, row)
        feed_forward(after, ng, ns, wup, ub, wdn, db, n2, act, slope, bias)
        start(c.n2, c.act, c.slope)
        total[0] = 0.0
        total[1] = 0.0

        @for_rows
        def _(part):
            updated = bias[part, :]
            current = x[part, :].astype(F32)
            share, _ = halting_share(current, column[part, :1], hw, hb)
            moved = updated - current
            change[part, :] = moved
            moved = share * moved
            result = current + moved
            out[part, :] = result.astype(BF16)
            total[0] += jnp.sum(result * result)
            total[1] += jnp.sum(moved * moved)

        start(c.out, c.change, c.result)
        vec[...] = jnp.zeros_like(vec)
        write_rms(vec, total)
        start(c.vec)
        wait(c.n2, c.act, c.slope, c.change, c.vec, c.result)

    @pl.when(decoding)
    def _():
        wait(c.cg, c.cs, c.wcq)

        @for_rows
        def _(part):
            normed2[part, :] = (normalize(after[part, :])[0] * cg[...] + cs[...]).astype(BF16)

        value = nn(normed2[...], wcq[...]).astype(BF16)
        out[...] = (value.astype(F32) * HEAD**-0.5).astype(BF16)
        start(c.out, c.normed2)
        vec[...] = jnp.zeros_like(vec)
        start(c.vec)
        wait(c.normed2, c.vec)

    wait(c.normed, c.packed, c.att, c.stat, c.after, c.out)


def kernel_b(
    row,
    x_hbm, cot_hbm, ng_hbm, ns_hbm, len_hbm, run_hbm, ub_hbm, db_hbm, hw_hbm, hb_hbm,
    wup_hbm, wdn_hbm, wkv_hbm, wco_hbm, mem_hbm, cq_hbm, after_hbm, _,
    vec_hbm, n2_hbm, act_hbm, gb_hbm, gp_hbm, att_hbm, gc_hbm, dq_hbm, gkv_hbm, back_hbm, ga_hbm, gx_hbm, result_hbm,
    x, cot, ng, ns, lens, run, ub, db, hw, hb, wup, wdn, wkv, wco, mem, cq, after,
    vec, n2, act, gb, gp, att, gc, dqb, gkv, back, gaf, gx,
    result, kv, slope, across, gatt, ubg, bias, bias2, stat, column, turned, dq, scores, drops, probs, slants, total, sems,
):
    c = Copies(
        sems,
        x=(x_hbm.at[0, row], x), cot=(cot_hbm.at[0, row], cot), ng=(ng_hbm.at[0], ng), ns=(ns_hbm.at[0], ns),
        lens=(len_hbm, lens), run=(run_hbm, run), ub=(ub_hbm, ub), db=(db_hbm, db), hw=(hw_hbm, hw), hb=(hb_hbm, hb),
        wup=(wup_hbm.at[0], wup), wdn=(wdn_hbm.at[0], wdn), wkv=(wkv_hbm, wkv),
        wco=(wco_hbm, wco), mem=(mem_hbm, mem), cq=(cq_hbm, cq), after=(after_hbm, after),
        vec=(vec, vec_hbm), n2=(n2, n2_hbm), act=(act, act_hbm), gb=(gb, gb_hbm), gp=(gp, gp_hbm), att=(att, att_hbm),
        gc=(gc, gc_hbm), dq=(dqb, dq_hbm), gkv=(gkv, gkv_hbm), back=(back, back_hbm), result=(result, result_hbm.at[0, row]),
        ga=(gaf, ga_hbm), gx=(gx, gx_hbm),
    )
    decoding = on_decoder()

    @pl.when(jnp.logical_not(decoding))
    def _():
        vec[...] = jnp.zeros_like(vec)
        start(c.vec)

    @pl.when(decoding)
    def _():
        start(c.mem, c.wkv, c.lens, c.cq, c.wco, c.after, c.ng, c.ns, c.ub, c.db, c.wup, c.wdn)
        start(c.x, c.cot, c.run, c.hw, c.hb)
        vec[...] = jnp.zeros_like(vec)
        wait(c.lens)
        write_bias(bias, lens, row, 1, 0, 1, None)
        write_bias(bias2, lens, row, 0, 1, 1, None)
        wait(c.mem, c.wkv)
        for cols in blocks_of(2 * D):
            kv[:, cols] = nn(mem[...], wkv[:, cols]).astype(BF16)
        wait(c.cq)
        attend_forward(cq, 0, kv, 0, kv, D, bias, att, stat, column, each_apart)
        start(c.att)
        wait(c.after, c.wco)
        across[...] = after[...] + nn(att[...], wco[...])
        wait(c.ng, c.ns, c.ub, c.db, c.wup, c.wdn, c.x, c.cot, c.run, c.hw, c.hb)
        write_running(column, run, row)
        feed_forward(across, ng, ns, wup, ub, wdn, db, n2, act, slope, dq, each_apart)
        start(c.n2, c.act)
        total[0] = 0.0
        total[1] = 0.0

        @for_rows
        def _(part):
            updated = dq[part, :]
            current = x[part, :].astype(F32)
            share, rate = halting_share(current, column[part, :1], hw, hb)
            moved = updated - current
            grad, own = halting_backward(
                cot[part, :].astype(F32), moved, current, share, rate, column[part, :1], hw, vec
            )
            gx[part, :] = own
            moved = share * moved
            value = current + moved
            result[part, :] = value.astype(BF16)
            total[0] += jnp.sum(value * value)
            total[1] += jnp.sum(moved * moved)
            gaf[part, :] = grad
            gb[part, :] = grad.astype(BF16)

        start(c.gb, c.result, c.gx)

        dq[...] = jnp.zeros_like(dq)
        feed_slope(gb, wdn, slope, gp, ubg, wup, dq, each_apart)
        start(c.gp)
        add_up_bias(vec, ubg)

        @for_rows
        def _(part):
            grad = feed_input_grad(across, dq[part, :], gaf, gb, ng, vec, part)
            gaf[part, :] = grad
            gc[part, :] = grad.astype(BF16)

        gatt[...] = nt(gc[...], wco[...]).astype(BF16)
        start(c.gc, c.ga)
        write_rms(vec, total)
        start(c.vec)
        attend_backward(
            cq, 0, kv, 0, kv, D, gatt, bias2, stat, turned, dq, scores, drops, probs, slants, gkv, 0
        )
        start(c.gkv)
        dqb[...] = (dq[...] * HEAD**-0.5).astype(BF16)
        start(c.dq)
        back[...] = (nt(gkv[:, 0:D], wkv[:, 0:D]) + nt(gkv[:, D:], wkv[:, D:])).astype(BF16)
        start(c.back)
        wait(c.att, c.n2, c.act, c.gb, c.gp, c.gc, c.result, c.gx, c.gkv, c.dq, c.back, c.ga)

    wait(c.vec)


def kernel_c(
    row,
    x_hbm, cot_hbm, ng_hbm, run_hbm, hw_hbm, hb_hbm, wup_hbm, wdn_hbm, back_hbm, after_hbm, slope_hbm, change_hbm,
    n2e_hbm, acte_hbm, n2_hbm, act_hbm, gb_hbm, gp_hbm, cg_hbm, wcq_hbm, dq_hbm, gad_hbm, *rest,
):
    prior_hbm, rest = (rest[0], rest[1:]) if row else (None, rest)
    vec_hbm, ga_hbm, gx_hbm, grads_hbm, gq_hbm = rest[:5]
    (
        x, cot, ng, run, hw, hb, wup, wdn, back, after, slope, change, n2, act, cg, wcq, dq, vec, gaf, gx, gb, gp, grads, gq,
        column, column32, turned, ubg, sems,
    ) = rest[5:]
    decoding = on_decoder()
    encoding = jnp.logical_not(decoding)
    c = Copies(
        sems,
        x=(x_hbm.at[0, row], x), cot=(cot_hbm.at[0, row], cot), ng=(ng_hbm.at[0], ng), run=(run_hbm, run),
        hw=(hw_hbm, hw), hb=(hb_hbm, hb), wup=(wup_hbm.at[0], wup), wdn=(wdn_hbm.at[0], wdn), back=(back_hbm, back),
        after=(after_hbm, after), slope=(slope_hbm, slope), change=(change_hbm, change), n2e=(n2e_hbm, n2),
        acte=(acte_hbm, act), n2=(n2_hbm, n2), act=(act_hbm, act), gb=(gb_hbm, gb), gp=(gp_hbm, gp),
        vec=(vec, vec_hbm), ga=(gaf, ga_hbm), gx=(gx, gx_hbm), grads=(grads, grads_hbm), cg=(cg_hbm, cg),
        wcq=(wcq_hbm, wcq), dq=(dq_hbm, dq), gad=(gad_hbm, gaf), gq=(gq, gq_hbm),
        **({"prior": (prior_hbm, grads)} if row else {}),
    )
    vec[...] = jnp.zeros_like(vec)

    @pl.when(encoding)
    def _():
        start(c.back, c.cot, c.x, c.change, c.run, c.hw, c.hb, c.wdn, c.slope, c.n2e, c.acte, c.wup, c.after, c.ng)
        if row:
            start(c.prior)
        wait(c.back, c.cot, c.x, c.change, c.run, c.hw, c.hb)
        write_running(column, run, row)

        @for_rows
        def _(part):
            grad = cot[part, :].astype(F32) + back[part, :].astype(F32)
            current = x[part, :].astype(F32)
            share, rate = halting_share(current, column[part, :1], hw, hb)
            grad, own = halting_backward(
                grad, change[part, :], current, share, rate, column[part, :1], hw, vec
            )
            gx[part, :] = own
            gaf[part, :] = grad
            gb[part, :] = grad.astype(BF16)

        start(c.gx)
        wait(c.wdn, c.slope)
        feed_slope(gb, wdn, slope, gp, ubg)
        add_up_bias(vec, ubg)
        wait(c.n2e, c.acte)

    @pl.when(decoding)
    def _():
        start(c.n2, c.gp, c.act, c.gb)
        if row:
            start(c.prior)
        start(c.dq, c.wcq, c.after, c.gad, c.cg)
        wait(c.n2, c.gp, c.act, c.gb)

    if row:
        wait(c.prior)
    turned[...] = n2[...].T

    def of_block(_, cols):
        add_block(grads, cols, nn(turned[...], gp[:, cols]), row)
        add_block(grads, pl.ds(FF + cols.start, D), tn(act[:, cols], gb[...]), row)

    each_apart(FF // D, D, of_block)
    start(c.grads)

    @pl.when(encoding)
    def _():
        wait(c.wup, c.after, c.ng)

        column32[...] = jnp.zeros_like(column32)

        def back_of(_, cols):
            column32[...] += nt(gp[:, cols], wup[:, cols])

        each(FF // D, D, back_of)

        @for_rows
        def _(part):
            gaf[part, :] = feed_input_grad(after, column32[part, :], gaf, gb, ng, vec, part)

        start(c.ga)
        wait(c.ga, c.gx)

    @pl.when(decoding)
    def _():
        wait(c.dq, c.wcq, c.after, c.gad, c.cg)
        gq[...] = dq[...].T
        start(c.gq)

        @for_rows
        def _(part):
            grad = nt(gq[part, :], wcq[...])
            xhat, scale = normalize(after[part, :])
            add_row(vec, V_GAINC, col_sum(grad * xhat))
            add_row(vec, V_SHIFTC, col_sum(grad))
            gaf[part, :] += norm_input_grad(grad, cg[...], xhat, scale)

        start(c.ga)
        wait(c.gq, c.ga)

    start(c.vec)
    wait(c.grads, c.vec)


def add_block(grads, rows, value, more):
    if more:
        value = value + grads[rows, :].astype(F32)
    grads[rows, :] = value.astype(BF16)


def kernel_s(count, x_hbm, ng_hbm, len_hbm, wqkv_hbm, wout_hbm, *rest):
    held = [rest[index * count : (index + 1) * count] for index in range(7)]
    vec_hbm, mine_hbm, other_hbm, grad_hbm = rest[7 * count : 7 * count + 4]
    (
        x, ng, lens, wqkv, wout, packed, stat, normed, att, gaf, gx, vec, grads, grad_out, sums, gs, gpack, gatt, bias,
        turned, dq, scores, drops, probs, slants, sems, row_sems, out_sems, half_sems,
    ) = rest[7 * count + 4 :]
    decoding = on_decoder()
    encoding = jnp.logical_not(decoding)
    c = Copies(
        sems,
        x=(x_hbm.at[0], x), ng=(ng_hbm.at[0], ng), lens=(len_hbm, lens), wqkv=(wqkv_hbm.at[0], wqkv),
        wout=(wout_hbm.at[0], wout), vec=(vec, vec_hbm),
    )
    halves = halves_out(grads, mine_hbm, other_hbm, half_sems)

    def of_row(row):
        places = (packed, stat, normed, att, gaf, gx, gx)
        return Copies(
            row_sems.at[row],
            **{
                name: (held[index][row], place.at[row])
                for index, (name, place) in enumerate(zip(("packed", "stat", "normed", "att", "ga", "gxe", "gxd"), places))
            },
        )

    lines = [of_row(row) for row in range(count)]
    start(c.lens, c.wout, lines[0].ga, lines[0].packed, lines[0].stat, lines[0].att, lines[0].normed, c.wqkv, c.x, c.ng)
    for line in lines[1:]:
        start(line.ga, line.packed, line.stat, line.att, line.normed)

    @pl.when(encoding)
    def _():
        start(*[line.gxe for line in lines])

    @pl.when(decoding)
    def _():
        start(*[line.gxd for line in lines])

    vec[...] = jnp.zeros_like(vec)
    sums[...] = jnp.zeros_like(sums)
    wait(c.lens, c.wout)
    side = decoding.astype(jnp.int32)

    def one_row(row, carry):
        for index in range(count):

            @pl.when(row == index)
            def _():
                wait(*[getattr(lines[index], name) for name in ("packed", "stat", "normed", "att", "ga")])

        write_bias(bias, lens, row, side, side, -1, decoding)
        gs[...] = gaf[row].astype(BF16)
        gatt[...] = nt(gs[...], wout[...]).astype(BF16)
        own = packed.at[row]
        attend_backward(
            own, 0, own, D, own, 2 * D, gatt, bias, stat.at[row], turned, dq, scores, drops, probs, slants, gpack, D
        )
        gpack[:, 0:D] = (dq[...] * HEAD**-0.5).astype(BF16).T
        sums[3 * D : 4 * D, :] += tn(att[row], gs[...])
        flipped = normed[row].T
        for cols in blocks_of(3 * D):
            sums[cols, :] += nn(flipped, gpack[:, cols])

        @pl.when(row == count - 1)
        def _():
            grads[...] = sums[...].astype(BF16)
            start(*halves)

        @pl.when(row == 0)
        def _():
            wait(c.wqkv, c.x, c.ng)

        for index in range(count):

            @pl.when((row == index) & encoding)
            def _():
                wait(lines[index].gxe)

            @pl.when((row == index) & decoding)
            def _():
                wait(lines[index].gxd)

        for index, cols in enumerate(blocks_of(3 * D)):
            value = nt(gpack[:, cols], wqkv[:, cols])
            grad = value if index == 0 else grad + value
        xhat, scale = normalize(x[row].astype(F32))
        add_row(vec, V_GAIN1, col_sum(grad * xhat))
        add_row(vec, V_SHIFT1, col_sum(grad))
        grad_out[row] = gaf[row] + gx[row] + norm_input_grad(grad, ng[0:1], xhat, scale)
        pltpu.make_async_copy(grad_out.at[row], grad_hbm.at[0, row], out_sems.at[row]).start()
        return carry

    lax.fori_loop(0, count, one_row, 0)
    start(c.vec)
    for row in range(count):
        pltpu.make_async_copy(grad_out.at[row], grad_hbm.at[0, row], out_sems.at[row]).wait()
    wait(*halves, c.vec)


def any_spec():
    return pl.BlockSpec(memory_space=pl.ANY)


def vmem_spec():
    return pl.BlockSpec(memory_space=pltpu.VMEM)


def smem_spec():
    return pl.BlockSpec(memory_space=pltpu.SMEM)


def shape(*dims, dtype=BF16):
    return jax.ShapeDtypeStruct(dims, dtype)


def scratch_of(shapes):
    return [pltpu.VMEM(item.shape, item.dtype) for item in shapes]


PARAMS = pltpu.CompilerParams(vmem_limit_bytes=63 * 1024 * 1024)


def made(dims, dtype=BF16):
    return pltpu.VMEM(dims, dtype)


def call(kernel, name, arrays, inputs, outs, extra, copies, aliases=None, unheld=()):
    return pl.pallas_call(
        kernel,
        out_shape=[shape(V_ROWS, D, dtype=F32)] + outs + list(unheld),
        in_specs=[any_spec()] * len(arrays),
        out_specs=[any_spec()] * (1 + len(outs) + len(unheld)),
        input_output_aliases=aliases or {},
        scratch_shapes=inputs
        + [made((V_ROWS, D), F32)]
        + scratch_of(outs)
        + extra
        + [pltpu.SemaphoreType.DMA((copies,))],
        compiler_params=PARAMS,
        name=name,
    )(*arrays)


VECTOR = made((1, D), F32)
PAIR = made((2, D), F32)
WIDE = made((1, FF), F32)
ROW = made((L, D))
ROW32 = made((L, D), F32)
WUP, WDN, WSQ = made((D, FF)), made((FF, D)), made((D, D))
STAT = made((HEADS, 1, L), F32)
COLUMN = made((L, 128), F32)
ONE = pltpu.SMEM((1,), F32)


def lens_of(arrays):
    return pltpu.SMEM(arrays.shape, arrays.dtype)


def call_a(row, lengths, running, arrays):
    outs = [
        shape(L, D), shape(L, D, dtype=F32), shape(L, 3 * D), shape(L, D), shape(HEADS, 1, L, dtype=F32), shape(L, D),
        shape(L, D), shape(L, FF), shape(L, FF), shape(L, D, dtype=F32), shape(L, D),
    ]
    inputs = [
        ROW, PAIR, PAIR, lens_of(lengths), made(running.shape, running.dtype), WIDE, VECTOR, VECTOR, ONE, VECTOR, VECTOR,
        made((D, 3 * D)), WSQ, WUP, WDN, WSQ,
    ]
    extra = [ROW32, COLUMN, pltpu.SMEM((2,), F32)]
    aliases = {len(arrays) - 1: 1 + len(outs)} if row else {}
    kernel = functools.partial(kernel_a, row)
    return call(kernel, "forward_a", arrays, inputs, outs, extra, 34, aliases, [shape(*arrays[0].shape)])


ATTEND_SCRATCH = [
    made((D, L)), ROW32, made((2, L, L), F32), made((2, L, L), F32), made((L, PER * L)), made((L, PER * L)),
]


def call_b(row, lengths, running, arrays):
    outs = [
        shape(L, D), shape(L, FF), shape(L, D), shape(L, FF), shape(L, D), shape(L, D), shape(D, L), shape(L, 2 * D),
        shape(L, D), shape(L, D, dtype=F32), shape(L, D, dtype=F32),
    ]
    inputs = [
        ROW, ROW, PAIR, PAIR, lens_of(lengths), made(running.shape, running.dtype), WIDE, VECTOR, VECTOR, ONE,
        WUP, WDN, made((D, 2 * D)), WSQ, ROW, ROW, ROW32,
    ]
    extra = [ROW, made((L, 2 * D)), made((L, FF)), ROW32, ROW, WIDE, ROW32, ROW32, STAT, COLUMN, *ATTEND_SCRATCH, pltpu.SMEM((2,), F32)]
    aliases = {len(arrays) - 1: 1 + len(outs)}
    kernel = functools.partial(kernel_b, row)
    return call(kernel, "decoder_b", arrays, inputs, outs, extra, 30, aliases, [shape(*arrays[0].shape)])


def call_c(row, running, arrays):
    outs = [shape(L, D, dtype=F32), shape(L, D, dtype=F32), shape(2 * FF, D), shape(L, D)]
    inputs = [
        ROW, ROW, PAIR, made(running.shape, running.dtype), VECTOR, ONE, WUP, WDN, ROW, ROW32, made((L, FF)), ROW32, ROW,
        made((L, FF)), VECTOR, WSQ, made((D, L)),
    ]
    held = scratch_of(outs)
    return pl.pallas_call(
        functools.partial(kernel_c, row),
        out_shape=[shape(V_ROWS, D, dtype=F32)] + outs,
        in_specs=[any_spec()] * len(arrays),
        out_specs=[any_spec()] * 5,
        scratch_shapes=inputs
        + [made((V_ROWS, D), F32), held[0], held[1], ROW, made((L, FF)), held[2], held[3], COLUMN, ROW32, made((D, L)), WIDE]
        + [pltpu.SemaphoreType.DMA((28,))],
        compiler_params=PARAMS,
        name="feed_backward",
    )(*arrays)


def call_s(count, lengths, arrays):
    def rows_of(dims, dtype=BF16):
        return made((count,) + dims, dtype)

    inputs = [
        rows_of((L, D)), PAIR, lens_of(lengths), made((D, 3 * D)), WSQ, rows_of((L, 3 * D)), rows_of((HEADS, 1, L), F32),
        rows_of((L, D)), rows_of((L, D)), rows_of((L, D), F32), rows_of((L, D), F32),
    ]
    extra = [rows_of((L, D), F32), made((4 * D, D), F32), ROW, made((L, 3 * D)), ROW, ROW32, *ATTEND_SCRATCH]
    return pl.pallas_call(
        functools.partial(kernel_s, count),
        out_shape=[shape(V_ROWS, D, dtype=F32)] + [shape(2 * D, D)] * 2 + [shape(*arrays[0].shape, dtype=F32)],
        in_specs=[any_spec()] * len(arrays),
        out_specs=[any_spec()] * 4,
        scratch_shapes=inputs
        + [made((V_ROWS, D), F32), made((4 * D, D))]
        + extra
        + [pltpu.SemaphoreType.DMA((7,)), pltpu.SemaphoreType.DMA((count, 7)), pltpu.SemaphoreType.DMA((count,))]
        + [pltpu.SemaphoreType.DMA((2,))],
        compiler_params=PARAMS,
        name="self_backward",
    )(*arrays)


def kernel_w(*refs):
    count = (len(refs) - 5) // 2
    sources, (mine_hbm, other_hbm), held = refs[:count], refs[count : count + 2], refs[count + 2 : -3]
    outs, sems, out_sems = refs[-3:]

    @pl.when(on_decoder())
    def _():
        copies = [pltpu.make_async_copy(sources[i], held[i], sems.at[i]) for i in range(count)]
        start(*copies)
        block, each = 0, count // 3
        for pair in range(3):
            mine = slice(pair * each, (pair + 1) * each)
            wait(*copies[mine])
            lefts, rights = held[mine][: each // 2], held[mine][each // 2 :]
            turned = [left[...].T for left in lefts]
            for cols in blocks_of(rights[0].shape[1]):
                value = nn(turned[0], rights[0][:, cols])
                for left, right in zip(turned[1:], rights[1:]):
                    value += nn(left, right[:, cols])
                outs[block * D : (block + 1) * D, :] = value.astype(BF16)
                block += 1
        copies = halves_out(outs, mine_hbm, other_hbm, out_sems)
        start(*copies)
        wait(*copies)


def call_w(pairs):
    flat = [item for lefts, rights in pairs for item in (*lefts, *rights)]
    return pl.pallas_call(
        kernel_w,
        out_shape=[shape(2 * D, D)] * 2,
        in_specs=[any_spec()] * len(flat),
        out_specs=[any_spec()] * 2,
        scratch_shapes=scratch_of(flat)
        + [made((4 * D, D)), pltpu.SemaphoreType.DMA((len(flat),)), pltpu.SemaphoreType.DMA((2,))],
        compiler_params=PARAMS,
        name="cross_weights",
    )(*flat)


class Places:
    def __init__(self):
        self.count = lax.axis_size(DP)
        self.far = self.count // 4
        me = lax.axis_index(DP)
        self.core, self.near, self.rest = me % 2, (me // 2) % 2, me // 4

    def swap(self, value, bit, axis=DP, base=0):
        pairs = [(base + i, base + (i ^ bit)) for i in range(self.count)]
        return lax.ppermute(value, axis, pairs)

    def turn(self, value, steps, axis=DP, base=0):
        pairs = [(base + i, base + (i + 4 * steps) % self.count) for i in range(self.count)]
        return lax.ppermute(value, axis, pairs)


def halves(value, bit):
    half = value.shape[0] // 2
    mine = lax.dynamic_slice_in_dim(value, bit * half, half, 0)
    other = lax.dynamic_slice_in_dim(value, (1 - bit) * half, half, 0)
    return mine, other


def plus(left, right):
    return (left.astype(F32) + right.astype(F32)).astype(BF16)


def scatter_steps(places, mine, other, axis=DP, base=0):
    value = plus(mine, (yield places.swap(other, 1, axis, base)))
    mine, other = halves(value, places.near)
    value = plus(mine, (yield places.swap(other, 2, axis, base)))
    parts = value.reshape(places.far, -1, D)
    total = lax.dynamic_index_in_dim(parts, places.rest, 0, keepdims=False).astype(F32)
    sent = []
    for step in range(1, places.far):
        part = lax.dynamic_index_in_dim(parts, (places.rest + step) % places.far, 0, keepdims=False)
        sent.append(places.turn(part, step, axis, base))
    for part in (yield sent):
        total = total + part.astype(F32)
    yield total.astype(BF16)


def gather_rest_first(places, share):
    parts = jnp.stack([share] + (yield [places.turn(share, step) for step in range(1, places.far)]))
    yield jnp.stack([parts, (yield places.swap(parts, 2))])


def gather_near_first(places, share):
    parts = jnp.stack([share, (yield places.swap(share, 2))])
    yield jnp.stack([parts] + (yield [places.turn(parts, step) for step in range(1, places.far)]))


def vector_steps(places, value):
    value = value + (yield places.swap(value, 1))
    value = value + (yield places.swap(value, 2))
    total = value
    for arrived in (yield [places.turn(value, step) for step in range(1, places.far)]):
        total = total + arrived
    cross = total[V_GAINC : V_SHIFTC + 1]
    yield total, cross + (yield lax.ppermute(cross, SECTION, [(0, 1), (1, 0)]))


def place_kernel(far, groups, near_first, where_ref, *refs):
    outs = refs[2 * len(groups) :]
    core, near, rest = where_ref[0], where_ref[1], where_ref[2]
    for index, blocks in enumerate(groups):
        own_ref, other_ref = refs[2 * index : 2 * index + 2]
        rows = own_ref.shape[2]
        for share in range(4 * far):
            c, n, q = share // (2 * far), share // far % 2, share % far
            out, col = blocks[share * rows // D]
            start = share * rows % D
            step = lax.rem(rest - q + far, far)
            which = lax.rem(near + n, 2)
            at = (step, which) if near_first[index] else (which, step)
            target = (out, slice(start, start + rows), slice(col * D, (col + 1) * D))

            @pl.when(core == c)
            def _(target=target, source=own_ref, at=at):
                outs[target[0]][target[1], target[2]] = source[at].astype(F32)

            @pl.when(core != c)
            def _(target=target, source=other_ref, at=at):
                outs[target[0]][target[1], target[2]] = source[at].astype(F32)


def put_in_place(places, gathered, groups, widths):
    where = jnp.stack([places.core, places.near, places.rest]).astype(jnp.int32)
    flat = [item for pair in gathered for item in pair]
    return pl.pallas_call(
        functools.partial(place_kernel, places.far, groups, (False, True)),
        out_shape=[shape(D, width, dtype=F32) for width in widths],
        in_specs=[smem_spec()] + [vmem_spec()] * len(flat),
        out_specs=[vmem_spec()] * len(widths),
        compiler_params=PARAMS,
        name="place_sums",
    )(where, *flat)


def widen_kernel(up_in, down_in, up_out, down_out):
    up_out[...] = up_in[...].astype(F32)
    down_out[...] = down_in[...].astype(F32)


def widen(grads):
    count = FF // D
    return pl.pallas_call(
        widen_kernel,
        grid=(count,),
        out_shape=[shape(D, FF, dtype=F32), shape(FF, D, dtype=F32)],
        in_specs=[pl.BlockSpec((D, D), lambda i: (i, 0)), pl.BlockSpec((D, D), lambda i: (count + i, 0))],
        out_specs=[pl.BlockSpec((D, D), lambda i: (0, i)), pl.BlockSpec((D, D), lambda i: (i, 0))],
        compiler_params=PARAMS,
        name="widen",
    )(grads, grads)


def shards(
    inputs, cotangent, lengths, running, norm_gain, norm_shift, qkv_weight, out_weight, up_weight, up_bias,
    down_weight, down_bias, halt_weight, halt_bias, cross_gain, cross_shift, cross_query, cross_kv, cross_out,
):
    decoding = on_decoder()
    places = Places()
    rows = range(inputs.shape[1])
    vectors = (norm_gain, norm_shift, lengths, running, up_bias, down_bias, halt_weight, halt_bias)
    crosses = (cross_gain[None], cross_shift[None])
    firsts, received = [], []
    for row in rows:
        arrays = (
            inputs, *vectors, *crosses, qkv_weight, out_weight, up_weight, down_weight, cross_query,
            *([firsts[row - 1][12]] if row else []),
        )
        firsts.append(call_a(row, lengths, running, arrays))
        received.append(lax.ppermute(firsts[row][1], SECTION, [(0, 1)]))
    result = firsts[-1][12]
    middles, returned = [], []
    for row in rows:
        _, out, after = firsts[row][:3]
        arrays = (
            inputs, cotangent, *vectors, up_weight, down_weight, cross_kv, cross_out, received[row], out, after, result,
        )
        middles.append(call_b(row, lengths, running, arrays))
        result = middles[row][12]
        returned.append(lax.ppermute(middles[row][9], SECTION, [(1, 0)]))

    def both(items, index):
        return [item[index] for item in items]

    feeds = []
    for row in rows:
        _, _, after, _, _, _, _, n2, act, slope, change, _, _ = firsts[row]
        arrays = (
            inputs, cotangent, norm_gain, running, halt_weight, halt_bias, up_weight, down_weight, returned[row], after,
            slope, change, n2, act, *middles[row][1:5], crosses[0], cross_query, middles[row][7], middles[row][10],
            *([feeds[row - 1][3]] if row else []),
        )
        feeds.append(call_c(row, running, arrays))
    feed_sum = lax.psum(feeds[-1][3], DP)
    vec_before = sum(both(middles, 0)) + sum(both(feeds, 0))
    groups = [[(0, 0), (0, 1), (0, 2), (1, 0)], [(2, 0), (3, 0), (3, 1), (4, 0)]]
    widths = [3 * D, D, D, 2 * D, D]

    def tail(operands):
        firsts, middles, feeds, received, vec = operands
        cross_grads = call_w(
            [
                (both(firsts, 11), both(feeds, 4)),
                (received, both(middles, 8)),
                (both(middles, 5), both(middles, 6)),
            ]
        )
        crosses = scatter_steps(places, *cross_grads, (SECTION, DP), places.count)
        cross, grad_after = lax.optimization_barrier((next(crosses), both(feeds, 1)))
        cross = crosses.send(cross)
        kinds = [both(firsts, 3), both(firsts, 5), both(firsts, 6), both(firsts, 4), grad_after, both(feeds, 2)]
        kinds = [item for kind in (*kinds, both(middles, 11)) for item in kind]
        vec_self, *self_grads, input_grad = call_s(
            len(rows), lengths, (inputs, norm_gain, lengths, qkv_weight, out_weight, *kinds)
        )
        cross, self_grads = lax.optimization_barrier((cross, self_grads))
        selfs, small = scatter_steps(places, *self_grads), vector_steps(places, vec + vec_self)
        own, vec = lax.optimization_barrier((next(selfs), next(small)))
        sent = selfs.send(own), small.send(vec), crosses.send(cross)
        own, vec, cross = lax.optimization_barrier(sent)
        cross = crosses.send(cross)
        sent = selfs.send(own), small.send(vec), lax.ppermute(cross, SECTION, [(1, 0)])
        own, vec, moved_cross = lax.optimization_barrier(sent)
        gathers = [
            gather_rest_first(places, selfs.send(own)),
            gather_near_first(places, jnp.where(decoding, cross, moved_cross)),
        ]
        sent = *(next(gather) for gather in gathers), small.send(vec)
        own, cross, vec = lax.optimization_barrier(sent)
        sent = gathers[0].send(own), gathers[1].send(cross)
        vec, cross_vec = small.send(vec)
        gathered = [gather.send(item) for gather, item in zip(gathers, lax.optimization_barrier(sent))]
        finals = (
            jnp.stack([vec[V_GAIN1], vec[V_GAIN2]])[None],
            jnp.stack([vec[V_SHIFT1], vec[V_SHIFT2]])[None],
            vec[V_UPB : V_UPB + 4].reshape(1, FF),
            vec[V_DOWNB][None],
            vec[V_HW][None],
            vec[V_HB, :1],
            cross_vec[0],
            cross_vec[1],
        )
        stats = [jnp.where(decoding, middles[row][0], firsts[row][0])[V_RMS, :2] for row in rows]
        row_rms = jnp.sqrt(jnp.stack(stats)[None] / (L * D) + 1e-06)
        return *gathered, *finals, row_rms, input_grad

    def nothing(operands):
        parts = jnp.zeros((2, places.far, 4 * D // places.count, D), BF16)
        swapped = parts.reshape(places.far, 2, -1, D)
        pair, one, wide = (jnp.zeros((1, size, D), F32) for size in (2, 1, 4))
        finals = (pair, pair, wide.reshape(1, FF), one[0], one[0], one[0, 0, :1], one[0, 0], one[0, 0])
        return parts, swapped, *finals, jnp.zeros(inputs.shape[:2] + (2,), F32), jnp.zeros(inputs.shape, F32)

    *gathered, gain, shift, up_b, down_b, halt_w, halt_b, cross_g, cross_s, row_rms, input_grad = lax.cond(
        lengths[0, 0, 0] > 0, tail, nothing, (firsts, middles, feeds, received, vec_before)
    )
    gathered = [(parts, places.swap(parts, 1)) for parts in gathered]
    qkv_sum, out_sum, query_sum, kv_sum, cross_out_sum = put_in_place(places, gathered, groups, widths)
    up_sum, down_sum = widen(feed_sum)
    return (
        result,
        input_grad,
        row_rms,
        gain,
        shift,
        qkv_sum[None],
        out_sum[None],
        up_sum[None],
        up_b,
        down_sum[None],
        down_b,
        halt_w,
        halt_b,
        cross_g,
        cross_s,
        query_sum,
        kv_sum,
        cross_out_sum,
    )


def solution(mesh):
    in_specs = (
        P(SECTION, DP, None, None),
        P(SECTION, DP, None, None),
        P(None, DP, None),
        P(SECTION, DP, None),
        P(SECTION, None, None),
        P(SECTION, None, None),
        P(SECTION, None, None),
        P(SECTION, None, None),
        P(SECTION, None, None),
        P(SECTION, None),
        P(SECTION, None, None),
        P(SECTION, None),
        P(SECTION, None),
        P(SECTION),
        P(),
        P(),
        P(),
        P(),
        P(),
    )
    out_specs = (
        P(SECTION, DP, None, None),
        P(SECTION, DP, None, None),
        P(SECTION, DP, None),
        P(SECTION, None, None),
        P(SECTION, None, None),
        P(SECTION, None, None),
        P(SECTION, None, None),
        P(SECTION, None, None),
        P(SECTION, None),
        P(SECTION, None, None),
        P(SECTION, None),
        P(SECTION, None),
        P(SECTION),
        P(),
        P(),
        P(),
        P(),
        P(),
    )
    return jax.shard_map(shards, mesh=mesh, in_specs=in_specs, out_specs=out_specs, check_vma=False)
```

```python
import functools

import jax
import jax.numpy as jnp
from jax import lax
from jax.experimental import pallas as pl
from jax.experimental.pallas import tpu as pltpu
from jax.sharding import PartitionSpec as P

L = 512
D = 512
FF = 2048
HEADS = 8
SECTION, DP = "section", "dp"
HEAD = D // HEADS
GROUP = 256
PER = GROUP // HEAD
RC = 512
EPS = 1e-05
MASKED = -1000000000.0
GELU_A = 0.7978845608028654
GELU_B = 0.044715
F32 = jnp.float32
BF16 = jnp.bfloat16

V_GAIN2, V_SHIFT2, V_UPB, V_DOWNB, V_HW, V_HB = 0, 1, 2, 6, 7, 8
V_GAINC, V_SHIFTC, V_GAIN1, V_SHIFT1, V_RMS = 9, 10, 11, 12, 13
V_ROWS = 16


def nn(left, right):
    return lax.dot_general(left, right, (((1,), (0,)), ((), ())), preferred_element_type=F32)


def nt(left, right):
    return lax.dot_general(left, right, (((1,), (1,)), ((), ())), preferred_element_type=F32)


def tn(left, right):
    return lax.dot_general(left, right, (((0,), (0,)), ((), ())), preferred_element_type=F32)


def col_sum(value):
    return jnp.sum(value, axis=0, keepdims=True)


def row_mean(value):
    return jnp.mean(value, axis=1, keepdims=True)


def normalize(value):
    centered = value - row_mean(value)
    scale = lax.rsqrt(row_mean(centered * centered) + EPS)
    return centered * scale, scale


def norm_input_grad(grad, gain, xhat, scale):
    scaled = grad * gain
    return scale * (scaled - row_mean(scaled) - xhat * row_mean(scaled * xhat))


def each(count, size, body):
    def step(index, carry):
        body(index, pl.ds(pl.multiple_of(index * size, size), size))
        return carry

    lax.fori_loop(0, count, step, 0)


def each_apart(count, size, body):
    for index in range(count):
        body(index, pl.ds(index * size, size))


def for_rows(body):
    for first in range(0, L, RC):
        body(slice(first, first + RC))


def head_masks():
    lane = lax.broadcasted_iota(jnp.int32, (1, GROUP), 1)
    return [(lane // HEAD) == place for place in range(PER)]


def keep(mask, value):
    return jnp.where(mask, value, jnp.zeros_like(value))


def segments(len_ref, side, row, shape, dim, first):
    place = lax.broadcasted_iota(jnp.int32, shape, dim) + first
    total = jnp.int32(0)
    found = jnp.zeros(shape, jnp.int32)
    for index in range(len_ref.shape[2]):
        total = total + len_ref[side, row, index]
        found = found + (place >= total).astype(jnp.int32)
    return found


def write_bias(bias_ref, len_ref, row, row_side, col_side, causal_sign, causal):
    across = segments(len_ref, col_side, row, (1, L), 1, 0)

    def some(part):
        allowed = segments(len_ref, row_side, row, (RC, 1), 0, part.start) == across
        if causal is not None:
            row_place = lax.broadcasted_iota(jnp.int32, (RC, L), 0) + part.start
            col_place = lax.broadcasted_iota(jnp.int32, (RC, L), 1)
            ordered = (row_place - col_place) * causal_sign >= 0
            allowed = allowed & (ordered | jnp.logical_not(causal))
        bias_ref[part, :] = jnp.where(allowed, 0.0, MASKED)

    for_rows(some)


def attend_forward(queries, q0, keys, k0, values, v0, bias_ref, out_ref, stat_ref, column_ref, loop=each):
    masks = head_masks()
    lane = lax.broadcasted_iota(jnp.int32, (1, 128), 1)
    column_ref[...] = jnp.zeros_like(column_ref)

    def of_group(index, cols):
        own_q, own_k, own_v = (ref[:, moved(cols, first)] for ref, first in ((queries, q0), (keys, k0), (values, v0)))
        stats = column_ref[...]
        weights = []
        for place in range(PER):
            scores = nt(keep(masks[place], own_q), own_k) + bias_ref[...]
            top = jnp.max(scores, axis=1, keepdims=True)
            expanded = jnp.exp(scores - top)
            total = jnp.sum(expanded, axis=1, keepdims=True)
            weights.append((expanded * (1.0 / total)).astype(BF16))
            stats = jnp.where(lane == index * PER + place, top + jnp.log(total), stats)
        column_ref[...] = stats
        stacked = jnp.concatenate([keep(mask, own_v) for mask in masks], axis=0)
        out_ref[:, cols] = nn(jnp.concatenate(weights, axis=1), stacked).astype(BF16)

    loop(D // GROUP, GROUP, of_group)
    turned = column_ref[...].T
    for head in range(HEADS):
        stat_ref[head] = turned[head : head + 1, :]


def moved(cols, first):
    place = cols.start + first
    return pl.ds(place if isinstance(place, int) else pl.multiple_of(place, GROUP), cols.size)


def attend_backward(
    queries, q0, keys, k0, values, v0, grads, bias_ref, stat_ref,
    turned_ref, dq_ref, scores_ref, drops_ref, probs_ref, slants_ref, target, t0,
):
    masks = head_masks()

    def of_group(index, cols):
        own_q, own_k, own_v = (ref[:, moved(cols, first)] for ref, first in ((queries, q0), (keys, k0), (values, v0)))
        own_g = grads[:, cols]
        turned_ref[cols, :] = own_k.T
        for place in range(PER):
            head, slot = index * PER + place, place % 2
            rows, across = pl.ds(pl.multiple_of(head * HEAD, HEAD), HEAD), slice(place * L, (place + 1) * L)
            scores_ref[slot] = nt(keep(masks[place], own_k), own_q)
            drops_ref[slot] = nt(keep(masks[place], own_v), own_g)
            log_total, inner = stat_ref[head], jnp.zeros((8, L), F32)
            for part in range(0, L, 64):
                lines = slice(part, part + 64)
                probs = jnp.exp(scores_ref[slot, lines, :] + bias_ref[lines, :] - log_total)
                scores_ref[slot, lines, :] = probs
                probs_ref[lines, across] = probs.astype(BF16)
                inner += jnp.sum((probs * drops_ref[slot, lines, :]).reshape(8, 8, L), axis=0)
            inner = col_sum(inner)
            for part in range(0, L, 64):
                lines = slice(part, part + 64)
                slant = scores_ref[slot, lines, :] * (drops_ref[slot, lines, :] - inner)
                slants_ref[lines, across] = slant.astype(BF16)
            dq_ref[rows, :] = nn(turned_ref[rows, :], slants_ref[:, across])
        stacked = jnp.concatenate([keep(mask, own_q) for mask in masks], axis=0)
        target[:, moved(cols, t0)] = nn(slants_ref[...], stacked).astype(BF16)
        stacked = jnp.concatenate([keep(mask, own_g) for mask in masks], axis=0)
        target[:, moved(cols, t0 + D)] = nn(probs_ref[...], stacked).astype(BF16)

    each(D // GROUP, GROUP, of_group)


def gelu_parts(pre):
    square = pre * pre
    half = 0.5 + 0.5 * jnp.tanh(pre * (GELU_A + GELU_A * GELU_B * square))
    slope = half + half * (1.0 - half) * pre * (2.0 * GELU_A + 6.0 * GELU_A * GELU_B * square)
    return pre * half, slope


def feed_forward(
    after_ref, norm_gain, norm_shift, w_up, up_bias, w_down, down_bias, n2_ref, act_ref, slope_ref, total_ref, loop=each
):
    after = after_ref[...]
    n2_ref[...] = (normalize(after)[0] * norm_gain[1:2] + norm_shift[1:2]).astype(BF16)
    total_ref[...] = after + down_bias[...]

    def of_block(_, cols):
        activated, slope = gelu_parts(nn(n2_ref[...], w_up[:, cols]) + up_bias[:, cols])
        activated = activated.astype(BF16)
        act_ref[:, cols] = activated
        if slope_ref is not None:
            slope_ref[:, cols] = slope.astype(BF16)
        total_ref[...] += nn(activated, w_down[cols, :])

    loop(FF // D, D, of_block)


def feed_slope(gb_ref, w_down, slope_ref, gp_ref, bias_ref, w_up=None, back_ref=None, loop=each):
    def of_block(_, cols):
        value = (nt(gb_ref[...], w_down[cols, :]) * slope_ref[:, cols].astype(F32)).astype(BF16)
        gp_ref[:, cols] = value
        bias_ref[:, cols] = col_sum(value.astype(F32))
        if w_up is not None:
            back_ref[...] += nt(value, w_up[:, cols])

    loop(FF // D, D, of_block)


def add_up_bias(vec, bias_ref):
    for index, cols in enumerate(blocks_of(FF)):
        add_row(vec, V_UPB + index, bias_ref[:, cols])


def feed_input_grad(after_ref, back, grad_ref, gb_ref, norm_gain, vec, part):
    add_row(vec, V_DOWNB, col_sum(gb_ref[part, :].astype(F32)))
    xhat, scale = normalize(after_ref[part, :])
    add_row(vec, V_GAIN2, col_sum(back * xhat))
    add_row(vec, V_SHIFT2, col_sum(back))
    return grad_ref[part, :] + norm_input_grad(back, norm_gain[1:2], xhat, scale)


def write_running(column_ref, run_ref, row):
    line = run_ref[0, row : row + 1, :].astype(F32)
    column_ref[...] = jnp.broadcast_to(line, (128, L)).T


def halting_share(current, run, halt_weight, halt_bias):
    logit = jnp.sum(current * halt_weight[...], axis=1, keepdims=True) + halt_bias[0]
    rate = jax.nn.sigmoid(logit)
    return run * rate, rate


def halting_backward(grad, change, current, share, rate, run, halt_weight, vec_ref):
    logit_grad = (
        run * jnp.sum(grad * change, axis=1, keepdims=True) * rate * (1.0 - rate)
    )
    vec_ref[V_HW : V_HW + 1, :] += col_sum(logit_grad * current)
    vec_ref[V_HB : V_HB + 1, :] += jnp.broadcast_to(col_sum(logit_grad), (1, D))
    return share * grad, (1.0 - share) * grad + logit_grad * halt_weight[...]


def write_rms(vec_ref, total_ref):
    lane = lax.broadcasted_iota(jnp.int32, (1, D), 1)
    vec_ref[V_RMS : V_RMS + 1, :] = jnp.where(lane == 0, total_ref[0], total_ref[1])


class Copies:
    def __init__(self, sems, **pairs):
        for index, (name, (source, target)) in enumerate(pairs.items()):
            setattr(self, name, pltpu.make_async_copy(source, target, sems.at[index]))


def start(*copies):
    for copy in copies:
        copy.start()


def wait(*copies):
    for copy in copies:
        copy.wait()


def blocks_of(width):
    return [slice(place, place + D) for place in range(0, width, D)]


def on_decoder():
    return lax.axis_index(SECTION) == 1


def halves_out(held, mine_hbm, other_hbm, sems):
    half = held.shape[0] // 2
    core = lax.rem(lax.axis_index(DP), 2)
    return [
        pltpu.make_async_copy(held.at[pl.ds(pl.multiple_of(place * half, half), half)], target, sems.at[index])
        for index, (place, target) in enumerate(((core, mine_hbm), (1 - core, other_hbm)))
    ]


def add_row(vec, row, value):
    vec[row : row + 1, :] += value


def kernel_a(
    row,
    x_hbm, ng_hbm, ns_hbm, len_hbm, run_hbm, ub_hbm, db_hbm, hw_hbm, hb_hbm, cg_hbm, cs_hbm,
    wqkv_hbm, wout_hbm, wup_hbm, wdn_hbm, wcq_hbm,
    *rest,
):
    (
        vec_hbm, out_hbm, after_hbm, packed_hbm, att_hbm, stat_hbm, normed_hbm, n2_hbm, act_hbm, change_hbm,
        normed2_hbm, result_hbm, x, ng, ns, lens, run, ub, db, hw, hb, cg, cs, wqkv, wout, wup, wdn, wcq,
        vec, out, after, packed, att, stat, normed, n2, act, change, normed2, bias, column, total, sems,
    ) = rest[row > 0 :]
    decoding = on_decoder()
    encoding = jnp.logical_not(decoding)
    c = Copies(
        sems,
        x=(x_hbm.at[0, row], x), ng=(ng_hbm.at[0], ng), ns=(ns_hbm.at[0], ns), lens=(len_hbm, lens), run=(run_hbm, run),
        ub=(ub_hbm, ub), db=(db_hbm, db), hw=(hw_hbm, hw), hb=(hb_hbm, hb), cg=(cg_hbm, cg), cs=(cs_hbm, cs),
        wqkv=(wqkv_hbm.at[0], wqkv), wout=(wout_hbm.at[0], wout), wup=(wup_hbm.at[0], wup), wdn=(wdn_hbm.at[0], wdn),
        wcq=(wcq_hbm, wcq),
        vec=(vec, vec_hbm), out=(out, out_hbm), after=(after, after_hbm), packed=(packed, packed_hbm),
        att=(att, att_hbm), stat=(stat, stat_hbm), normed=(normed, normed_hbm), normed2=(normed2, normed2_hbm),
        n2=(n2, n2_hbm), act=(act, act_hbm), change=(change, change_hbm),
        result=(out, result_hbm.at[0, row]),
    )
    start(c.x, c.ng, c.ns, c.lens, c.wqkv, c.wout)

    @pl.when(encoding)
    def _():
        start(c.run, c.ub, c.db, c.hw, c.hb, c.wup, c.wdn)

    @pl.when(decoding)
    def _():
        start(c.cg, c.cs, c.wcq)

    wait(c.lens)
    side = decoding.astype(jnp.int32)
    write_bias(bias, lens, row, side, side, 1, decoding)
    wait(c.x, c.ng, c.ns)

    @for_rows
    def _(part):
        normed[part, :] = (normalize(x[part, :].astype(F32))[0] * ng[0:1] + ns[0:1]).astype(BF16)

    start(c.normed)
    wait(c.wqkv)
    for index, cols in enumerate(blocks_of(3 * D)):
        value = nn(normed[...], wqkv[:, cols]).astype(BF16)
        if index == 0:
            value = (value.astype(F32) * HEAD**-0.5).astype(BF16)
        packed[:, cols] = value
    start(c.packed)
    attend_forward(packed, 0, packed, D, packed, 2 * D, bias, att, stat, column, each_apart)
    start(c.att, c.stat)
    wait(c.wout)
    after[...] = x[...].astype(F32) + nn(att[...], wout[...])
    start(c.after)

    @pl.when(encoding)
    def _():
        wait(c.run, c.ub, c.db, c.hw, c.hb, c.wup, c.wdn)
        write_running(column, run, row)
        feed_forward(after, ng, ns, wup, ub, wdn, db, n2, act, None, bias)
        start(c.n2, c.act)
        total[0] = 0.0
        total[1] = 0.0

        @for_rows
        def _(part):
            updated = bias[part, :]
            current = x[part, :].astype(F32)
            share, _ = halting_share(current, column[part, :1], hw, hb)
            moved = updated - current
            change[part, :] = moved
            moved = share * moved
            result = current + moved
            out[part, :] = result.astype(BF16)
            total[0] += jnp.sum(result * result)
            total[1] += jnp.sum(moved * moved)

        start(c.out, c.change, c.result)
        vec[...] = jnp.zeros_like(vec)
        write_rms(vec, total)
        start(c.vec)
        wait(c.n2, c.act, c.change, c.vec, c.result)

    @pl.when(decoding)
    def _():
        wait(c.cg, c.cs, c.wcq)

        @for_rows
        def _(part):
            normed2[part, :] = (normalize(after[part, :])[0] * cg[...] + cs[...]).astype(BF16)

        value = nn(normed2[...], wcq[...]).astype(BF16)
        out[...] = (value.astype(F32) * HEAD**-0.5).astype(BF16)
        start(c.out, c.normed2)
        vec[...] = jnp.zeros_like(vec)
        start(c.vec)
        wait(c.normed2, c.vec)

    wait(c.normed, c.packed, c.att, c.stat, c.after, c.out)


def kernel_b(
    row,
    x_hbm, cot_hbm, ng_hbm, ns_hbm, len_hbm, run_hbm, ub_hbm, db_hbm, hw_hbm, hb_hbm,
    wup_hbm, wdn_hbm, wkv_hbm, wco_hbm, mem_hbm, cq_hbm, after_hbm, n2e_hbm, _,
    vec_hbm, n2_hbm, act_hbm, gb_hbm, gp_hbm, att_hbm, gc_hbm, dq_hbm, gkv_hbm, back_hbm, ga_hbm, gx_hbm, result_hbm, slope_hbm,
    x, cot, ng, ns, lens, run, ub, db, hw, hb, wup, wdn, wkv, wco, mem, cq, after,
    vec, n2, act, gb, gp, att, gc, dqb, gkv, back, gaf, gx,
    result, kv, slope, across, gatt, ubg, bias, bias2, stat, column, turned, dq, scores, drops, probs, slants, total, sems,
):
    c = Copies(
        sems,
        x=(x_hbm.at[0, row], x), cot=(cot_hbm.at[0, row], cot), ng=(ng_hbm.at[0], ng), ns=(ns_hbm.at[0], ns),
        lens=(len_hbm, lens), run=(run_hbm, run), ub=(ub_hbm, ub), db=(db_hbm, db), hw=(hw_hbm, hw), hb=(hb_hbm, hb),
        wup=(wup_hbm.at[0], wup), wdn=(wdn_hbm.at[0], wdn), wkv=(wkv_hbm, wkv),
        wco=(wco_hbm, wco), mem=(mem_hbm, mem), cq=(cq_hbm, cq), after=(after_hbm, after),
        vec=(vec, vec_hbm), n2=(n2, n2_hbm), act=(act, act_hbm), gb=(gb, gb_hbm), gp=(gp, gp_hbm), att=(att, att_hbm),
        gc=(gc, gc_hbm), dq=(dqb, dq_hbm), gkv=(gkv, gkv_hbm), back=(back, back_hbm), result=(result, result_hbm.at[0, row]),
        ga=(gaf, ga_hbm), gx=(gx, gx_hbm), n2e=(n2e_hbm, n2), slope=(slope, slope_hbm),
    )
    decoding = on_decoder()

    @pl.when(jnp.logical_not(decoding))
    def _():
        start(c.n2e, c.wup, c.ub)
        vec[...] = jnp.zeros_like(vec)
        start(c.vec)
        wait(c.n2e, c.wup, c.ub)

        def of_block(_, cols):
            slope[:, cols] = gelu_parts(nn(n2[...], wup[:, cols]) + ub[:, cols])[1].astype(BF16)

        each(FF // D, D, of_block)
        start(c.slope)
        wait(c.slope)

    @pl.when(decoding)
    def _():
        start(c.mem, c.wkv, c.lens, c.cq, c.wco, c.after, c.ng, c.ns, c.ub, c.db, c.wup, c.wdn)
        start(c.x, c.cot, c.run, c.hw, c.hb)
        vec[...] = jnp.zeros_like(vec)
        wait(c.lens)
        write_bias(bias, lens, row, 1, 0, 1, None)
        write_bias(bias2, lens, row, 0, 1, 1, None)
        wait(c.mem, c.wkv)
        for cols in blocks_of(2 * D):
            kv[:, cols] = nn(mem[...], wkv[:, cols]).astype(BF16)
        wait(c.cq)
        attend_forward(cq, 0, kv, 0, kv, D, bias, att, stat, column, each_apart)
        start(c.att)
        wait(c.after, c.wco)
        across[...] = after[...] + nn(att[...], wco[...])
        wait(c.ng, c.ns, c.ub, c.db, c.wup, c.wdn, c.x, c.cot, c.run, c.hw, c.hb)
        write_running(column, run, row)
        feed_forward(across, ng, ns, wup, ub, wdn, db, n2, act, slope, dq, each_apart)
        start(c.n2, c.act)
        total[0] = 0.0
        total[1] = 0.0

        @for_rows
        def _(part):
            updated = dq[part, :]
            current = x[part, :].astype(F32)
            share, rate = halting_share(current, column[part, :1], hw, hb)
            moved = updated - current
            grad, own = halting_backward(
                cot[part, :].astype(F32), moved, current, share, rate, column[part, :1], hw, vec
            )
            gx[part, :] = own
            moved = share * moved
            value = current + moved
            result[part, :] = value.astype(BF16)
            total[0] += jnp.sum(value * value)
            total[1] += jnp.sum(moved * moved)
            gaf[part, :] = grad
            gb[part, :] = grad.astype(BF16)

        start(c.gb, c.result, c.gx)

        dq[...] = jnp.zeros_like(dq)
        feed_slope(gb, wdn, slope, gp, ubg, wup, dq, each_apart)
        start(c.gp)
        add_up_bias(vec, ubg)

        @for_rows
        def _(part):
            grad = feed_input_grad(across, dq[part, :], gaf, gb, ng, vec, part)
            gaf[part, :] = grad
            gc[part, :] = grad.astype(BF16)

        gatt[...] = nt(gc[...], wco[...]).astype(BF16)
        start(c.gc, c.ga)
        write_rms(vec, total)
        start(c.vec)
        attend_backward(
            cq, 0, kv, 0, kv, D, gatt, bias2, stat, turned, dq, scores, drops, probs, slants, gkv, 0
        )
        start(c.gkv)
        dqb[...] = (dq[...] * HEAD**-0.5).astype(BF16)
        start(c.dq)
        back[...] = (nt(gkv[:, 0:D], wkv[:, 0:D]) + nt(gkv[:, D:], wkv[:, D:])).astype(BF16)
        start(c.back)
        wait(c.att, c.n2, c.act, c.gb, c.gp, c.gc, c.result, c.gx, c.gkv, c.dq, c.back, c.ga)

    wait(c.vec)


def kernel_c(
    row,
    x_hbm, cot_hbm, ng_hbm, run_hbm, hw_hbm, hb_hbm, wup_hbm, wdn_hbm, back_hbm, after_hbm, slope_hbm, change_hbm,
    n2e_hbm, acte_hbm, n2_hbm, act_hbm, gb_hbm, gp_hbm, cg_hbm, wcq_hbm, dq_hbm, gad_hbm, *rest,
):
    prior_hbm, rest = (rest[0], rest[1:]) if row else (None, rest)
    vec_hbm, ga_hbm, gx_hbm, grads_hbm, gq_hbm = rest[:5]
    (
        x, cot, ng, run, hw, hb, wup, wdn, back, after, slope, change, n2, act, cg, wcq, dq, vec, gaf, gx, gb, gp, grads, gq,
        column, column32, turned, ubg, sems,
    ) = rest[5:]
    decoding = on_decoder()
    encoding = jnp.logical_not(decoding)
    c = Copies(
        sems,
        x=(x_hbm.at[0, row], x), cot=(cot_hbm.at[0, row], cot), ng=(ng_hbm.at[0], ng), run=(run_hbm, run),
        hw=(hw_hbm, hw), hb=(hb_hbm, hb), wup=(wup_hbm.at[0], wup), wdn=(wdn_hbm.at[0], wdn), back=(back_hbm, back),
        after=(after_hbm, after), slope=(slope_hbm, slope), change=(change_hbm, change), n2e=(n2e_hbm, n2),
        acte=(acte_hbm, act), n2=(n2_hbm, n2), act=(act_hbm, act), gb=(gb_hbm, gb), gp=(gp_hbm, gp),
        vec=(vec, vec_hbm), ga=(gaf, ga_hbm), gx=(gx, gx_hbm), grads=(grads, grads_hbm), cg=(cg_hbm, cg),
        wcq=(wcq_hbm, wcq), dq=(dq_hbm, dq), gad=(gad_hbm, gaf), gq=(gq, gq_hbm),
        **({"prior": (prior_hbm, grads)} if row else {}),
    )
    vec[...] = jnp.zeros_like(vec)

    @pl.when(encoding)
    def _():
        start(c.back, c.cot, c.x, c.change, c.run, c.hw, c.hb, c.wdn, c.slope, c.n2e, c.acte, c.wup, c.after, c.ng)
        if row:
            start(c.prior)
        wait(c.back, c.cot, c.x, c.change, c.run, c.hw, c.hb)
        write_running(column, run, row)

        @for_rows
        def _(part):
            grad = cot[part, :].astype(F32) + back[part, :].astype(F32)
            current = x[part, :].astype(F32)
            share, rate = halting_share(current, column[part, :1], hw, hb)
            grad, own = halting_backward(
                grad, change[part, :], current, share, rate, column[part, :1], hw, vec
            )
            gx[part, :] = own
            gaf[part, :] = grad
            gb[part, :] = grad.astype(BF16)

        start(c.gx)
        wait(c.wdn, c.slope)
        feed_slope(gb, wdn, slope, gp, ubg)
        add_up_bias(vec, ubg)
        wait(c.n2e, c.acte)

    @pl.when(decoding)
    def _():
        start(c.n2, c.gp, c.act, c.gb)
        if row:
            start(c.prior)
        start(c.dq, c.wcq, c.after, c.gad, c.cg)
        wait(c.n2, c.gp, c.act, c.gb)

    if row:
        wait(c.prior)
    turned[...] = n2[...].T

    def of_block(_, cols):
        add_block(grads, cols, nn(turned[...], gp[:, cols]), row)
        add_block(grads, pl.ds(FF + cols.start, D), tn(act[:, cols], gb[...]), row)

    each_apart(FF // D, D, of_block)
    start(c.grads)

    @pl.when(encoding)
    def _():
        wait(c.wup, c.after, c.ng)

        column32[...] = jnp.zeros_like(column32)

        def back_of(_, cols):
            column32[...] += nt(gp[:, cols], wup[:, cols])

        each(FF // D, D, back_of)

        @for_rows
        def _(part):
            gaf[part, :] = feed_input_grad(after, column32[part, :], gaf, gb, ng, vec, part)

        start(c.ga)
        wait(c.ga, c.gx)

    @pl.when(decoding)
    def _():
        wait(c.dq, c.wcq, c.after, c.gad, c.cg)
        gq[...] = dq[...].T
        start(c.gq)

        @for_rows
        def _(part):
            grad = nt(gq[part, :], wcq[...])
            xhat, scale = normalize(after[part, :])
            add_row(vec, V_GAINC, col_sum(grad * xhat))
            add_row(vec, V_SHIFTC, col_sum(grad))
            gaf[part, :] += norm_input_grad(grad, cg[...], xhat, scale)

        start(c.ga)
        wait(c.gq, c.ga)

    start(c.vec)
    wait(c.grads, c.vec)


def add_block(grads, rows, value, more):
    if more:
        value = value + grads[rows, :].astype(F32)
    grads[rows, :] = value.astype(BF16)


def kernel_s(count, x_hbm, ng_hbm, len_hbm, wqkv_hbm, wout_hbm, *rest):
    held = [rest[index * count : (index + 1) * count] for index in range(7)]
    vec_hbm, mine_hbm, other_hbm, grad_hbm = rest[7 * count : 7 * count + 4]
    (
        x, ng, lens, wqkv, wout, packed, stat, normed, att, gaf, gx, vec, grads, grad_out, sums, gs, gpack, gatt, bias,
        turned, dq, scores, drops, probs, slants, sems, row_sems, out_sems, half_sems,
    ) = rest[7 * count + 4 :]
    decoding = on_decoder()
    encoding = jnp.logical_not(decoding)
    c = Copies(
        sems,
        x=(x_hbm.at[0], x), ng=(ng_hbm.at[0], ng), lens=(len_hbm, lens), wqkv=(wqkv_hbm.at[0], wqkv),
        wout=(wout_hbm.at[0], wout), vec=(vec, vec_hbm),
    )
    halves = halves_out(grads, mine_hbm, other_hbm, half_sems)

    def of_row(row):
        places = (packed, stat, normed, att, gaf, gx, gx)
        return Copies(
            row_sems.at[row],
            **{
                name: (held[index][row], place.at[row])
                for index, (name, place) in enumerate(zip(("packed", "stat", "normed", "att", "ga", "gxe", "gxd"), places))
            },
        )

    lines = [of_row(row) for row in range(count)]
    start(c.lens, c.wout, lines[0].ga, lines[0].packed, lines[0].stat, lines[0].att, lines[0].normed, c.wqkv, c.x, c.ng)
    for line in lines[1:]:
        start(line.ga, line.packed, line.stat, line.att, line.normed)

    @pl.when(encoding)
    def _():
        start(*[line.gxe for line in lines])

    @pl.when(decoding)
    def _():
        start(*[line.gxd for line in lines])

    vec[...] = jnp.zeros_like(vec)
    sums[...] = jnp.zeros_like(sums)
    wait(c.lens, c.wout)
    side = decoding.astype(jnp.int32)

    def one_row(row, carry):
        for index in range(count):

            @pl.when(row == index)
            def _():
                wait(*[getattr(lines[index], name) for name in ("packed", "stat", "normed", "att", "ga")])

        write_bias(bias, lens, row, side, side, -1, decoding)
        gs[...] = gaf[row].astype(BF16)
        gatt[...] = nt(gs[...], wout[...]).astype(BF16)
        own = packed.at[row]
        attend_backward(
            own, 0, own, D, own, 2 * D, gatt, bias, stat.at[row], turned, dq, scores, drops, probs, slants, gpack, D
        )
        gpack[:, 0:D] = (dq[...] * HEAD**-0.5).astype(BF16).T
        sums[3 * D : 4 * D, :] += tn(att[row], gs[...])
        flipped = normed[row].T
        for cols in blocks_of(3 * D):
            sums[cols, :] += nn(flipped, gpack[:, cols])

        @pl.when(row == count - 1)
        def _():
            grads[...] = sums[...].astype(BF16)
            start(*halves)

        @pl.when(row == 0)
        def _():
            wait(c.wqkv, c.x, c.ng)

        for index in range(count):

            @pl.when((row == index) & encoding)
            def _():
                wait(lines[index].gxe)

            @pl.when((row == index) & decoding)
            def _():
                wait(lines[index].gxd)

        for index, cols in enumerate(blocks_of(3 * D)):
            value = nt(gpack[:, cols], wqkv[:, cols])
            grad = value if index == 0 else grad + value
        xhat, scale = normalize(x[row].astype(F32))
        add_row(vec, V_GAIN1, col_sum(grad * xhat))
        add_row(vec, V_SHIFT1, col_sum(grad))
        grad_out[row] = gaf[row] + gx[row] + norm_input_grad(grad, ng[0:1], xhat, scale)
        pltpu.make_async_copy(grad_out.at[row], grad_hbm.at[0, row], out_sems.at[row]).start()
        return carry

    lax.fori_loop(0, count, one_row, 0)
    start(c.vec)
    for row in range(count):
        pltpu.make_async_copy(grad_out.at[row], grad_hbm.at[0, row], out_sems.at[row]).wait()
    wait(*halves, c.vec)


def any_spec():
    return pl.BlockSpec(memory_space=pl.ANY)


def vmem_spec():
    return pl.BlockSpec(memory_space=pltpu.VMEM)


def smem_spec():
    return pl.BlockSpec(memory_space=pltpu.SMEM)


def shape(*dims, dtype=BF16):
    return jax.ShapeDtypeStruct(dims, dtype)


def scratch_of(shapes):
    return [pltpu.VMEM(item.shape, item.dtype) for item in shapes]


PARAMS = pltpu.CompilerParams(vmem_limit_bytes=63 * 1024 * 1024)


def made(dims, dtype=BF16):
    return pltpu.VMEM(dims, dtype)


def call(kernel, name, arrays, inputs, outs, extra, copies, aliases=None, unheld=()):
    return pl.pallas_call(
        kernel,
        out_shape=[shape(V_ROWS, D, dtype=F32)] + outs + list(unheld),
        in_specs=[any_spec()] * len(arrays),
        out_specs=[any_spec()] * (1 + len(outs) + len(unheld)),
        input_output_aliases=aliases or {},
        scratch_shapes=inputs
        + [made((V_ROWS, D), F32)]
        + scratch_of(outs)
        + extra
        + [pltpu.SemaphoreType.DMA((copies,))],
        compiler_params=PARAMS,
        name=name,
    )(*arrays)


VECTOR = made((1, D), F32)
PAIR = made((2, D), F32)
WIDE = made((1, FF), F32)
ROW = made((L, D))
ROW32 = made((L, D), F32)
WUP, WDN, WSQ = made((D, FF)), made((FF, D)), made((D, D))
STAT = made((HEADS, 1, L), F32)
COLUMN = made((L, 128), F32)
ONE = pltpu.SMEM((1,), F32)


def lens_of(arrays):
    return pltpu.SMEM(arrays.shape, arrays.dtype)


def call_a(row, lengths, running, arrays):
    outs = [
        shape(L, D), shape(L, D, dtype=F32), shape(L, 3 * D), shape(L, D), shape(HEADS, 1, L, dtype=F32), shape(L, D),
        shape(L, D), shape(L, FF), shape(L, D, dtype=F32), shape(L, D),
    ]
    inputs = [
        ROW, PAIR, PAIR, lens_of(lengths), made(running.shape, running.dtype), WIDE, VECTOR, VECTOR, ONE, VECTOR, VECTOR,
        made((D, 3 * D)), WSQ, WUP, WDN, WSQ,
    ]
    extra = [ROW32, COLUMN, pltpu.SMEM((2,), F32)]
    aliases = {len(arrays) - 1: 1 + len(outs)} if row else {}
    kernel = functools.partial(kernel_a, row)
    return call(kernel, "forward_a", arrays, inputs, outs, extra, 34, aliases, [shape(*arrays[0].shape)])


ATTEND_SCRATCH = [
    made((D, L)), ROW32, made((2, L, L), F32), made((2, L, L), F32), made((L, PER * L)), made((L, PER * L)),
]


def call_b(row, lengths, running, arrays):
    outs = [
        shape(L, D), shape(L, FF), shape(L, D), shape(L, FF), shape(L, D), shape(L, D), shape(D, L), shape(L, 2 * D),
        shape(L, D), shape(L, D, dtype=F32), shape(L, D, dtype=F32),
    ]
    inputs = [
        ROW, ROW, PAIR, PAIR, lens_of(lengths), made(running.shape, running.dtype), WIDE, VECTOR, VECTOR, ONE,
        WUP, WDN, made((D, 2 * D)), WSQ, ROW, ROW, ROW32,
    ]
    extra = [ROW, made((L, 2 * D)), made((L, FF)), ROW32, ROW, WIDE, ROW32, ROW32, STAT, COLUMN, *ATTEND_SCRATCH, pltpu.SMEM((2,), F32)]
    aliases = {len(arrays) - 1: 1 + len(outs)}
    kernel = functools.partial(kernel_b, row)
    unheld = [shape(*arrays[0].shape), shape(L, FF)]
    return call(kernel, "decoder_b", arrays, inputs, outs, extra, 32, aliases, unheld)


def call_c(row, running, arrays):
    outs = [shape(L, D, dtype=F32), shape(L, D, dtype=F32), shape(2 * FF, D), shape(L, D)]
    inputs = [
        ROW, ROW, PAIR, made(running.shape, running.dtype), VECTOR, ONE, WUP, WDN, ROW, ROW32, made((L, FF)), ROW32, ROW,
        made((L, FF)), VECTOR, WSQ, made((D, L)),
    ]
    held = scratch_of(outs)
    return pl.pallas_call(
        functools.partial(kernel_c, row),
        out_shape=[shape(V_ROWS, D, dtype=F32)] + outs,
        in_specs=[any_spec()] * len(arrays),
        out_specs=[any_spec()] * 5,
        scratch_shapes=inputs
        + [made((V_ROWS, D), F32), held[0], held[1], ROW, made((L, FF)), held[2], held[3], COLUMN, ROW32, made((D, L)), WIDE]
        + [pltpu.SemaphoreType.DMA((28,))],
        compiler_params=PARAMS,
        name="feed_backward",
    )(*arrays)


def call_s(count, lengths, arrays):
    def rows_of(dims, dtype=BF16):
        return made((count,) + dims, dtype)

    inputs = [
        rows_of((L, D)), PAIR, lens_of(lengths), made((D, 3 * D)), WSQ, rows_of((L, 3 * D)), rows_of((HEADS, 1, L), F32),
        rows_of((L, D)), rows_of((L, D)), rows_of((L, D), F32), rows_of((L, D), F32),
    ]
    extra = [rows_of((L, D), F32), made((4 * D, D), F32), ROW, made((L, 3 * D)), ROW, ROW32, *ATTEND_SCRATCH]
    return pl.pallas_call(
        functools.partial(kernel_s, count),
        out_shape=[shape(V_ROWS, D, dtype=F32)] + [shape(2 * D, D)] * 2 + [shape(*arrays[0].shape, dtype=F32)],
        in_specs=[any_spec()] * len(arrays),
        out_specs=[any_spec()] * 4,
        scratch_shapes=inputs
        + [made((V_ROWS, D), F32), made((4 * D, D))]
        + extra
        + [pltpu.SemaphoreType.DMA((7,)), pltpu.SemaphoreType.DMA((count, 7)), pltpu.SemaphoreType.DMA((count,))]
        + [pltpu.SemaphoreType.DMA((2,))],
        compiler_params=PARAMS,
        name="self_backward",
    )(*arrays)


def kernel_w(*refs):
    count = (len(refs) - 5) // 2
    sources, (mine_hbm, other_hbm), held = refs[:count], refs[count : count + 2], refs[count + 2 : -3]
    outs, sems, out_sems = refs[-3:]

    @pl.when(on_decoder())
    def _():
        copies = [pltpu.make_async_copy(sources[i], held[i], sems.at[i]) for i in range(count)]
        start(*copies)
        block, each = 0, count // 3
        for pair in range(3):
            mine = slice(pair * each, (pair + 1) * each)
            wait(*copies[mine])
            lefts, rights = held[mine][: each // 2], held[mine][each // 2 :]
            turned = [left[...].T for left in lefts]
            for cols in blocks_of(rights[0].shape[1]):
                value = nn(turned[0], rights[0][:, cols])
                for left, right in zip(turned[1:], rights[1:]):
                    value += nn(left, right[:, cols])
                outs[block * D : (block + 1) * D, :] = value.astype(BF16)
                block += 1
        copies = halves_out(outs, mine_hbm, other_hbm, out_sems)
        start(*copies)
        wait(*copies)


def call_w(pairs):
    flat = [item for lefts, rights in pairs for item in (*lefts, *rights)]
    return pl.pallas_call(
        kernel_w,
        out_shape=[shape(2 * D, D)] * 2,
        in_specs=[any_spec()] * len(flat),
        out_specs=[any_spec()] * 2,
        scratch_shapes=scratch_of(flat)
        + [made((4 * D, D)), pltpu.SemaphoreType.DMA((len(flat),)), pltpu.SemaphoreType.DMA((2,))],
        compiler_params=PARAMS,
        name="cross_weights",
    )(*flat)


class Places:
    def __init__(self):
        self.count = lax.axis_size(DP)
        self.far = self.count // 4
        me = lax.axis_index(DP)
        self.core, self.near, self.rest = me % 2, (me // 2) % 2, me // 4

    def swap(self, value, bit, axis=DP, base=0):
        pairs = [(base + i, base + (i ^ bit)) for i in range(self.count)]
        return lax.ppermute(value, axis, pairs)

    def turn(self, value, steps, axis=DP, base=0):
        pairs = [(base + i, base + (i + 4 * steps) % self.count) for i in range(self.count)]
        return lax.ppermute(value, axis, pairs)


def halves(value, bit):
    half = value.shape[0] // 2
    mine = lax.dynamic_slice_in_dim(value, bit * half, half, 0)
    other = lax.dynamic_slice_in_dim(value, (1 - bit) * half, half, 0)
    return mine, other


def plus(left, right):
    return (left.astype(F32) + right.astype(F32)).astype(BF16)


def scatter_steps(places, mine, other, axis=DP, base=0):
    value = plus(mine, (yield places.swap(other, 1, axis, base)))
    mine, other = halves(value, places.near)
    value = plus(mine, (yield places.swap(other, 2, axis, base)))
    parts = value.reshape(places.far, -1, D)
    total = lax.dynamic_index_in_dim(parts, places.rest, 0, keepdims=False).astype(F32)
    sent = []
    for step in range(1, places.far):
        part = lax.dynamic_index_in_dim(parts, (places.rest + step) % places.far, 0, keepdims=False)
        sent.append(places.turn(part, step, axis, base))
    for part in (yield sent):
        total = total + part.astype(F32)
    yield total.astype(BF16)


def gather_rest_first(places, share):
    parts = jnp.stack([share] + (yield [places.turn(share, step) for step in range(1, places.far)]))
    yield jnp.stack([parts, (yield places.swap(parts, 2))])


def gather_near_first(places, share):
    parts = jnp.stack([share, (yield places.swap(share, 2))])
    yield jnp.stack([parts] + (yield [places.turn(parts, step) for step in range(1, places.far)]))


def vector_steps(places, value):
    value = value + (yield places.swap(value, 1))
    value = value + (yield places.swap(value, 2))
    total = value
    for arrived in (yield [places.turn(value, step) for step in range(1, places.far)]):
        total = total + arrived
    cross = total[V_GAINC : V_SHIFTC + 1]
    yield total, cross + (yield lax.ppermute(cross, SECTION, [(0, 1), (1, 0)]))


def place_kernel(far, groups, where_ref, *refs):
    own_refs, outs = refs[:4], refs[4:]
    core, near, rest = where_ref[0], where_ref[1], where_ref[2]
    half = own_refs[2].shape[2]
    rows = 2 * half
    for share in range(4 * far):
        c, n, q = share // (2 * far), share // far % 2, share % far
        step, which = lax.rem(rest - q + far, far), lax.rem(near + n, 2)

        def put(rest_first, near_first, share=share, step=step, which=which):
            parts = [(0, 0, rows, rest_first, (which, step)), (1, 0, half, rest_first, (which, step))]
            parts.append((1, half, half, near_first, (step, which)))
            taken = 0
            for group, first, size, source, at in parts:
                out, col = groups[group][share * rows // D]
                start_row = share * rows % D + first
                place = taken if source is rest_first else 0
                value = source[at[0], at[1], place : place + size, :]
                outs[out][start_row : start_row + size, col * D : (col + 1) * D] = value.astype(F32)
                taken += size

        pl.when(core == c)(functools.partial(put, own_refs[0], own_refs[2]))
        pl.when(core != c)(functools.partial(put, own_refs[1], own_refs[3]))


def put_in_place(places, gathered, groups, widths):
    where = jnp.stack([places.core, places.near, places.rest]).astype(jnp.int32)
    flat = [item for pair in gathered for item in pair]
    return pl.pallas_call(
        functools.partial(place_kernel, places.far, groups),
        out_shape=[shape(D, width, dtype=F32) for width in widths],
        in_specs=[smem_spec()] + [vmem_spec()] * len(flat),
        out_specs=[vmem_spec()] * len(widths),
        compiler_params=PARAMS,
        name="place_sums",
    )(where, *flat)


def widen_kernel(up_in, down_in, up_out, down_out):
    up_out[...] = up_in[...].astype(F32)
    down_out[...] = down_in[...].astype(F32)


def widen(grads):
    count = FF // D
    return pl.pallas_call(
        widen_kernel,
        grid=(count,),
        out_shape=[shape(D, FF, dtype=F32), shape(FF, D, dtype=F32)],
        in_specs=[pl.BlockSpec((D, D), lambda i: (i, 0)), pl.BlockSpec((D, D), lambda i: (count + i, 0))],
        out_specs=[pl.BlockSpec((D, D), lambda i: (0, i)), pl.BlockSpec((D, D), lambda i: (i, 0))],
        compiler_params=PARAMS,
        name="widen",
    )(grads, grads)


def shards(
    inputs, cotangent, lengths, running, norm_gain, norm_shift, qkv_weight, out_weight, up_weight, up_bias,
    down_weight, down_bias, halt_weight, halt_bias, cross_gain, cross_shift, cross_query, cross_kv, cross_out,
):
    decoding = on_decoder()
    places = Places()
    rows = range(inputs.shape[1])
    vectors = (norm_gain, norm_shift, lengths, running, up_bias, down_bias, halt_weight, halt_bias)
    crosses = (cross_gain[None], cross_shift[None])
    firsts, received = [], []
    for row in rows:
        arrays = (
            inputs, *vectors, *crosses, qkv_weight, out_weight, up_weight, down_weight, cross_query,
            *([firsts[row - 1][11]] if row else []),
        )
        firsts.append(call_a(row, lengths, running, arrays))
        received.append(lax.ppermute(firsts[row][1], SECTION, [(0, 1)]))
    result = firsts[-1][11]
    middles, returned = [], []
    for row in rows:
        _, out, after = firsts[row][:3]
        arrays = (
            inputs, cotangent, *vectors, up_weight, down_weight, cross_kv, cross_out, received[row], out, after,
            firsts[row][7], result,
        )
        middles.append(call_b(row, lengths, running, arrays))
        result = middles[row][12]
        returned.append(lax.ppermute(middles[row][9], SECTION, [(1, 0)]))

    def both(items, index):
        return [item[index] for item in items]

    feeds = []
    for row in rows:
        _, _, after, _, _, _, _, n2, act, change, _, _ = firsts[row]
        arrays = (
            inputs, cotangent, norm_gain, running, halt_weight, halt_bias, up_weight, down_weight, returned[row], after,
            middles[row][13], change, n2, act, *middles[row][1:5], crosses[0], cross_query, middles[row][7], middles[row][10],
            *([feeds[row - 1][3]] if row else []),
        )
        feeds.append(call_c(row, running, arrays))
    feed_sum = lax.psum(feeds[-1][3], DP)
    groups = [[(0, 0), (0, 1), (0, 2), (1, 0)], [(2, 0), (3, 0), (3, 1), (4, 0)]]
    widths = [3 * D, D, D, 2 * D, D]

    def tail(operands):
        firsts, middles, feeds, received = operands
        vec = sum(both(middles, 0)) + sum(both(feeds, 0))
        cross_grads = call_w(
            [
                (both(firsts, 10), both(feeds, 4)),
                (received, both(middles, 8)),
                (both(middles, 5), both(middles, 6)),
            ]
        )
        crosses = scatter_steps(places, *cross_grads, (SECTION, DP), places.count)
        cross, grad_after = lax.optimization_barrier((next(crosses), both(feeds, 1)))
        cross = crosses.send(cross)
        kinds = [both(firsts, 3), both(firsts, 5), both(firsts, 6), both(firsts, 4), grad_after, both(feeds, 2)]
        kinds = [item for kind in (*kinds, both(middles, 11)) for item in kind]
        vec_self, *self_grads, input_grad = call_s(
            len(rows), lengths, (inputs, norm_gain, lengths, qkv_weight, out_weight, *kinds)
        )
        cross, self_grads = lax.optimization_barrier((cross, self_grads))
        selfs, small = scatter_steps(places, *self_grads), vector_steps(places, vec + vec_self)
        own, vec = lax.optimization_barrier((next(selfs), next(small)))
        sent = selfs.send(own), small.send(vec), crosses.send(cross)
        own, vec, cross = lax.optimization_barrier(sent)
        cross = crosses.send(cross)
        sent = selfs.send(own), small.send(vec), lax.ppermute(cross, SECTION, [(1, 0)])
        own, vec, moved_cross = lax.optimization_barrier(sent)
        cross_share = jnp.where(decoding, cross, moved_cross)
        half = cross_share.shape[0] // 2
        gathers = [
            gather_rest_first(places, jnp.concatenate([selfs.send(own), cross_share[:half]])),
            gather_near_first(places, cross_share[half:]),
        ]
        sent = *(next(gather) for gather in gathers), small.send(vec)
        own, cross, vec = lax.optimization_barrier(sent)
        sent = gathers[0].send(own), gathers[1].send(cross)
        vec, cross_vec = small.send(vec)
        gathered = [gather.send(item) for gather, item in zip(gathers, lax.optimization_barrier(sent))]
        finals = (
            jnp.stack([vec[V_GAIN1], vec[V_GAIN2]])[None],
            jnp.stack([vec[V_SHIFT1], vec[V_SHIFT2]])[None],
            vec[V_UPB : V_UPB + 4].reshape(1, FF),
            vec[V_DOWNB][None],
            vec[V_HW][None],
            vec[V_HB, :1],
            cross_vec[0],
            cross_vec[1],
        )
        stats = [jnp.where(decoding, middles[row][0], firsts[row][0])[V_RMS, :2] for row in rows]
        row_rms = jnp.sqrt(jnp.stack(stats)[None] / (L * D) + 1e-06)
        return *gathered, *finals, row_rms, input_grad

    def nothing(operands):
        parts = jnp.zeros((2, places.far, 6 * D // places.count, D), BF16)
        swapped = jnp.zeros((places.far, 2, 2 * D // places.count, D), BF16)
        pair, one, wide = (jnp.zeros((1, size, D), F32) for size in (2, 1, 4))
        finals = (pair, pair, wide.reshape(1, FF), one[0], one[0], one[0, 0, :1], one[0, 0], one[0, 0])
        return parts, swapped, *finals, jnp.zeros(inputs.shape[:2] + (2,), F32), jnp.zeros(inputs.shape, F32)

    *gathered, gain, shift, up_b, down_b, halt_w, halt_b, cross_g, cross_s, row_rms, input_grad = lax.cond(
        lengths[0, 0, 0] > 0, tail, nothing, (firsts, middles, feeds, received)
    )
    gathered = [(parts, places.swap(parts, 1)) for parts in gathered]
    qkv_sum, out_sum, query_sum, kv_sum, cross_out_sum = put_in_place(places, gathered, groups, widths)
    up_sum, down_sum = widen(feed_sum)
    return (
        result,
        input_grad,
        row_rms,
        gain,
        shift,
        qkv_sum[None],
        out_sum[None],
        up_sum[None],
        up_b,
        down_sum[None],
        down_b,
        halt_w,
        halt_b,
        cross_g,
        cross_s,
        query_sum,
        kv_sum,
        cross_out_sum,
    )


def solution(mesh):
    in_specs = (
        P(SECTION, DP, None, None),
        P(SECTION, DP, None, None),
        P(None, DP, None),
        P(SECTION, DP, None),
        P(SECTION, None, None),
        P(SECTION, None, None),
        P(SECTION, None, None),
        P(SECTION, None, None),
        P(SECTION, None, None),
        P(SECTION, None),
        P(SECTION, None, None),
        P(SECTION, None),
        P(SECTION, None),
        P(SECTION),
        P(),
        P(),
        P(),
        P(),
        P(),
    )
    out_specs = (
        P(SECTION, DP, None, None),
        P(SECTION, DP, None, None),
        P(SECTION, DP, None),
        P(SECTION, None, None),
        P(SECTION, None, None),
        P(SECTION, None, None),
        P(SECTION, None, None),
        P(SECTION, None, None),
        P(SECTION, None),
        P(SECTION, None, None),
        P(SECTION, None),
        P(SECTION, None),
        P(SECTION),
        P(),
        P(),
        P(),
        P(),
        P(),
    )
    return jax.shard_map(shards, mesh=mesh, in_specs=in_specs, out_specs=out_specs, check_vma=False)
```

```python
import functools

import jax
import jax.numpy as jnp
from jax import lax
from jax.experimental import pallas as pl
from jax.experimental.pallas import tpu as pltpu
from jax.sharding import PartitionSpec as P

L = 512
D = 512
FF = 2048
HEADS = 8
SECTION, DP = "section", "dp"
HEAD = D // HEADS
GROUP = 256
PER = GROUP // HEAD
RC = 512
EPS = 1e-05
MASKED = -1000000000.0
GELU_A = 0.7978845608028654
GELU_B = 0.044715
F32 = jnp.float32
BF16 = jnp.bfloat16

V_GAIN2, V_SHIFT2, V_UPB, V_DOWNB, V_HW, V_HB = 0, 1, 2, 6, 7, 8
V_GAINC, V_SHIFTC, V_GAIN1, V_SHIFT1, V_RMS = 9, 10, 11, 12, 13
V_ROWS = 16


def nn(left, right):
    return lax.dot_general(left, right, (((1,), (0,)), ((), ())), preferred_element_type=F32)


def nt(left, right):
    return lax.dot_general(left, right, (((1,), (1,)), ((), ())), preferred_element_type=F32)


def tn(left, right):
    return lax.dot_general(left, right, (((0,), (0,)), ((), ())), preferred_element_type=F32)


def col_sum(value):
    return jnp.sum(value, axis=0, keepdims=True)


def row_mean(value):
    return jnp.mean(value, axis=1, keepdims=True)


def normalize(value):
    centered = value - row_mean(value)
    scale = lax.rsqrt(row_mean(centered * centered) + EPS)
    return centered * scale, scale


def norm_input_grad(grad, gain, xhat, scale):
    scaled = grad * gain
    return scale * (scaled - row_mean(scaled) - xhat * row_mean(scaled * xhat))


def each(count, size, body):
    def step(index, carry):
        body(index, pl.ds(pl.multiple_of(index * size, size), size))
        return carry

    lax.fori_loop(0, count, step, 0)


def each_apart(count, size, body):
    for index in range(count):
        body(index, pl.ds(index * size, size))


def for_rows(body):
    for first in range(0, L, RC):
        body(slice(first, first + RC))


def head_masks():
    lane = lax.broadcasted_iota(jnp.int32, (1, GROUP), 1)
    return [(lane // HEAD) == place for place in range(PER)]


def keep(mask, value):
    return jnp.where(mask, value, jnp.zeros_like(value))


def segments(len_ref, side, row, shape, dim, first):
    place = lax.broadcasted_iota(jnp.int32, shape, dim) + first
    total = jnp.int32(0)
    found = jnp.zeros(shape, jnp.int32)
    for index in range(len_ref.shape[2]):
        total = total + len_ref[side, row, index]
        found = found + (place >= total).astype(jnp.int32)
    return found


def write_bias(bias_ref, len_ref, row, row_side, col_side, causal_sign, causal):
    across = segments(len_ref, col_side, row, (1, L), 1, 0)

    def some(part):
        allowed = segments(len_ref, row_side, row, (RC, 1), 0, part.start) == across
        if causal is not None:
            row_place = lax.broadcasted_iota(jnp.int32, (RC, L), 0) + part.start
            col_place = lax.broadcasted_iota(jnp.int32, (RC, L), 1)
            ordered = (row_place - col_place) * causal_sign >= 0
            allowed = allowed & (ordered | jnp.logical_not(causal))
        bias_ref[part, :] = jnp.where(allowed, 0.0, MASKED)

    for_rows(some)


def attend_forward(queries, q0, keys, k0, values, v0, bias_ref, out_ref, stat_ref, column_ref, loop=each):
    masks = head_masks()
    lane = lax.broadcasted_iota(jnp.int32, (1, 128), 1)
    column_ref[...] = jnp.zeros_like(column_ref)

    def of_group(index, cols):
        own_q, own_k, own_v = (ref[:, moved(cols, first)] for ref, first in ((queries, q0), (keys, k0), (values, v0)))
        stats = column_ref[...]
        weights = []
        for place in range(PER):
            scores = nt(keep(masks[place], own_q), own_k) + bias_ref[...]
            top = jnp.max(scores, axis=1, keepdims=True)
            expanded = jnp.exp(scores - top)
            total = jnp.sum(expanded, axis=1, keepdims=True)
            weights.append((expanded * (1.0 / total)).astype(BF16))
            stats = jnp.where(lane == index * PER + place, top + jnp.log(total), stats)
        column_ref[...] = stats
        stacked = jnp.concatenate([keep(mask, own_v) for mask in masks], axis=0)
        out_ref[:, cols] = nn(jnp.concatenate(weights, axis=1), stacked).astype(BF16)

    loop(D // GROUP, GROUP, of_group)
    turned = column_ref[...].T
    for head in range(HEADS):
        stat_ref[head] = turned[head : head + 1, :]


def moved(cols, first):
    place = cols.start + first
    return pl.ds(place if isinstance(place, int) else pl.multiple_of(place, GROUP), cols.size)


def attend_backward(
    queries, q0, keys, k0, values, v0, grads, bias_ref, stat_ref,
    turned_ref, dq_ref, scores_ref, drops_ref, probs_ref, slants_ref, target, t0,
):
    masks = head_masks()

    def of_group(index, cols):
        own_q, own_k, own_v = (ref[:, moved(cols, first)] for ref, first in ((queries, q0), (keys, k0), (values, v0)))
        own_g = grads[:, cols]
        turned_ref[cols, :] = own_k.T
        for place in range(PER):
            head, slot = index * PER + place, place % 2
            rows, across = pl.ds(pl.multiple_of(head * HEAD, HEAD), HEAD), slice(place * L, (place + 1) * L)
            scores_ref[slot] = nt(keep(masks[place], own_k), own_q)
            drops_ref[slot] = nt(keep(masks[place], own_v), own_g)
            log_total, inner = stat_ref[head], jnp.zeros((8, L), F32)
            for part in range(0, L, 64):
                lines = slice(part, part + 64)
                probs = jnp.exp(scores_ref[slot, lines, :] + bias_ref[lines, :] - log_total)
                scores_ref[slot, lines, :] = probs
                probs_ref[lines, across] = probs.astype(BF16)
                inner += jnp.sum((probs * drops_ref[slot, lines, :]).reshape(8, 8, L), axis=0)
            inner = col_sum(inner)
            for part in range(0, L, 64):
                lines = slice(part, part + 64)
                slant = scores_ref[slot, lines, :] * (drops_ref[slot, lines, :] - inner)
                slants_ref[lines, across] = slant.astype(BF16)
            dq_ref[rows, :] = nn(turned_ref[rows, :], slants_ref[:, across])
        stacked = jnp.concatenate([keep(mask, own_q) for mask in masks], axis=0)
        target[:, moved(cols, t0)] = nn(slants_ref[...], stacked).astype(BF16)
        stacked = jnp.concatenate([keep(mask, own_g) for mask in masks], axis=0)
        target[:, moved(cols, t0 + D)] = nn(probs_ref[...], stacked).astype(BF16)

    each(D // GROUP, GROUP, of_group)


def gelu_parts(pre):
    square = pre * pre
    half = 0.5 + 0.5 * jnp.tanh(pre * (GELU_A + GELU_A * GELU_B * square))
    slope = half + half * (1.0 - half) * pre * (2.0 * GELU_A + 6.0 * GELU_A * GELU_B * square)
    return pre * half, slope


def feed_forward(
    after_ref, norm_gain, norm_shift, w_up, up_bias, w_down, down_bias, n2_ref, act_ref, slope_ref, total_ref, loop=each
):
    after = after_ref[...]
    n2_ref[...] = (normalize(after)[0] * norm_gain[1:2] + norm_shift[1:2]).astype(BF16)
    total_ref[...] = after + down_bias[...]

    def of_block(_, cols):
        activated, slope = gelu_parts(nn(n2_ref[...], w_up[:, cols]) + up_bias[:, cols])
        activated = activated.astype(BF16)
        act_ref[:, cols] = activated
        if slope_ref is not None:
            slope_ref[:, cols] = slope.astype(BF16)
        total_ref[...] += nn(activated, w_down[cols, :])

    loop(FF // D, D, of_block)


def feed_slope(gb_ref, w_down, slope_ref, gp_ref, bias_ref, w_up=None, back_ref=None, loop=each):
    def of_block(_, cols):
        value = (nt(gb_ref[...], w_down[cols, :]) * slope_ref[:, cols].astype(F32)).astype(BF16)
        gp_ref[:, cols] = value
        bias_ref[:, cols] = col_sum(value.astype(F32))
        if w_up is not None:
            back_ref[...] += nt(value, w_up[:, cols])

    loop(FF // D, D, of_block)


def add_up_bias(vec, bias_ref):
    for index, cols in enumerate(blocks_of(FF)):
        add_row(vec, V_UPB + index, bias_ref[:, cols])


def feed_input_grad(after_ref, back, grad_ref, gb_ref, norm_gain, vec, part):
    add_row(vec, V_DOWNB, col_sum(gb_ref[part, :].astype(F32)))
    xhat, scale = normalize(after_ref[part, :])
    add_row(vec, V_GAIN2, col_sum(back * xhat))
    add_row(vec, V_SHIFT2, col_sum(back))
    return grad_ref[part, :] + norm_input_grad(back, norm_gain[1:2], xhat, scale)


def write_running(column_ref, run_ref, row):
    line = run_ref[0, row : row + 1, :].astype(F32)
    column_ref[...] = jnp.broadcast_to(line, (128, L)).T


def halting_share(current, run, halt_weight, halt_bias):
    logit = jnp.sum(current * halt_weight[...], axis=1, keepdims=True) + halt_bias[0]
    rate = jax.nn.sigmoid(logit)
    return run * rate, rate


def halting_backward(grad, change, current, share, rate, run, halt_weight, vec_ref):
    logit_grad = (
        run * jnp.sum(grad * change, axis=1, keepdims=True) * rate * (1.0 - rate)
    )
    vec_ref[V_HW : V_HW + 1, :] += col_sum(logit_grad * current)
    vec_ref[V_HB : V_HB + 1, :] += jnp.broadcast_to(col_sum(logit_grad), (1, D))
    return share * grad, (1.0 - share) * grad + logit_grad * halt_weight[...]


def write_rms(vec_ref, total_ref):
    lane = lax.broadcasted_iota(jnp.int32, (1, D), 1)
    vec_ref[V_RMS : V_RMS + 1, :] = jnp.where(lane == 0, total_ref[0], total_ref[1])


class Copies:
    def __init__(self, sems, **pairs):
        for index, (name, (source, target)) in enumerate(pairs.items()):
            setattr(self, name, pltpu.make_async_copy(source, target, sems.at[index]))


def start(*copies):
    for copy in copies:
        copy.start()


def wait(*copies):
    for copy in copies:
        copy.wait()


def blocks_of(width):
    return [slice(place, place + D) for place in range(0, width, D)]


def on_decoder():
    return lax.axis_index(SECTION) == 1


def halves_out(held, mine_hbm, other_hbm, sems):
    half = held.shape[0] // 2
    core = lax.rem(lax.axis_index(DP), 2)
    return [
        pltpu.make_async_copy(held.at[pl.ds(pl.multiple_of(place * half, half), half)], target, sems.at[index])
        for index, (place, target) in enumerate(((core, mine_hbm), (1 - core, other_hbm)))
    ]


def add_row(vec, row, value):
    vec[row : row + 1, :] += value


def kernel_a(
    row,
    x_hbm, ng_hbm, ns_hbm, len_hbm, run_hbm, ub_hbm, db_hbm, hw_hbm, hb_hbm, cg_hbm, cs_hbm,
    wqkv_hbm, wout_hbm, wup_hbm, wdn_hbm, wcq_hbm,
    *rest,
):
    (
        vec_hbm, out_hbm, after_hbm, packed_hbm, att_hbm, stat_hbm, normed_hbm, n2_hbm, act_hbm, change_hbm,
        normed2_hbm, result_hbm, x, ng, ns, lens, run, ub, db, hw, hb, cg, cs, wqkv, wout, wup, wdn, wcq,
        vec, out, after, packed, att, stat, normed, n2, act, change, normed2, bias, column, total, sems,
    ) = rest[row > 0 :]
    decoding = on_decoder()
    encoding = jnp.logical_not(decoding)
    c = Copies(
        sems,
        x=(x_hbm.at[0, row], x), ng=(ng_hbm.at[0], ng), ns=(ns_hbm.at[0], ns), lens=(len_hbm, lens), run=(run_hbm, run),
        ub=(ub_hbm, ub), db=(db_hbm, db), hw=(hw_hbm, hw), hb=(hb_hbm, hb), cg=(cg_hbm, cg), cs=(cs_hbm, cs),
        wqkv=(wqkv_hbm.at[0], wqkv), wout=(wout_hbm.at[0], wout), wup=(wup_hbm.at[0], wup), wdn=(wdn_hbm.at[0], wdn),
        wcq=(wcq_hbm, wcq),
        vec=(vec, vec_hbm), out=(out, out_hbm), after=(after, after_hbm), packed=(packed, packed_hbm),
        att=(att, att_hbm), stat=(stat, stat_hbm), normed=(normed, normed_hbm), normed2=(normed2, normed2_hbm),
        n2=(n2, n2_hbm), act=(act, act_hbm), change=(change, change_hbm),
        result=(out, result_hbm.at[0, row]),
    )
    start(c.x, c.ng, c.ns, c.lens, c.wqkv, c.wout)

    @pl.when(encoding)
    def _():
        start(c.run, c.ub, c.db, c.hw, c.hb, c.wup, c.wdn)

    @pl.when(decoding)
    def _():
        start(c.cg, c.cs, c.wcq)

    wait(c.lens)
    side = decoding.astype(jnp.int32)
    write_bias(bias, lens, row, side, side, 1, decoding)
    wait(c.x, c.ng, c.ns)

    @for_rows
    def _(part):
        normed[part, :] = (normalize(x[part, :].astype(F32))[0] * ng[0:1] + ns[0:1]).astype(BF16)

    start(c.normed)
    wait(c.wqkv)
    for index, cols in enumerate(blocks_of(3 * D)):
        value = nn(normed[...], wqkv[:, cols]).astype(BF16)
        if index == 0:
            value = (value.astype(F32) * HEAD**-0.5).astype(BF16)
        packed[:, cols] = value
    start(c.packed)
    attend_forward(packed, 0, packed, D, packed, 2 * D, bias, att, stat, column, each_apart)
    start(c.att, c.stat)
    wait(c.wout)
    after[...] = x[...].astype(F32) + nn(att[...], wout[...])
    start(c.after)

    @pl.when(encoding)
    def _():
        wait(c.run, c.ub, c.db, c.hw, c.hb, c.wup, c.wdn)
        write_running(column, run, row)
        feed_forward(after, ng, ns, wup, ub, wdn, db, n2, act, None, bias)
        start(c.n2, c.act)
        total[0] = 0.0
        total[1] = 0.0

        @for_rows
        def _(part):
            updated = bias[part, :]
            current = x[part, :].astype(F32)
            share, _ = halting_share(current, column[part, :1], hw, hb)
            moved = updated - current
            change[part, :] = moved
            moved = share * moved
            result = current + moved
            out[part, :] = result.astype(BF16)
            start(c.out, c.change, c.result)
            total[0] += jnp.sum(result * result)
            total[1] += jnp.sum(moved * moved)

        vec[...] = jnp.zeros_like(vec)
        write_rms(vec, total)
        start(c.vec)
        wait(c.n2, c.act, c.change, c.vec, c.result)

    @pl.when(decoding)
    def _():
        wait(c.cg, c.cs, c.wcq)

        @for_rows
        def _(part):
            normed2[part, :] = (normalize(after[part, :])[0] * cg[...] + cs[...]).astype(BF16)

        value = nn(normed2[...], wcq[...]).astype(BF16)
        out[...] = (value.astype(F32) * HEAD**-0.5).astype(BF16)
        start(c.out, c.normed2)
        vec[...] = jnp.zeros_like(vec)
        start(c.vec)
        wait(c.normed2, c.vec)

    wait(c.normed, c.packed, c.att, c.stat, c.after, c.out)


def kernel_b(
    row,
    x_hbm, cot_hbm, ng_hbm, ns_hbm, len_hbm, run_hbm, ub_hbm, db_hbm, hw_hbm, hb_hbm,
    wup_hbm, wdn_hbm, wkv_hbm, wco_hbm, mem_hbm, cq_hbm, after_hbm, n2e_hbm, _,
    vec_hbm, n2_hbm, act_hbm, gb_hbm, gp_hbm, att_hbm, gc_hbm, dq_hbm, gkv_hbm, back_hbm, ga_hbm, gx_hbm, result_hbm, slope_hbm,
    x, cot, ng, ns, lens, run, ub, db, hw, hb, wup, wdn, wkv, wco, mem, cq, after,
    vec, n2, act, gb, gp, att, gc, dqb, gkv, back, gaf, gx,
    result, kv, slope, across, gatt, ubg, bias, bias2, stat, column, turned, dq, scores, drops, probs, slants, total, sems,
):
    c = Copies(
        sems,
        x=(x_hbm.at[0, row], x), cot=(cot_hbm.at[0, row], cot), ng=(ng_hbm.at[0], ng), ns=(ns_hbm.at[0], ns),
        lens=(len_hbm, lens), run=(run_hbm, run), ub=(ub_hbm, ub), db=(db_hbm, db), hw=(hw_hbm, hw), hb=(hb_hbm, hb),
        wup=(wup_hbm.at[0], wup), wdn=(wdn_hbm.at[0], wdn), wkv=(wkv_hbm, wkv),
        wco=(wco_hbm, wco), mem=(mem_hbm, mem), cq=(cq_hbm, cq), after=(after_hbm, after),
        vec=(vec, vec_hbm), n2=(n2, n2_hbm), act=(act, act_hbm), gb=(gb, gb_hbm), gp=(gp, gp_hbm), att=(att, att_hbm),
        gc=(gc, gc_hbm), dq=(dqb, dq_hbm), gkv=(gkv, gkv_hbm), back=(back, back_hbm), result=(result, result_hbm.at[0, row]),
        ga=(gaf, ga_hbm), gx=(gx, gx_hbm), n2e=(n2e_hbm, n2), slope=(slope, slope_hbm),
    )
    decoding = on_decoder()

    @pl.when(jnp.logical_not(decoding))
    def _():
        start(c.n2e, c.wup, c.ub)
        vec[...] = jnp.zeros_like(vec)
        start(c.vec)
        wait(c.n2e, c.wup, c.ub)

        def of_block(_, cols):
            slope[:, cols] = gelu_parts(nn(n2[...], wup[:, cols]) + ub[:, cols])[1].astype(BF16)

        each(FF // D, D, of_block)
        start(c.slope)
        wait(c.slope)

    @pl.when(decoding)
    def _():
        start(c.mem, c.wkv, c.lens, c.cq, c.wco, c.after, c.ng, c.ns, c.ub, c.db, c.wup, c.wdn)
        start(c.x, c.cot, c.run, c.hw, c.hb)
        vec[...] = jnp.zeros_like(vec)
        wait(c.lens)
        write_bias(bias, lens, row, 1, 0, 1, None)
        write_bias(bias2, lens, row, 0, 1, 1, None)
        wait(c.mem, c.wkv)
        for cols in blocks_of(2 * D):
            kv[:, cols] = nn(mem[...], wkv[:, cols]).astype(BF16)
        wait(c.cq)
        attend_forward(cq, 0, kv, 0, kv, D, bias, att, stat, column, each_apart)
        start(c.att)
        wait(c.after, c.wco)
        across[...] = after[...] + nn(att[...], wco[...])
        wait(c.ng, c.ns, c.ub, c.db, c.wup, c.wdn, c.x, c.cot, c.run, c.hw, c.hb)
        write_running(column, run, row)
        feed_forward(across, ng, ns, wup, ub, wdn, db, n2, act, slope, dq, each_apart)
        start(c.n2, c.act)
        total[0] = 0.0
        total[1] = 0.0

        @for_rows
        def _(part):
            updated = dq[part, :]
            current = x[part, :].astype(F32)
            share, rate = halting_share(current, column[part, :1], hw, hb)
            moved = updated - current
            grad, own = halting_backward(
                cot[part, :].astype(F32), moved, current, share, rate, column[part, :1], hw, vec
            )
            gx[part, :] = own
            moved = share * moved
            value = current + moved
            result[part, :] = value.astype(BF16)
            total[0] += jnp.sum(value * value)
            total[1] += jnp.sum(moved * moved)
            gaf[part, :] = grad
            gb[part, :] = grad.astype(BF16)

        start(c.gb, c.result, c.gx)

        dq[...] = jnp.zeros_like(dq)
        feed_slope(gb, wdn, slope, gp, ubg, wup, dq, each_apart)
        start(c.gp)
        add_up_bias(vec, ubg)

        @for_rows
        def _(part):
            grad = feed_input_grad(across, dq[part, :], gaf, gb, ng, vec, part)
            gaf[part, :] = grad
            gc[part, :] = grad.astype(BF16)

        gatt[...] = nt(gc[...], wco[...]).astype(BF16)
        start(c.gc, c.ga)
        write_rms(vec, total)
        start(c.vec)
        attend_backward(
            cq, 0, kv, 0, kv, D, gatt, bias2, stat, turned, dq, scores, drops, probs, slants, gkv, 0
        )
        start(c.gkv)
        dqb[...] = (dq[...] * HEAD**-0.5).astype(BF16)
        start(c.dq)
        back[...] = (nt(gkv[:, 0:D], wkv[:, 0:D]) + nt(gkv[:, D:], wkv[:, D:])).astype(BF16)
        start(c.back)
        wait(c.att, c.n2, c.act, c.gb, c.gp, c.gc, c.result, c.gx, c.gkv, c.dq, c.back, c.ga)

    wait(c.vec)


def kernel_c(
    row,
    x_hbm, cot_hbm, ng_hbm, run_hbm, hw_hbm, hb_hbm, wup_hbm, wdn_hbm, back_hbm, after_hbm, slope_hbm, change_hbm,
    n2e_hbm, acte_hbm, n2_hbm, act_hbm, gb_hbm, gp_hbm, cg_hbm, wcq_hbm, dq_hbm, gad_hbm, *rest,
):
    prior_hbm, rest = (rest[0], rest[1:]) if row else (None, rest)
    vec_hbm, ga_hbm, gx_hbm, grads_hbm, gq_hbm = rest[:5]
    (
        x, cot, ng, run, hw, hb, wup, wdn, back, after, slope, change, n2, act, cg, wcq, dq, vec, gaf, gx, gb, gp, grads, gq,
        column, column32, turned, ubg, sems,
    ) = rest[5:]
    decoding = on_decoder()
    encoding = jnp.logical_not(decoding)
    ups, downs = pl.ds(0, FF), pl.ds(FF, FF)
    c = Copies(
        sems,
        x=(x_hbm.at[0, row], x), cot=(cot_hbm.at[0, row], cot), ng=(ng_hbm.at[0], ng), run=(run_hbm, run),
        hw=(hw_hbm, hw), hb=(hb_hbm, hb), wup=(wup_hbm.at[0], wup), wdn=(wdn_hbm.at[0], wdn), back=(back_hbm, back),
        after=(after_hbm, after), slope=(slope_hbm, slope), change=(change_hbm, change), n2e=(n2e_hbm, n2),
        acte=(acte_hbm, act), n2=(n2_hbm, n2), act=(act_hbm, act), gb=(gb_hbm, gb), gp=(gp_hbm, gp),
        vec=(vec, vec_hbm), ga=(gaf, ga_hbm), gx=(gx, gx_hbm), grads=(grads, grads_hbm), cg=(cg_hbm, cg),
        wcq=(wcq_hbm, wcq), dq=(dq_hbm, dq), gad=(gad_hbm, gaf), gq=(gq, gq_hbm),
        **({"prior_up": (prior_hbm.at[ups], grads.at[ups]), "prior_down": (prior_hbm.at[downs], grads.at[downs])} if row else {}),
    )
    vec[...] = jnp.zeros_like(vec)

    @pl.when(encoding)
    def _():
        start(c.back, c.cot, c.x, c.change, c.run, c.hw, c.hb, c.wdn, c.slope, c.n2e)
        if row:
            start(c.prior_up, c.acte, c.prior_down)
        else:
            start(c.acte)
        start(c.wup, c.after, c.ng)
        wait(c.back, c.cot, c.x, c.change, c.run, c.hw, c.hb)
        write_running(column, run, row)

        @for_rows
        def _(part):
            grad = cot[part, :].astype(F32) + back[part, :].astype(F32)
            current = x[part, :].astype(F32)
            share, rate = halting_share(current, column[part, :1], hw, hb)
            grad, own = halting_backward(
                grad, change[part, :], current, share, rate, column[part, :1], hw, vec
            )
            gx[part, :] = own
            gaf[part, :] = grad
            gb[part, :] = grad.astype(BF16)

        start(c.gx)
        wait(c.wdn, c.slope)
        feed_slope(gb, wdn, slope, gp, ubg)
        add_up_bias(vec, ubg)
        wait(c.n2e)

    @pl.when(decoding)
    def _():
        start(c.n2, c.gp)
        if row:
            start(c.prior_up)
        start(c.gb, c.act)
        if row:
            start(c.prior_down)
        start(c.dq, c.wcq, c.after, c.gad, c.cg)
        wait(c.n2, c.gp)

    if row:
        wait(c.prior_up)
    turned[...] = n2[...].T

    def up_block(_, cols):
        add_block(grads, cols, nn(turned[...], gp[:, cols]), row)

    def down_block(_, cols):
        add_block(grads, pl.ds(FF + cols.start, D), tn(act[:, cols], gb[...]), row)

    each_apart(FF // D, D, up_block)

    @pl.when(encoding)
    def _():
        wait(c.acte)

    @pl.when(decoding)
    def _():
        wait(c.gb, c.act)

    if row:
        wait(c.prior_down)
    each_apart(FF // D, D, down_block)
    start(c.grads)

    @pl.when(encoding)
    def _():
        wait(c.wup, c.after, c.ng)

        column32[...] = jnp.zeros_like(column32)

        def back_of(_, cols):
            column32[...] += nt(gp[:, cols], wup[:, cols])

        each(FF // D, D, back_of)

        @for_rows
        def _(part):
            gaf[part, :] = feed_input_grad(after, column32[part, :], gaf, gb, ng, vec, part)

        start(c.ga)
        wait(c.ga, c.gx)

    @pl.when(decoding)
    def _():
        wait(c.dq, c.wcq, c.after, c.gad, c.cg)
        gq[...] = dq[...].T
        start(c.gq)

        @for_rows
        def _(part):
            grad = nt(gq[part, :], wcq[...])
            xhat, scale = normalize(after[part, :])
            add_row(vec, V_GAINC, col_sum(grad * xhat))
            add_row(vec, V_SHIFTC, col_sum(grad))
            gaf[part, :] += norm_input_grad(grad, cg[...], xhat, scale)

        start(c.ga)
        wait(c.gq, c.ga)

    start(c.vec)
    wait(c.grads, c.vec)


def add_block(grads, rows, value, more):
    if more:
        value = value + grads[rows, :].astype(F32)
    grads[rows, :] = value.astype(BF16)


def kernel_s(count, x_hbm, ng_hbm, len_hbm, wqkv_hbm, wout_hbm, *rest):
    held = [rest[index * count : (index + 1) * count] for index in range(7)]
    vec_hbm, mine_hbm, other_hbm, grad_hbm = rest[7 * count : 7 * count + 4]
    (
        x, ng, lens, wqkv, wout, packed, stat, normed, att, gaf, gx, vec, grads, grad_out, sums, gs, gpack, gatt, bias,
        turned, dq, scores, drops, probs, slants, sems, row_sems, out_sems, half_sems,
    ) = rest[7 * count + 4 :]
    decoding = on_decoder()
    encoding = jnp.logical_not(decoding)
    c = Copies(
        sems,
        x=(x_hbm.at[0], x), ng=(ng_hbm.at[0], ng), lens=(len_hbm, lens), wqkv=(wqkv_hbm.at[0], wqkv),
        wout=(wout_hbm.at[0], wout), vec=(vec, vec_hbm),
    )
    halves = halves_out(grads, mine_hbm, other_hbm, half_sems)

    def of_row(row):
        places = (packed, stat, normed, att, gaf, gx, gx)
        return Copies(
            row_sems.at[row],
            **{
                name: (held[index][row], place.at[row])
                for index, (name, place) in enumerate(zip(("packed", "stat", "normed", "att", "ga", "gxe", "gxd"), places))
            },
        )

    lines = [of_row(row) for row in range(count)]
    start(c.lens, c.wout, lines[0].ga, lines[0].packed, lines[0].stat, lines[0].att, lines[0].normed, c.wqkv, c.x, c.ng)
    for line in lines[1:]:
        start(line.ga, line.packed, line.stat, line.att, line.normed)

    @pl.when(encoding)
    def _():
        start(*[line.gxe for line in lines])

    @pl.when(decoding)
    def _():
        start(*[line.gxd for line in lines])

    vec[...] = jnp.zeros_like(vec)
    sums[...] = jnp.zeros_like(sums)
    wait(c.lens, c.wout)
    side = decoding.astype(jnp.int32)

    def one_row(row, carry):
        for index in range(count):

            @pl.when(row == index)
            def _():
                wait(*[getattr(lines[index], name) for name in ("packed", "stat", "normed", "att", "ga")])

        write_bias(bias, lens, row, side, side, -1, decoding)
        gs[...] = gaf[row].astype(BF16)
        gatt[...] = nt(gs[...], wout[...]).astype(BF16)
        own = packed.at[row]
        attend_backward(
            own, 0, own, D, own, 2 * D, gatt, bias, stat.at[row], turned, dq, scores, drops, probs, slants, gpack, D
        )
        gpack[:, 0:D] = (dq[...] * HEAD**-0.5).astype(BF16).T
        sums[3 * D : 4 * D, :] += tn(att[row], gs[...])
        flipped = normed[row].T
        for cols in blocks_of(3 * D):
            sums[cols, :] += nn(flipped, gpack[:, cols])

        @pl.when(row == count - 1)
        def _():
            grads[...] = sums[...].astype(BF16)
            start(*halves)

        @pl.when(row == 0)
        def _():
            wait(c.wqkv, c.x, c.ng)

        for index in range(count):

            @pl.when((row == index) & encoding)
            def _():
                wait(lines[index].gxe)

            @pl.when((row == index) & decoding)
            def _():
                wait(lines[index].gxd)

        for index, cols in enumerate(blocks_of(3 * D)):
            value = nt(gpack[:, cols], wqkv[:, cols])
            grad = value if index == 0 else grad + value
        xhat, scale = normalize(x[row].astype(F32))
        add_row(vec, V_GAIN1, col_sum(grad * xhat))
        add_row(vec, V_SHIFT1, col_sum(grad))
        grad_out[row] = gaf[row] + gx[row] + norm_input_grad(grad, ng[0:1], xhat, scale)
        pltpu.make_async_copy(grad_out.at[row], grad_hbm.at[0, row], out_sems.at[row]).start()
        return carry

    lax.fori_loop(0, count, one_row, 0)
    start(c.vec)
    for row in range(count):
        pltpu.make_async_copy(grad_out.at[row], grad_hbm.at[0, row], out_sems.at[row]).wait()
    wait(*halves, c.vec)


def any_spec():
    return pl.BlockSpec(memory_space=pl.ANY)


def vmem_spec():
    return pl.BlockSpec(memory_space=pltpu.VMEM)


def smem_spec():
    return pl.BlockSpec(memory_space=pltpu.SMEM)


def shape(*dims, dtype=BF16):
    return jax.ShapeDtypeStruct(dims, dtype)


def scratch_of(shapes):
    return [pltpu.VMEM(item.shape, item.dtype) for item in shapes]


PARAMS = pltpu.CompilerParams(vmem_limit_bytes=63 * 1024 * 1024)


def made(dims, dtype=BF16):
    return pltpu.VMEM(dims, dtype)


def call(kernel, name, arrays, inputs, outs, extra, copies, aliases=None, unheld=()):
    return pl.pallas_call(
        kernel,
        out_shape=[shape(V_ROWS, D, dtype=F32)] + outs + list(unheld),
        in_specs=[any_spec()] * len(arrays),
        out_specs=[any_spec()] * (1 + len(outs) + len(unheld)),
        input_output_aliases=aliases or {},
        scratch_shapes=inputs
        + [made((V_ROWS, D), F32)]
        + scratch_of(outs)
        + extra
        + [pltpu.SemaphoreType.DMA((copies,))],
        compiler_params=PARAMS,
        name=name,
    )(*arrays)


VECTOR = made((1, D), F32)
PAIR = made((2, D), F32)
WIDE = made((1, FF), F32)
ROW = made((L, D))
ROW32 = made((L, D), F32)
WUP, WDN, WSQ = made((D, FF)), made((FF, D)), made((D, D))
STAT = made((HEADS, 1, L), F32)
COLUMN = made((L, 128), F32)
ONE = pltpu.SMEM((1,), F32)


def lens_of(arrays):
    return pltpu.SMEM(arrays.shape, arrays.dtype)


def call_a(row, lengths, running, arrays):
    outs = [
        shape(L, D), shape(L, D, dtype=F32), shape(L, 3 * D), shape(L, D), shape(HEADS, 1, L, dtype=F32), shape(L, D),
        shape(L, D), shape(L, FF), shape(L, D, dtype=F32), shape(L, D),
    ]
    inputs = [
        ROW, PAIR, PAIR, lens_of(lengths), made(running.shape, running.dtype), WIDE, VECTOR, VECTOR, ONE, VECTOR, VECTOR,
        made((D, 3 * D)), WSQ, WUP, WDN, WSQ,
    ]
    extra = [ROW32, COLUMN, pltpu.SMEM((2,), F32)]
    aliases = {len(arrays) - 1: 1 + len(outs)} if row else {}
    kernel = functools.partial(kernel_a, row)
    return call(kernel, "forward_a", arrays, inputs, outs, extra, 34, aliases, [shape(*arrays[0].shape)])


ATTEND_SCRATCH = [
    made((D, L)), ROW32, made((2, L, L), F32), made((2, L, L), F32), made((L, PER * L)), made((L, PER * L)),
]


def call_b(row, lengths, running, arrays):
    outs = [
        shape(L, D), shape(L, FF), shape(L, D), shape(L, FF), shape(L, D), shape(L, D), shape(D, L), shape(L, 2 * D),
        shape(L, D), shape(L, D, dtype=F32), shape(L, D, dtype=F32),
    ]
    inputs = [
        ROW, ROW, PAIR, PAIR, lens_of(lengths), made(running.shape, running.dtype), WIDE, VECTOR, VECTOR, ONE,
        WUP, WDN, made((D, 2 * D)), WSQ, ROW, ROW, ROW32,
    ]
    extra = [ROW, made((L, 2 * D)), made((L, FF)), ROW32, ROW, WIDE, ROW32, ROW32, STAT, COLUMN, *ATTEND_SCRATCH, pltpu.SMEM((2,), F32)]
    aliases = {len(arrays) - 1: 1 + len(outs)}
    kernel = functools.partial(kernel_b, row)
    unheld = [shape(*arrays[0].shape), shape(L, FF)]
    return call(kernel, "decoder_b", arrays, inputs, outs, extra, 32, aliases, unheld)


def call_c(row, running, arrays):
    outs = [shape(L, D, dtype=F32), shape(L, D, dtype=F32), shape(2 * FF, D), shape(L, D)]
    inputs = [
        ROW, ROW, PAIR, made(running.shape, running.dtype), VECTOR, ONE, WUP, WDN, ROW, ROW32, made((L, FF)), ROW32, ROW,
        made((L, FF)), VECTOR, WSQ, made((D, L)),
    ]
    held = scratch_of(outs)
    return pl.pallas_call(
        functools.partial(kernel_c, row),
        out_shape=[shape(V_ROWS, D, dtype=F32)] + outs,
        in_specs=[any_spec()] * len(arrays),
        out_specs=[any_spec()] * 5,
        scratch_shapes=inputs
        + [made((V_ROWS, D), F32), held[0], held[1], ROW, made((L, FF)), held[2], held[3], COLUMN, ROW32, made((D, L)), WIDE]
        + [pltpu.SemaphoreType.DMA((29,))],
        compiler_params=PARAMS,
        name="feed_backward",
    )(*arrays)


def call_s(count, lengths, arrays):
    def rows_of(dims, dtype=BF16):
        return made((count,) + dims, dtype)

    inputs = [
        rows_of((L, D)), PAIR, lens_of(lengths), made((D, 3 * D)), WSQ, rows_of((L, 3 * D)), rows_of((HEADS, 1, L), F32),
        rows_of((L, D)), rows_of((L, D)), rows_of((L, D), F32), rows_of((L, D), F32),
    ]
    extra = [rows_of((L, D), F32), made((4 * D, D), F32), ROW, made((L, 3 * D)), ROW, ROW32, *ATTEND_SCRATCH]
    return pl.pallas_call(
        functools.partial(kernel_s, count),
        out_shape=[shape(V_ROWS, D, dtype=F32)] + [shape(2 * D, D)] * 2 + [shape(*arrays[0].shape, dtype=F32)],
        in_specs=[any_spec()] * len(arrays),
        out_specs=[any_spec()] * 4,
        scratch_shapes=inputs
        + [made((V_ROWS, D), F32), made((4 * D, D))]
        + extra
        + [pltpu.SemaphoreType.DMA((7,)), pltpu.SemaphoreType.DMA((count, 7)), pltpu.SemaphoreType.DMA((count,))]
        + [pltpu.SemaphoreType.DMA((2,))],
        compiler_params=PARAMS,
        name="self_backward",
    )(*arrays)


def kernel_w(*refs):
    count = (len(refs) - 5) // 2
    sources, (mine_hbm, other_hbm), held = refs[:count], refs[count : count + 2], refs[count + 2 : -3]
    outs, sems, out_sems = refs[-3:]

    @pl.when(on_decoder())
    def _():
        copies = [pltpu.make_async_copy(sources[i], held[i], sems.at[i]) for i in range(count)]
        start(*copies)
        block, each = 0, count // 3
        for pair in range(3):
            mine = slice(pair * each, (pair + 1) * each)
            wait(*copies[mine])
            lefts, rights = held[mine][: each // 2], held[mine][each // 2 :]
            turned = [left[...].T for left in lefts]
            for cols in blocks_of(rights[0].shape[1]):
                value = nn(turned[0], rights[0][:, cols])
                for left, right in zip(turned[1:], rights[1:]):
                    value += nn(left, right[:, cols])
                outs[block * D : (block + 1) * D, :] = value.astype(BF16)
                block += 1
        copies = halves_out(outs, mine_hbm, other_hbm, out_sems)
        start(*copies)
        wait(*copies)


def call_w(pairs):
    flat = [item for lefts, rights in pairs for item in (*lefts, *rights)]
    return pl.pallas_call(
        kernel_w,
        out_shape=[shape(2 * D, D)] * 2,
        in_specs=[any_spec()] * len(flat),
        out_specs=[any_spec()] * 2,
        scratch_shapes=scratch_of(flat)
        + [made((4 * D, D)), pltpu.SemaphoreType.DMA((len(flat),)), pltpu.SemaphoreType.DMA((2,))],
        compiler_params=PARAMS,
        name="cross_weights",
    )(*flat)


class Places:
    def __init__(self):
        self.count = lax.axis_size(DP)
        self.far = self.count // 4
        me = lax.axis_index(DP)
        self.core, self.near, self.rest = me % 2, (me // 2) % 2, me // 4

    def swap(self, value, bit, axis=DP, base=0):
        pairs = [(base + i, base + (i ^ bit)) for i in range(self.count)]
        return lax.ppermute(value, axis, pairs)

    def turn(self, value, steps, axis=DP, base=0):
        pairs = [(base + i, base + (i + 4 * steps) % self.count) for i in range(self.count)]
        return lax.ppermute(value, axis, pairs)


def halves(value, bit):
    half = value.shape[0] // 2
    mine = lax.dynamic_slice_in_dim(value, bit * half, half, 0)
    other = lax.dynamic_slice_in_dim(value, (1 - bit) * half, half, 0)
    return mine, other


def plus(left, right):
    return (left.astype(F32) + right.astype(F32)).astype(BF16)


def scatter_steps(places, mine, other, axis=DP, base=0):
    value = plus(mine, (yield places.swap(other, 1, axis, base)))
    mine, other = halves(value, places.near)
    value = plus(mine, (yield places.swap(other, 2, axis, base)))
    parts = value.reshape(places.far, -1, D)
    total = lax.dynamic_index_in_dim(parts, places.rest, 0, keepdims=False).astype(F32)
    sent = []
    for step in range(1, places.far):
        part = lax.dynamic_index_in_dim(parts, (places.rest + step) % places.far, 0, keepdims=False)
        sent.append(places.turn(part, step, axis, base))
    for part in (yield sent):
        total = total + part.astype(F32)
    yield total.astype(BF16)


def gather_rest_first(places, share):
    parts = jnp.stack([share] + (yield [places.turn(share, step) for step in range(1, places.far)]))
    yield jnp.stack([parts, (yield places.swap(parts, 2))])


def gather_near_first(places, share):
    parts = jnp.stack([share, (yield places.swap(share, 2))])
    yield jnp.stack([parts] + (yield [places.turn(parts, step) for step in range(1, places.far)]))


def vector_steps(places, value):
    value = value + (yield places.swap(value, 1))
    value = value + (yield places.swap(value, 2))
    total = value
    for arrived in (yield [places.turn(value, step) for step in range(1, places.far)]):
        total = total + arrived
    cross = total[V_GAINC : V_SHIFTC + 1]
    yield total, cross + (yield lax.ppermute(cross, SECTION, [(0, 1), (1, 0)]))


def place_kernel(far, groups, where_ref, *refs):
    own_refs, outs = refs[:4], refs[4:]
    core, near, rest = where_ref[0], where_ref[1], where_ref[2]
    half = own_refs[2].shape[2]
    rows = 2 * half
    for share in range(4 * far):
        c, n, q = share // (2 * far), share // far % 2, share % far
        step, which = lax.rem(rest - q + far, far), lax.rem(near + n, 2)

        def put(rest_first, near_first, share=share, step=step, which=which):
            parts = [(0, 0, rows, rest_first, (which, step)), (1, 0, half, rest_first, (which, step))]
            parts.append((1, half, half, near_first, (step, which)))
            taken = 0
            for group, first, size, source, at in parts:
                out, col = groups[group][share * rows // D]
                start_row = share * rows % D + first
                place = taken if source is rest_first else 0
                value = source[at[0], at[1], place : place + size, :]
                outs[out][start_row : start_row + size, col * D : (col + 1) * D] = value.astype(F32)
                taken += size

        pl.when(core == c)(functools.partial(put, own_refs[0], own_refs[2]))
        pl.when(core != c)(functools.partial(put, own_refs[1], own_refs[3]))


def put_in_place(places, gathered, groups, widths):
    where = jnp.stack([places.core, places.near, places.rest]).astype(jnp.int32)
    flat = [item for pair in gathered for item in pair]
    return pl.pallas_call(
        functools.partial(place_kernel, places.far, groups),
        out_shape=[shape(D, width, dtype=F32) for width in widths],
        in_specs=[smem_spec()] + [vmem_spec()] * len(flat),
        out_specs=[vmem_spec()] * len(widths),
        compiler_params=PARAMS,
        name="place_sums",
    )(where, *flat)


def widen_kernel(up_in, down_in, up_out, down_out):
    up_out[...] = up_in[...].astype(F32)
    down_out[...] = down_in[...].astype(F32)


def widen(grads):
    count = FF // D
    return pl.pallas_call(
        widen_kernel,
        grid=(count,),
        out_shape=[shape(D, FF, dtype=F32), shape(FF, D, dtype=F32)],
        in_specs=[pl.BlockSpec((D, D), lambda i: (i, 0)), pl.BlockSpec((D, D), lambda i: (count + i, 0))],
        out_specs=[pl.BlockSpec((D, D), lambda i: (0, i)), pl.BlockSpec((D, D), lambda i: (i, 0))],
        compiler_params=PARAMS,
        name="widen",
    )(grads, grads)


def shards(
    inputs, cotangent, lengths, running, norm_gain, norm_shift, qkv_weight, out_weight, up_weight, up_bias,
    down_weight, down_bias, halt_weight, halt_bias, cross_gain, cross_shift, cross_query, cross_kv, cross_out,
):
    decoding = on_decoder()
    places = Places()
    rows = range(inputs.shape[1])
    vectors = (norm_gain, norm_shift, lengths, running, up_bias, down_bias, halt_weight, halt_bias)
    crosses = (cross_gain[None], cross_shift[None])
    firsts, received = [], []
    for row in rows:
        arrays = (
            inputs, *vectors, *crosses, qkv_weight, out_weight, up_weight, down_weight, cross_query,
            *([firsts[row - 1][11]] if row else []),
        )
        firsts.append(call_a(row, lengths, running, arrays))
        received.append(lax.ppermute(firsts[row][1], SECTION, [(0, 1)]))
    result = firsts[-1][11]
    middles, returned = [], []
    for row in rows:
        _, out, after = firsts[row][:3]
        arrays = (
            inputs, cotangent, *vectors, up_weight, down_weight, cross_kv, cross_out, received[row], out, after,
            firsts[row][7], result,
        )
        middles.append(call_b(row, lengths, running, arrays))
        result = middles[row][12]
        returned.append(lax.ppermute(middles[row][9], SECTION, [(1, 0)]))

    def both(items, index):
        return [item[index] for item in items]

    feeds = []
    for row in rows:
        _, _, after, _, _, _, _, n2, act, change, _, _ = firsts[row]
        arrays = (
            inputs, cotangent, norm_gain, running, halt_weight, halt_bias, up_weight, down_weight, returned[row], after,
            middles[row][13], change, n2, act, *middles[row][1:5], crosses[0], cross_query, middles[row][7], middles[row][10],
            *([feeds[row - 1][3]] if row else []),
        )
        feeds.append(call_c(row, running, arrays))
    feed_sum = lax.psum(feeds[-1][3], DP)
    groups = [[(0, 0), (0, 1), (0, 2), (1, 0)], [(2, 0), (3, 0), (3, 1), (4, 0)]]
    widths = [3 * D, D, D, 2 * D, D]

    def tail(operands):
        firsts, middles, feeds, received = operands
        vec = sum(both(middles, 0)) + sum(both(feeds, 0))
        cross_grads = call_w(
            [
                (both(firsts, 10), both(feeds, 4)),
                (received, both(middles, 8)),
                (both(middles, 5), both(middles, 6)),
            ]
        )
        crosses = scatter_steps(places, *cross_grads, (SECTION, DP), places.count)
        cross, grad_after = lax.optimization_barrier((next(crosses), both(feeds, 1)))
        cross = crosses.send(cross)
        kinds = [both(firsts, 3), both(firsts, 5), both(firsts, 6), both(firsts, 4), grad_after, both(feeds, 2)]
        kinds = [item for kind in (*kinds, both(middles, 11)) for item in kind]
        vec_self, *self_grads, input_grad = call_s(
            len(rows), lengths, (inputs, norm_gain, lengths, qkv_weight, out_weight, *kinds)
        )
        cross, self_grads = lax.optimization_barrier((cross, self_grads))
        selfs, small = scatter_steps(places, *self_grads), vector_steps(places, vec + vec_self)
        own, vec = lax.optimization_barrier((next(selfs), next(small)))
        sent = selfs.send(own), small.send(vec), crosses.send(cross)
        own, vec, cross = lax.optimization_barrier(sent)
        cross = crosses.send(cross)
        sent = selfs.send(own), small.send(vec), lax.ppermute(cross, SECTION, [(1, 0)])
        own, vec, moved_cross = lax.optimization_barrier(sent)
        cross_share = jnp.where(decoding, cross, moved_cross)
        half = cross_share.shape[0] // 2
        gathers = [
            gather_rest_first(places, jnp.concatenate([selfs.send(own), cross_share[:half]])),
            gather_near_first(places, cross_share[half:]),
        ]
        sent = *(next(gather) for gather in gathers), small.send(vec)
        own, cross, vec = lax.optimization_barrier(sent)
        sent = gathers[0].send(own), gathers[1].send(cross)
        vec, cross_vec = small.send(vec)
        gathered = [gather.send(item) for gather, item in zip(gathers, lax.optimization_barrier(sent))]
        finals = (
            jnp.stack([vec[V_GAIN1], vec[V_GAIN2]])[None],
            jnp.stack([vec[V_SHIFT1], vec[V_SHIFT2]])[None],
            vec[V_UPB : V_UPB + 4].reshape(1, FF),
            vec[V_DOWNB][None],
            vec[V_HW][None],
            vec[V_HB, :1],
            cross_vec[0],
            cross_vec[1],
        )
        stats = [jnp.where(decoding, middles[row][0], firsts[row][0])[V_RMS, :2] for row in rows]
        row_rms = jnp.sqrt(jnp.stack(stats)[None] / (L * D) + 1e-06)
        return *gathered, *finals, row_rms, input_grad

    def nothing(operands):
        parts = jnp.zeros((2, places.far, 6 * D // places.count, D), BF16)
        swapped = jnp.zeros((places.far, 2, 2 * D // places.count, D), BF16)
        pair, one, wide = (jnp.zeros((1, size, D), F32) for size in (2, 1, 4))
        finals = (pair, pair, wide.reshape(1, FF), one[0], one[0], one[0, 0, :1], one[0, 0], one[0, 0])
        return parts, swapped, *finals, jnp.zeros(inputs.shape[:2] + (2,), F32), jnp.zeros(inputs.shape, F32)

    *gathered, gain, shift, up_b, down_b, halt_w, halt_b, cross_g, cross_s, row_rms, input_grad = lax.cond(
        lengths[0, 0, 0] > 0, tail, nothing, (firsts, middles, feeds, received)
    )
    gathered = [(parts, places.swap(parts, 1)) for parts in gathered]
    qkv_sum, out_sum, query_sum, kv_sum, cross_out_sum = put_in_place(places, gathered, groups, widths)
    up_sum, down_sum = widen(feed_sum)
    return (
        result,
        input_grad,
        row_rms,
        gain,
        shift,
        qkv_sum[None],
        out_sum[None],
        up_sum[None],
        up_b,
        down_sum[None],
        down_b,
        halt_w,
        halt_b,
        cross_g,
        cross_s,
        query_sum,
        kv_sum,
        cross_out_sum,
    )


def solution(mesh):
    in_specs = (
        P(SECTION, DP, None, None),
        P(SECTION, DP, None, None),
        P(None, DP, None),
        P(SECTION, DP, None),
        P(SECTION, None, None),
        P(SECTION, None, None),
        P(SECTION, None, None),
        P(SECTION, None, None),
        P(SECTION, None, None),
        P(SECTION, None),
        P(SECTION, None, None),
        P(SECTION, None),
        P(SECTION, None),
        P(SECTION),
        P(),
        P(),
        P(),
        P(),
        P(),
    )
    out_specs = (
        P(SECTION, DP, None, None),
        P(SECTION, DP, None, None),
        P(SECTION, DP, None),
        P(SECTION, None, None),
        P(SECTION, None, None),
        P(SECTION, None, None),
        P(SECTION, None, None),
        P(SECTION, None, None),
        P(SECTION, None),
        P(SECTION, None, None),
        P(SECTION, None),
        P(SECTION, None),
        P(SECTION),
        P(),
        P(),
        P(),
        P(),
        P(),
    )
    return jax.shard_map(shards, mesh=mesh, in_specs=in_specs, out_specs=out_specs, check_vma=False)
```
